32 devices in a mesh: groups: 2 (over y), grid: 4 (over z), dp: 4 (over x, core).
Axes of the slice: x: 2, y: 2, z: 4, core: 2. Of those that a mesh axis runs over, the one named last changes fastest.
Arguments:
- tokens: bfloat16 [128, 4096], P(('groups', 'grid'), 'dp'), parts along dimension 0, may hold values from -6 to 6
- w_gate: bfloat16 [4096, 16384], P('dp', 'grid'), may hold values from -0.09375 to 0.09375
- w_up: bfloat16 [4096, 16384], P('dp', 'grid'), may hold values from -0.09375 to 0.09375
- w_down: bfloat16 [16384, 4096], P('grid', 'dp'), may hold values from -0.046875 to 0.046875
- mask_gate: int32 [64, 128], P(('groups', 'dp'), 'grid'), parts along dimension 0, may hold values from 0 to 1, as said below
- mask_up: int32 [64, 128], P(('groups', 'dp'), 'grid'), parts along dimension 0, may hold values from 0 to 1, as said below
- mask_down: int32 [256, 32], P(('groups', 'grid'), 'dp'), parts along dimension 0, may hold values from 0 to 1, as said below
- grad_out: bfloat16 [128, 4096], P(('groups', 'grid'), 'dp'), parts along dimension 0, may hold values from -6 to 6
Outputs:
- output: bfloat16 [128, 4096], P(('groups', 'grid'), 'dp'), parts along dimension 0
- grad_tokens: bfloat16 [128, 4096], P(('groups', 'grid'), 'dp'), parts along dimension 0
- grad_gate: float32 [8192, 16384], P(('groups', 'dp'), 'grid'), parts along dimension 0
- grad_up: float32 [8192, 16384], P(('groups', 'dp'), 'grid'), parts along dimension 0
- grad_down: float32 [32768, 4096], P(('groups', 'grid'), 'dp'), parts along dimension 0
The draws below stay inside these ranges and needn't reach their ends.
There are 2 independent parts, one for each index of `groups`. The reference program is written for one: setup_inputs(seed, part) draws one part's arguments, and reference() takes and returns one part's arrays. A program takes and returns all parts, laid end to end along the dimension named above; an argument that names none is the same for every part. Nothing has to cross between parts.
Inputs may be any that keep to these rules, and one draw needn't show every extreme that they name: `mask_gate`: 1 keeps the weight block, 0 drops it; the share kept differs between bands of 4 x 4 blocks. `mask_up`: as for mask_gate, drawn independently. `mask_down`: as for mask_gate, drawn independently.
All inputs are finite; a program needn't handle non-finite values.
Results may differ from the reference program's by a relative error of at most 0.005.
Values may be sent and summed in bfloat16 or wider, within the bound.
No kernel may reach another device: no remote copies, remote signals or barrier semaphores. Data moves between devices by JAX's collectives and lax.ppermute only.
A program may use at most 320 MiB of HBM per device.

```python
import jax
import jax.numpy as jnp

D = 4096
FF = 16384
BLK = 128
TOKENS = 64


def band_mask(key, rows, cols):
    first, second = jax.random.split(key)
    levels = jax.random.randint(first, (rows // 4, cols // 4), 2, 9)
    levels = jnp.repeat(jnp.repeat(levels, 4, axis=0), 4, axis=1)
    rolled = jax.random.randint(second, (rows, cols), 0, 10)
    return (rolled < levels).astype(jnp.int32)


def draw_mask_gate(key, part):
    key = jax.random.fold_in(key, 11)
    return band_mask(key, D // BLK, FF // BLK)


def draw_mask_up(key, part):
    key = jax.random.fold_in(key, 23)
    return band_mask(key, D // BLK, FF // BLK)


def draw_mask_down(key, part):
    key = jax.random.fold_in(key, 37)
    return band_mask(key, FF // BLK, D // BLK)


def block_levels(key, dims, pieces, smallest, largest):
    level, own = 1.0, jax.random.fold_in(key, 6)
    for position, blocks in pieces:
        heights = jnp.exp(jax.random.uniform(jax.random.fold_in(own, position), (blocks,), jnp.float32, smallest / len(pieces), largest / len(pieces)))
        level = level * jnp.repeat(heights, dims[position] // blocks).reshape([-1 if axis == position else 1 for axis in range(len(dims))])
    return level


def scatter_about(rng, dims, scale, bound, shards=(), kind=jnp.bfloat16):
    array = scale * jax.random.normal(rng, dims, jnp.float32)
    if shards:
        array = array * block_levels(rng, dims, shards, -0.22, 0.18)
    return jnp.clip(array, -bound, bound).astype(kind)


def setup_inputs(seed: int = 0, part: int = 0) -> dict:
    splits = jax.random.split(jax.random.key(seed), 9)
    own_keys = jax.random.split(jax.random.fold_in(splits[8], part), 9)
    return {
        "tokens": scatter_about(own_keys[0], (TOKENS, D), 1.0, 6.0, ((0, 4), (1, 4))),
        "w_gate": scatter_about(splits[1], (D, FF), D ** -0.5, 0.09375, ((0, 4), (1, 4))),
        "w_up": scatter_about(splits[2], (D, FF), D ** -0.5, 0.09375, ((0, 4), (1, 4))),
        "w_down": scatter_about(splits[3], (FF, D), FF ** -0.5, 0.046875, ((0, 4), (1, 4))),
        "mask_gate": draw_mask_gate(jax.random.fold_in(jax.random.fold_in(splits[8], part), 71), part),
        "mask_up": draw_mask_up(jax.random.fold_in(jax.random.fold_in(splits[8], part), 71), part),
        "mask_down": draw_mask_down(jax.random.fold_in(jax.random.fold_in(splits[8], part), 71), part),
        "grad_out": scatter_about(own_keys[7], (TOKENS, D), 1.0, 6.0, ((0, 4), (1, 4))),
    }


def blocked(weight, mask):
    rows, cols = weight.shape
    mask_rows, mask_cols = mask.shape
    shaped = weight.reshape(mask_rows, rows // mask_rows, mask_cols, cols // mask_cols)
    return (shaped * mask.astype(weight.dtype)[:, None, :, None]).reshape(rows, cols)


def swiglu_parts(gate):
    sigmoid_gate = jax.nn.sigmoid(gate)
    silu_gate = gate * sigmoid_gate
    slope = sigmoid_gate * (1.0 + gate * (1.0 - sigmoid_gate))
    return silu_gate, slope


def reference(tokens, w_gate, w_up, w_down, mask_gate, mask_up, mask_down, grad_out):
    gate_eff = blocked(w_gate, mask_gate)
    up_eff = blocked(w_up, mask_up)
    down_eff = blocked(w_down, mask_down)
    gate = jnp.dot(tokens, gate_eff, preferred_element_type=jnp.float32)
    up_val = jnp.dot(tokens, up_eff, preferred_element_type=jnp.float32)
    silu_gate, slope = swiglu_parts(gate)
    hidden = (silu_gate * up_val).astype(jnp.bfloat16)
    output = jnp.dot(hidden, down_eff, preferred_element_type=jnp.float32).astype(jnp.bfloat16)
    hidden_grad = jnp.dot(grad_out, down_eff.T, preferred_element_type=jnp.float32)
    gate_grad = (hidden_grad * up_val * slope).astype(jnp.bfloat16)
    up_grad = (hidden_grad * silu_gate).astype(jnp.bfloat16)
    grad_tokens = (jnp.dot(gate_grad, gate_eff.T, preferred_element_type=jnp.float32)
                   + jnp.dot(up_grad, up_eff.T, preferred_element_type=jnp.float32)).astype(jnp.bfloat16)
    grad_gate = blocked(jnp.dot(tokens.T, gate_grad, preferred_element_type=jnp.float32), mask_gate)
    grad_up = blocked(jnp.dot(tokens.T, up_grad, preferred_element_type=jnp.float32), mask_up)
    grad_down = blocked(jnp.dot(hidden.T, grad_out, preferred_element_type=jnp.float32), mask_down)
    return (output, grad_tokens, grad_gate, grad_up, grad_down)
```

```python
import functools

import jax
import jax.numpy as jnp
from jax import lax
from jax.experimental import pallas as pl
from jax.experimental.pallas import tpu as pltpu
from jax.sharding import PartitionSpec as P

BLK = 128
MIB = 1024 * 1024
F32 = jnp.float32
BF16 = jnp.bfloat16


def dot(left, right, dims=(1, 0)):
    return lax.dot_general(
        left, right, (((dims[0],), (dims[1],)), ((), ())), preferred_element_type=F32
    )


def masked_rows(w_ref, row_of):
    bands = [
        w_ref[b * BLK : (b + 1) * BLK, :] * row_of(b).astype(BF16)
        for b in range(w_ref.shape[0] // BLK)
    ]
    return bands[0] if len(bands) == 1 else jnp.concatenate(bands, axis=0)


def call(kernel, scalars, grid, ins, outs, scratch=(), aliases=None, cost=None, name=None):
    return pl.pallas_call(
        kernel,
        out_shape=[shape for shape, _ in outs],
        grid_spec=pltpu.PrefetchScalarGridSpec(
            num_scalar_prefetch=1,
            grid=grid,
            in_specs=[spec for _, spec in ins],
            out_specs=[spec for _, spec in outs],
            scratch_shapes=list(scratch),
        ),
        input_output_aliases=aliases or {},
        compiler_params=pltpu.CompilerParams(vmem_limit_bytes=32 * MIB),
        cost_estimate=cost,
        name=name,
    )(scalars, *[array for array, _ in ins])


def whole(array):
    return pl.BlockSpec(array.shape, lambda *_: (0,) * len(array.shape))


def partial_kernel(add, idx, tok, cot, wg, wu, wd, mg, mu, md, *rest):
    gate = dot(tok[...], masked_rows(wg, lambda b: mg[b : b + 1, :]))
    up = dot(tok[...], masked_rows(wu, lambda b: mu[b : b + 1, :]))
    back = dot(cot[...], masked_rows(wd, lambda b: md[b]), (1, 1))
    if add:
        received, own, send = rest
        for k, value in enumerate((gate, up, back)):
            total = value + received[k].astype(F32)
            own[k] = total
            send[k] = total.astype(BF16)
    else:
        (send,) = rest
        for k, value in enumerate((gate, up, back)):
            send[k] = value.astype(BF16)


def act_kernel(idx, own, *rest):
    act = rest[-1]
    gate, up, back = (
        sum((r[k].astype(F32) for r in rest[:-1]), own[k]) for k in range(3)
    )
    sigma = 1.0 / (1.0 + jnp.exp(-gate))
    silu = gate * sigma
    slope = sigma * (1.0 + gate * (1.0 - sigma))
    act[0] = (silu * up).astype(BF16)
    act[1] = (back * up * slope).astype(BF16)
    act[2] = (back * silu).astype(BF16)


def rows_kernel(first, last, tiles, idx, own, other, wg, wu, wd, mg, mu, md, *rest):
    if first:
        carried, rest = None, rest
    else:
        carried, rest = rest[0], rest[1:]
    outs, acc = rest[:-1], rest[-1]
    step = pl.program_id(0)

    @pl.when(step == 0)
    def _():
        if first:
            acc[...] = jnp.zeros_like(acc)
        else:
            acc[...] = carried[...]

    def add(act):
        down = masked_rows(wd, lambda b: md[b])
        acc[0] += dot(act[0], down)
        gate = masked_rows(wg, lambda b: mg[b : b + 1, :])
        up = masked_rows(wu, lambda b: mu[b : b + 1, :])
        acc[1] += dot(act[1], gate, (1, 1)) + dot(act[2], up, (1, 1))

    @pl.when(step < tiles)
    def _():
        add(own)

    @pl.when(step >= tiles)
    def _():
        add(other)

    @pl.when(step == 2 * tiles - 1)
    def _():
        if last:
            rows = outs[0].shape[1]
            for k, out in enumerate(outs):
                out[...] = acc[:, k * rows : (k + 1) * rows, :].astype(out.dtype)
        else:
            outs[0][...] = acc[...]


def grads_kernel(carried, idx, act, tok_t, cot, mg, mu, md, *rest):
    gg, gu, gd = rest[-3:]
    for out, k, mask in ((gg, 1, mg), (gu, 2, mu)):
        for b in range(gg.shape[0] // BLK):
            band = slice(b * BLK, (b + 1) * BLK)
            out[band, :] = dot(tok_t[band, :], act[k]) * mask[b : b + 1, :]
    hidden_t = act[0].T
    for b in range(gd.shape[0] // BLK):
        band = slice(b * BLK, (b + 1) * BLK)
        gd[band, :] = dot(hidden_t[band, :], cot[...]) * md[b]


def shards(sizes, tokens, w_gate, w_up, w_down, mask_gate, mask_up, mask_down, grad_out):
    n_grid, n_dp = sizes
    width, units = w_gate.shape
    pairs = n_dp // 2
    half = units // 2
    pieces = 2 if half % (2 * BLK) == 0 else 1
    piece = half // pieces
    tile = 256 if piece % 256 == 0 else BLK
    tiles = piece // tile

    core = lax.axis_index("dp") % 2
    scalars = jnp.stack([core, 1 - core]).astype(jnp.int32)

    def gather(block):
        if n_grid > 4:
            return lax.all_gather(block, "grid", axis=0, tiled=True)
        blocks = [block]
        for s in range(1, n_grid):
            blocks.append(
                lax.ppermute(block, "grid", [(i, (i + s) % n_grid) for i in range(n_grid)])
            )
        return jnp.concatenate(blocks, axis=0)

    def swap(array):
        return lax.ppermute(array, "dp", [(i, i ^ 1) for i in range(n_dp)])

    def across(array):
        return [
            lax.ppermute(
                array,
                "dp",
                [(i, ((i // 2 + s) % pairs) * 2 + i % 2) for i in range(n_dp)],
            )
            for s in range(1, pairs)
        ]

    tok = gather(tokens)
    cot = gather(grad_out)
    rows = tok.shape[0]
    tok_t = tok.T

    mg = jnp.repeat(mask_gate.astype(F32), BLK, axis=1)
    mu = jnp.repeat(mask_up.astype(F32), BLK, axis=1)
    md = jnp.repeat(mask_down.astype(F32), BLK, axis=1)[:, None, :]

    def place(which, p):
        def at(step, idx):
            return idx[which] * (half // tile) + p * tiles + step

        return at

    def cols(at, height):
        return pl.BlockSpec((height, tile), lambda i, idx: (0, at(i, idx)))

    def bands(at):
        return pl.BlockSpec((tile // BLK, 1, width), lambda i, idx: (at(i, idx), 0, 0))

    def downs(at):
        return pl.BlockSpec((tile, width), lambda i, idx: (at(i, idx), 0))

    def weights(at):
        return [
            (w_gate, cols(at, width)),
            (w_up, cols(at, width)),
            (w_down, downs(at)),
            (mg, cols(at, width // BLK)),
            (mu, cols(at, width // BLK)),
            (md, bands(at)),
        ]

    trio = pl.BlockSpec((3, rows, tile), lambda i, idx: (0, 0, i))
    trio_bf16 = (jax.ShapeDtypeStruct((3, rows, piece), BF16), trio)
    trio_f32 = (jax.ShapeDtypeStruct((3, rows, piece), F32), trio)
    macs = 3 * rows * width * piece
    weight_bytes = 3 * width * piece * 2

    def partials(which, p, received=None):
        ins = [(tok, whole(tok)), (cot, whole(cot))] + weights(place(which, p))
        outs = [trio_bf16]
        if received is not None:
            ins.append((received, trio))
            outs = [trio_f32, trio_bf16]
        return call(
            functools.partial(partial_kernel, received is not None),
            scalars,
            (tiles,),
            ins,
            outs,
            cost=pl.CostEstimate(flops=2 * macs, bytes_accessed=weight_bytes, transcendentals=0),
            name="partials",
        )

    def activate(own, others):
        ins = [(a, whole(a)) for a in (own, *others)]
        shape = jax.ShapeDtypeStruct(own.shape, BF16)
        return call(
            act_kernel,
            scalars,
            (1,),
            ins,
            [(shape, whole(shape))],
            cost=pl.CostEstimate(
                flops=20 * rows * piece, bytes_accessed=12 * rows * piece, transcendentals=rows * piece
            ),
            name="activate",
        )[0]

    n_out = n_grid if n_grid <= 4 else 1

    def sum_rows(p, own, other, carried):
        first, last = carried is None, p == pieces - 1

        def at(step, idx):
            which = step // tiles
            return (idx[0] * (1 - which) + idx[1] * which) * (half // tile) + p * tiles + step % tiles

        acts = [
            (own, pl.BlockSpec((3, rows, tile), lambda i, idx: (0, 0, jnp.minimum(i, tiles - 1)))),
            (other, pl.BlockSpec((3, rows, tile), lambda i, idx: (0, 0, jnp.maximum(i - tiles, 0)))),
        ]
        ins = acts + weights(at)
        if not first:
            ins.append((carried, whole(carried)))
        if last:
            kind = BF16 if n_out > 1 else F32
            shape = jax.ShapeDtypeStruct((2, rows // n_out, width), kind)
            outs = [(shape, whole(shape))] * n_out
        else:
            shape = jax.ShapeDtypeStruct((2, rows, width), F32)
            outs = [(shape, whole(shape))]
        return call(
            functools.partial(rows_kernel, first, last, tiles),
            scalars,
            (2 * tiles,),
            ins,
            outs,
            scratch=[pltpu.VMEM((2, rows, width), F32)],
            cost=pl.CostEstimate(flops=4 * macs, bytes_accessed=2 * weight_bytes, transcendentals=0),
            name="sum_rows",
        )

    def weight_grads(which, p, act, carried):
        at = place(which, p)
        ins = [(act, trio), (tok_t, whole(tok_t)), (cot, whole(cot))] + weights(at)[3:]
        shapes = [
            jax.ShapeDtypeStruct((width, units), F32),
            jax.ShapeDtypeStruct((width, units), F32),
            jax.ShapeDtypeStruct((units, width), F32),
        ]
        specs = [cols(at, width), cols(at, width), downs(at)]
        aliases = {}
        if carried is not None:
            aliases = {1 + len(ins) + k: k for k in range(3)}
            ins = ins + [(c, pl.BlockSpec(memory_space=pl.ANY)) for c in carried]
        return call(
            functools.partial(grads_kernel, carried is not None),
            scalars,
            (tiles,),
            ins,
            list(zip(shapes, specs)),
            aliases=aliases,
            cost=pl.CostEstimate(flops=2 * macs, bytes_accessed=2 * weight_bytes, transcendentals=0),
            name="weight_grads",
        )

    sent = [swap(partials(1, p)[0]) for p in range(pieces)]
    sums, theirs = [], []
    for p in range(pieces):
        own, send = partials(0, p, sent[p])
        sums.append(own)
        theirs.append(across(send))

    grads, carried = None, None
    for p in range(pieces):
        act = activate(sums[p], theirs[p])
        act_other = swap(act)
        carried = sum_rows(p, act, act_other, carried)
        if p < pieces - 1:
            carried = carried[0]
        grads = weight_grads(0, p, act, grads)
        grads = weight_grads(1, p, act_other, grads)

    if n_out == 1:
        both = lax.psum_scatter(carried[0], "grid", scatter_dimension=1, tiled=True)
    else:
        both = carried[0].astype(F32)
        for s in range(1, n_grid):
            both += lax.ppermute(
                carried[s], "grid", [(i, (i - s) % n_grid) for i in range(n_grid)]
            ).astype(F32)
    both = both.astype(BF16)
    return (both[0], both[1], *grads)


def solution(mesh):
    in_specs = (
        P(("groups", "grid"), "dp"),
        P("dp", "grid"),
        P("dp", "grid"),
        P("grid", "dp"),
        P(("groups", "dp"), "grid"),
        P(("groups", "dp"), "grid"),
        P(("groups", "grid"), "dp"),
        P(("groups", "grid"), "dp"),
    )
    out_specs = (
        P(("groups", "grid"), "dp"),
        P(("groups", "grid"), "dp"),
        P(("groups", "dp"), "grid"),
        P(("groups", "dp"), "grid"),
        P(("groups", "grid"), "dp"),
    )
    sizes = (mesh.shape["grid"], mesh.shape["dp"])
    return jax.shard_map(
        functools.partial(shards, sizes),
        mesh=mesh,
        in_specs=in_specs,
        out_specs=out_specs,
        check_vma=False,
    )
```

```python
import functools
import types

import jax
import jax.numpy as jnp
from jax import lax
from jax.experimental import pallas as pl
from jax.experimental.pallas import tpu as pltpu
from jax.sharding import PartitionSpec as P

BLK = 128
PIECES = [3, 3, 2]
MIB = 1024 * 1024
F32 = jnp.float32
BF16 = jnp.bfloat16


def dot(left, right, dims=(1, 0)):
    return lax.dot_general(
        left, right, (((dims[0],), (dims[1],)), ((), ())), preferred_element_type=F32
    )


def masked_rows(w_ref, row_of):
    bands = [
        w_ref[b * BLK : (b + 1) * BLK, :] * row_of(b).astype(BF16)
        for b in range(w_ref.shape[0] // BLK)
    ]
    return bands[0] if len(bands) == 1 else jnp.concatenate(bands, axis=0)


def call(kernel, name, scalars, grid, ins, outs, scratch=None, aliases=None, cost=None):
    scratch = scratch or {}
    names = [*ins, *outs, *scratch]
    in_names, out_names = list(ins), list(outs)

    def body(_, *refs):
        kernel(types.SimpleNamespace(**dict(zip(names, refs))))

    results = pl.pallas_call(
        body,
        out_shape=[shape for shape, _ in outs.values()],
        grid_spec=pltpu.PrefetchScalarGridSpec(
            num_scalar_prefetch=1,
            grid=grid,
            in_specs=[spec for _, spec in ins.values()],
            out_specs=[spec for _, spec in outs.values()],
            scratch_shapes=list(scratch.values()),
        ),
        input_output_aliases={
            1 + in_names.index(i): out_names.index(o) for i, o in (aliases or {}).items()
        },
        compiler_params=pltpu.CompilerParams(vmem_limit_bytes=40 * MIB),
        cost_estimate=cost,
        name=name,
    )(scalars, *[array for array, _ in ins.values()])
    return dict(zip(out_names, results))


def whole(array):
    return pl.BlockSpec(array.shape, lambda *_: (0,) * len(array.shape))


def assemble_kernel(r):
    blocks = [ref for name, ref in vars(r).items() if name.startswith("block")]
    rows = blocks[0].shape[1]
    for k, block in enumerate(blocks):
        r.tok[k * rows : (k + 1) * rows, :] = block[0]
        r.cot[k * rows : (k + 1) * rows, :] = block[1]
    r.tok_t[...] = r.tok[...].T


def partial_kernel(r):
    gate = dot(r.tok[...], masked_rows(r.wg, lambda b: r.mg[b : b + 1, :]))
    up = dot(r.tok[...], masked_rows(r.wu, lambda b: r.mu[b : b + 1, :]))
    back = dot(masked_rows(r.wd, lambda b: r.md[b]), r.cot[...], (1, 1)).T
    for k, value in enumerate((gate, up, back)):
        if hasattr(r, "received"):
            value = value + r.received[k]
            r.own[k] = value
        r.send[k] = value.astype(r.send.dtype)


def act_kernel(r):
    others = [ref for name, ref in vars(r).items() if name.startswith("other")]
    gate, up, back = (
        sum((other[k].astype(F32) for other in others), r.own[k]) for k in range(3)
    )
    sigma = 1.0 / (1.0 + jnp.exp(-gate))
    silu = gate * sigma
    slope = sigma * (1.0 + gate * (1.0 - sigma))
    r.act[0] = (silu * up).astype(BF16)
    r.act[1] = (back * up * slope).astype(BF16)
    r.act[2] = (back * silu).astype(BF16)


def add_rows(r, tiles):
    step = pl.program_id(0)

    @pl.when(step == 0)
    def _():
        for acc, carried in ((r.acc_out, "sum_out"), (r.acc_tok, "sum_tok")):
            acc[...] = getattr(r, carried)[...] if hasattr(r, carried) else jnp.zeros_like(acc)

    r.acc_out[...] += dot(r.act[0], masked_rows(r.wd, lambda b: r.md[b]))
    r.acc_tok[...] += dot(
        masked_rows(r.wg, lambda b: r.mg[b : b + 1, :]), r.act[1], (1, 1)
    ) + dot(masked_rows(r.wu, lambda b: r.mu[b : b + 1, :]), r.act[2], (1, 1))

    @pl.when(step == tiles - 1)
    def _():
        if hasattr(r, "new_out"):
            r.new_out[...] = r.acc_out[...]
            r.new_tok[...] = r.acc_tok[...]
        else:
            outs = [ref for name, ref in vars(r).items() if name.startswith("rows")]
            grad_tok = r.acc_tok[...].T
            rows = outs[0].shape[1]
            for k, out in enumerate(outs):
                band = slice(k * rows, (k + 1) * rows)
                out[0] = r.acc_out[band, :].astype(out.dtype)
                out[1] = grad_tok[band, :].astype(out.dtype)


def weight_grads(r):
    for out, k, mask in ((r.gg, 1, r.mg), (r.gu, 2, r.mu)):
        for b in range(out.shape[0] // BLK):
            band = slice(b * BLK, (b + 1) * BLK)
            out[band, :] = dot(r.tok_t[band, :], r.act[k]) * mask[b : b + 1, :]
    hidden_t = r.act[0].T
    for b in range(r.gd.shape[0] // BLK):
        band = slice(b * BLK, (b + 1) * BLK)
        r.gd[band, :] = dot(hidden_t[band, :], r.cot[...]) * r.md[b]


def back_kernel(do_rows, do_grads, tiles, r):
    if do_rows:
        add_rows(r, tiles)
    if do_grads:
        weight_grads(r)


def shards(sizes, tokens, w_gate, w_up, w_down, mask_gate, mask_up, mask_down, grad_out):
    n_grid, n_dp = sizes
    width, units = w_gate.shape
    pairs = n_dp // 2
    half = units // 2
    tile = 256 if half % 256 == 0 and half >= 1024 else BLK
    split = PIECES if sum(PIECES) * tile == half else [half // tile]
    starts = [sum(split[:p]) for p in range(len(split))]
    direct = n_grid == 4

    core = lax.axis_index("dp") % 2
    scalars = jnp.stack([core, 1 - core]).astype(jnp.int32)
    w_gate, w_up, w_down = (
        pltpu.with_memory_space_constraint(w, pltpu.HBM) for w in (w_gate, w_up, w_down)
    )

    def trade(array, s):
        return lax.ppermute(array, "grid", [(i, i ^ s) for i in range(n_grid)])

    def swap(array):
        return lax.ppermute(array, "dp", [(i, i ^ 1) for i in range(n_dp)])

    def across(array):
        return [
            lax.ppermute(
                array,
                "dp",
                [(i, ((i // 2 + s) % pairs) * 2 + i % 2) for i in range(n_dp)],
            )
            for s in range(1, pairs)
        ]

    mg = jnp.repeat(mask_gate.astype(F32), BLK, axis=1)
    mu = jnp.repeat(mask_up.astype(F32), BLK, axis=1)
    md = jnp.repeat(mask_down.astype(F32), BLK, axis=1)[:, None, :]

    block = jnp.stack([tokens, grad_out])
    if direct:
        blocks = [block] + [trade(block, s) for s in range(1, n_grid)]
    else:
        blocks = [lax.all_gather(block, "grid", axis=1, tiled=True)]
    rows = sum(b.shape[1] for b in blocks)
    row_shape = jax.ShapeDtypeStruct((rows, width), BF16)
    col_shape = jax.ShapeDtypeStruct((width, rows), BF16)
    gathered = call(
        assemble_kernel,
        "assemble",
        scalars,
        (1,),
        {f"block{k}": (b, whole(b)) for k, b in enumerate(blocks)},
        {
            "tok": (row_shape, whole(row_shape)),
            "cot": (row_shape, whole(row_shape)),
            "tok_t": (col_shape, whole(col_shape)),
        },
    )
    tok, cot, tok_t = gathered["tok"], gathered["cot"], gathered["tok_t"]

    def place(which, p):
        return lambda step, idx: idx[which] * (half // tile) + starts[p] + step

    def cols(at, height):
        return pl.BlockSpec((height, tile), lambda i, idx: (0, at(i, idx)))

    def downs(at):
        return pl.BlockSpec((tile, width), lambda i, idx: (at(i, idx), 0))

    def masks(at):
        bands = pl.BlockSpec((tile // BLK, 1, width), lambda i, idx: (at(i, idx), 0, 0))
        return {
            "mg": (mg, cols(at, width // BLK)),
            "mu": (mu, cols(at, width // BLK)),
            "md": (md, bands),
        }

    def weights(at):
        return {
            "wg": (w_gate, cols(at, width)),
            "wu": (w_up, cols(at, width)),
            "wd": (w_down, downs(at)),
        }

    trio = pl.BlockSpec((3, rows, tile), lambda i, idx: (0, 0, i))

    def trio_of(p, kind):
        return (jax.ShapeDtypeStruct((3, rows, split[p] * tile), kind), trio)

    def cost(p, matmuls, mats):
        step = width * split[p] * tile
        return pl.CostEstimate(
            flops=2 * matmuls * rows * step, bytes_accessed=2 * mats * step, transcendentals=0
        )

    def partials(which, p, after=None, received=None):
        at = place(which, p)
        ins = {"tok": (tok, whole(tok)), "cot": (cot, whole(cot)), **weights(at), **masks(at)}
        outs = {"send": trio_of(p, F32)}
        if after is not None:
            ins["after"] = (after, pl.BlockSpec(memory_space=pl.ANY))
        if received is not None:
            ins["received"] = (received, trio)
            outs = {"own": trio_of(p, F32), "send": trio_of(p, BF16)}
        return call(
            partial_kernel, "partials", scalars, (split[p],), ins, outs, cost=cost(p, 3, 3)
        )

    def activate(own, others, after):
        ins = {"own": (own, whole(own)), "after": (after, pl.BlockSpec(memory_space=pl.ANY))}
        ins.update({f"other{k}": (a, whole(a)) for k, a in enumerate(others)})
        shape = jax.ShapeDtypeStruct(own.shape, BF16)
        return call(act_kernel, "activate", scalars, (1,), ins, {"act": (shape, whole(shape))})["act"]

    def back(which, p, act, do_rows, do_grads, state, last=False):
        at = place(which, p)
        ins = {"act": (act, trio), **masks(at)}
        outs, aliases, scratch = {}, {}, {}
        if do_rows:
            ins.update(weights(at))
            sums = {
                "out": jax.ShapeDtypeStruct((rows, width), F32),
                "tok": jax.ShapeDtypeStruct((width, rows), F32),
            }
            for k, shape in sums.items():
                if "sum_" + k in state:
                    ins["sum_" + k] = (state["sum_" + k], whole(shape))
                scratch["acc_" + k] = pltpu.VMEM(shape.shape, F32)
            if last:
                n_out = n_grid if direct else 1
                shape = jax.ShapeDtypeStruct((2, rows // n_out, width), BF16 if direct else F32)
                outs.update({f"rows{k}": (shape, whole(shape)) for k in range(n_out)})
            else:
                outs.update({"new_" + k: (shape, whole(shape)) for k, shape in sums.items()})
        if do_grads:
            ins.update(tok_t=(tok_t, whole(tok_t)), cot=(cot, whole(cot)))
            by_cols = jax.ShapeDtypeStruct((width, units), F32)
            by_rows = jax.ShapeDtypeStruct((units, width), F32)
            outs["gg"] = (by_cols, cols(at, width))
            outs["gu"] = (by_cols, cols(at, width))
            outs["gd"] = (by_rows, downs(at))
            for k in ("gg", "gu", "gd"):
                if k in state:
                    ins["old_" + k] = (state[k], pl.BlockSpec(memory_space=pl.ANY))
                    aliases["old_" + k] = k
            if "rows0" in state:
                ins["after"] = (state["rows0"], pl.BlockSpec(memory_space=pl.ANY))
        got = call(
            functools.partial(back_kernel, do_rows, do_grads, split[p]),
            "_".join(["back"] + ["rows"] * do_rows + ["grads"] * do_grads),
            scalars,
            (split[p],),
            ins,
            outs,
            scratch=scratch,
            aliases=aliases,
            cost=cost(p, 3 * do_rows + 3 * do_grads, 3 * do_rows + 6 * do_grads),
        )
        renamed = {k.replace("new_", "sum_"): v for k, v in got.items()}
        return {**state, **renamed}

    n = len(split)
    sent, sums, theirs, after = [], [], [], None
    for p in range(n + 1):
        if p < n:
            after = partials(1, p, after)["send"]
            sent.append(swap(after))
        if p > 0:
            got = partials(0, p - 1, after, sent[p - 1])
            after = got["own"]
            sums.append(after)
            theirs.append(across(got["send"]))

    state = {}
    for p in range(n):
        last = p == n - 1
        act = activate(sums[p], theirs[p], state.get("sum_out", after))
        act_other = swap(act)
        state = back(0, p, act, True, not last, state)
        state = back(1, p, act_other, True, not last, state, last)
        if last:
            state = back(0, p, act, False, True, state)
            state = back(1, p, act_other, False, True, state)

    if direct:
        both = state["rows0"].astype(F32)
        for s in range(1, n_grid):
            both += trade(state[f"rows{s}"], s).astype(F32)
    else:
        both = lax.psum_scatter(state["rows0"], "grid", scatter_dimension=1, tiled=True)
    both = both.astype(BF16)
    return (both[0], both[1], state["gg"], state["gu"], state["gd"])


def solution(mesh):
    in_specs = (
        P(("groups", "grid"), "dp"),
        P("dp", "grid"),
        P("dp", "grid"),
        P("grid", "dp"),
        P(("groups", "dp"), "grid"),
        P(("groups", "dp"), "grid"),
        P(("groups", "grid"), "dp"),
        P(("groups", "grid"), "dp"),
    )
    out_specs = (
        P(("groups", "grid"), "dp"),
        P(("groups", "grid"), "dp"),
        P(("groups", "dp"), "grid"),
        P(("groups", "dp"), "grid"),
        P(("groups", "grid"), "dp"),
    )
    sizes = (mesh.shape["grid"], mesh.shape["dp"])
    return jax.shard_map(
        functools.partial(shards, sizes),
        mesh=mesh,
        in_specs=in_specs,
        out_specs=out_specs,
        check_vma=False,
    )
```

```python
import functools
import types

import jax
import jax.numpy as jnp
from jax import lax
from jax.experimental import pallas as pl
from jax.experimental.pallas import tpu as pltpu
from jax.sharding import PartitionSpec as P

BLK = 128
PIECES = [3, 3, 2]
MIB = 1024 * 1024
F32 = jnp.float32
BF16 = jnp.bfloat16


def dot(left, right, dims=(1, 0)):
    return lax.dot_general(
        left, right, (((dims[0],), (dims[1],)), ((), ())), preferred_element_type=F32
    )


def pinned(array):
    spec = pl.BlockSpec(memory_space=pltpu.VMEM)
    if isinstance(array, jax.ShapeDtypeStruct):
        return (pltpu.VMEM(array.shape, array.dtype), spec)
    return (pltpu.with_memory_space_constraint(array, pltpu.VMEM), spec)


def call(kernel, name, scalars, grid, ins, outs, scratch=None, aliases=None, cost=None):
    scratch = scratch or {}
    names = ["place", *ins, *outs, *scratch]
    in_names, out_names = list(ins), list(outs)

    def body(*refs):
        kernel(types.SimpleNamespace(**dict(zip(names, refs))))

    results = pl.pallas_call(
        body,
        out_shape=[shape for shape, _ in outs.values()],
        grid_spec=pltpu.PrefetchScalarGridSpec(
            num_scalar_prefetch=1,
            grid=grid,
            in_specs=[spec for _, spec in ins.values()],
            out_specs=[spec for _, spec in outs.values()],
            scratch_shapes=list(scratch.values()),
        ),
        input_output_aliases={
            1 + in_names.index(i): out_names.index(o) for i, o in (aliases or {}).items()
        },
        compiler_params=pltpu.CompilerParams(vmem_limit_bytes=11 * MIB),
        cost_estimate=cost,
        name=name,
    )(scalars, *[array for array, _ in ins.values()])
    return dict(zip(out_names, results))


def hbm(array):
    return pltpu.with_memory_space_constraint(array, pltpu.HBM)


def whole(array):
    return pl.BlockSpec(array.shape, lambda *_: (0,) * len(array.shape))


def assemble_kernel(r):
    blocks = [ref for name, ref in vars(r).items() if name.startswith("block")]
    rows = blocks[0].shape[1]
    for k, block in enumerate(blocks):
        r.tok[k * rows : (k + 1) * rows, :] = block[0]
        r.cot[k * rows : (k + 1) * rows, :] = block[1]
    r.tok_t[...] = r.tok[...].T


def mask_kernel(r):
    step = pl.program_id(0)

    @pl.when(step == 0)
    def _():
        for mask, out in ((r.mask_gate, r.mg), (r.mask_up, r.mu), (r.mask_down, r.md)):
            blocks, lanes = mask.shape[1], mask.shape[1] * BLK
            at = lax.broadcasted_iota(jnp.int32, (blocks, lanes), 0)
            column = lax.broadcasted_iota(jnp.int32, (blocks, lanes), 1)
            first = at * BLK
            spread = ((column >= first) & (column < first + BLK)).astype(F32).astype(BF16)
            wide = dot(mask[...].astype(F32).astype(BF16), spread)
            for b in range(mask.shape[0]):
                out[b] = wide[b : b + 1, :]

    for w, mask, out in ((r.w_gate, r.mg, r.wg), (r.w_up, r.mu, r.wu), (r.w_down, r.md, r.wd)):
        rows = w.shape[0]
        for b in range(rows // BLK):
            keep = mask[step * (rows // BLK) + b].astype(BF16)
            band = pl.ds(pl.multiple_of(step * rows + b * BLK, BLK), BLK)
            out[band, :] = w[b * BLK : (b + 1) * BLK, :] * keep


def tile_at(r, tile):
    return pl.ds(pl.multiple_of((r.place[0] + pl.program_id(0)) * tile, tile), tile)


def partial_kernel(r):
    at = tile_at(r, r.send.shape[2])
    gate = dot(r.tok[...], r.wg[:, at])
    up = dot(r.tok[...], r.wu[:, at])
    back = dot(r.cot[...], r.wd[at, :], (1, 1))
    for k, value in enumerate((gate, up, back)):
        if hasattr(r, "received"):
            value = value + r.received[k]
            r.own[k] = value
        r.send[k] = value.astype(r.send.dtype)


def act_kernel(r):
    others = [ref for name, ref in vars(r).items() if name.startswith("other")]
    gate, up, back = (
        sum((other[k].astype(F32) for other in others), r.own[k]) for k in range(3)
    )
    sigma = 1.0 / (1.0 + jnp.exp(-gate))
    silu = gate * sigma
    slope = sigma * (1.0 + gate * (1.0 - sigma))
    r.act[0] = (silu * up).astype(BF16)
    r.act[1] = (back * up * slope).astype(BF16)
    r.act[2] = (back * silu).astype(BF16)


def add_rows(r, tiles):
    step = pl.program_id(0)
    at = tile_at(r, r.act.shape[2])

    @pl.when(step == 0)
    def _():
        r.acc[...] = r.sums[...] if hasattr(r, "sums") else jnp.zeros_like(r.acc)

    r.acc[0] += dot(r.act[0], r.wd[at, :])
    r.acc[1] += dot(r.act[1], r.wg[:, at], (1, 1)) + dot(r.act[2], r.wu[:, at], (1, 1))

    @pl.when(step == tiles - 1)
    def _():
        if hasattr(r, "new_sums"):
            r.new_sums[...] = r.acc[...]
        else:
            outs = [ref for name, ref in vars(r).items() if name.startswith("rows")]
            rows = outs[0].shape[1]
            for k, out in enumerate(outs):
                out[...] = r.acc[:, k * rows : (k + 1) * rows, :].astype(out.dtype)


def weight_grads(r):
    tile = r.act.shape[2]
    at = tile_at(r, tile)
    for out, k, mask in ((r.gg, 1, r.mg), (r.gu, 2, r.mu)):
        value = dot(r.tok_t[...], r.act[k])
        for b in range(out.shape[0] // BLK):
            band = slice(b * BLK, (b + 1) * BLK)
            out[band, :] = value[band, :] * mask[b, :, at]
    value = dot(r.act[0].T, r.cot[...])
    for b in range(tile // BLK):
        band = slice(b * BLK, (b + 1) * BLK)
        row = (r.place[0] + pl.program_id(0)) * (tile // BLK) + b
        r.gd[band, :] = value[band, :] * r.md[row]


def back_kernel(do_rows, do_grads, tiles, r):
    if do_rows:
        add_rows(r, tiles)
    if do_grads:
        weight_grads(r)


def shards(sizes, tokens, w_gate, w_up, w_down, mask_gate, mask_up, mask_down, grad_out):
    n_grid, n_dp = sizes
    width, units = w_gate.shape
    pairs = n_dp // 2
    half = units // 2
    tile = 256 if half % 256 == 0 and half >= 1024 else BLK
    split = PIECES if sum(PIECES) * tile == half else [half // tile]
    starts = [sum(split[:p]) for p in range(len(split))]
    direct = n_grid == 4

    core = lax.axis_index("dp") % 2
    firsts = [
        jnp.stack([(half // tile) * h + start]).astype(jnp.int32)
        for h in (core, 1 - core)
        for start in starts
    ]
    place = lambda which, p: firsts[which * len(split) + p]
    none = jnp.zeros((1,), jnp.int32)

    def trade(array, s):
        return lax.ppermute(array, "grid", [(i, i ^ s) for i in range(n_grid)])

    def swap(array):
        return lax.ppermute(array, "dp", [(i, i ^ 1) for i in range(n_dp)])

    def across(array):
        return [
            lax.ppermute(
                array,
                "dp",
                [(i, ((i // 2 + s) % pairs) * 2 + i % 2) for i in range(n_dp)],
            )
            for s in range(1, pairs)
        ]

    block = jnp.stack([tokens, grad_out])
    if direct:
        blocks = [block] + [trade(block, s) for s in range(1, n_grid)]
    else:
        blocks = [lax.all_gather(block, "grid", axis=1, tiled=True)]
    rows = sum(b.shape[1] for b in blocks)
    row_shape = jax.ShapeDtypeStruct((rows, width), BF16)
    col_shape = jax.ShapeDtypeStruct((width, rows), BF16)
    bands = width // BLK
    by_cols = pl.BlockSpec((BLK, units), lambda i, _: (i, 0))
    by_rows = pl.BlockSpec((units // bands, width), lambda i, _: (i, 0))

    def spread(mask):
        return pinned(jax.ShapeDtypeStruct((mask.shape[0], 1, mask.shape[1] * BLK), F32))

    kept = call(
        mask_kernel,
        "mask",
        none,
        (bands,),
        {
            "mask_gate": (mask_gate, whole(mask_gate)),
            "mask_up": (mask_up, whole(mask_up)),
            "mask_down": (mask_down, whole(mask_down)),
            "w_gate": (hbm(w_gate), by_cols),
            "w_up": (hbm(w_up), by_cols),
            "w_down": (hbm(w_down), by_rows),
        },
        {
            "mg": spread(mask_gate),
            "mu": spread(mask_up),
            "md": spread(mask_down),
            "wg": pinned(jax.ShapeDtypeStruct(w_gate.shape, BF16)),
            "wu": pinned(jax.ShapeDtypeStruct(w_up.shape, BF16)),
            "wd": pinned(jax.ShapeDtypeStruct(w_down.shape, BF16)),
        },
        cost=pl.CostEstimate(flops=0, bytes_accessed=6 * width * units, transcendentals=0),
    )
    gathered = call(
        assemble_kernel,
        "assemble",
        none,
        (1,),
        {
            "after": (kept["mg"], pl.BlockSpec(memory_space=pl.ANY)),
            **{f"block{k}": (b, whole(b)) for k, b in enumerate(blocks)},
        },
        {"tok": pinned(row_shape), "cot": pinned(row_shape), "tok_t": pinned(col_shape)},
    )

    def held(*names):
        return {k: pinned(kept[k] if k in kept else gathered[k]) for k in names}

    trio = pl.BlockSpec((3, rows, tile), lambda i, idx: (0, 0, i))

    def trio_of(p, kind):
        return (jax.ShapeDtypeStruct((3, rows, split[p] * tile), kind), trio)

    def cost(p, matmuls, mats):
        step = width * split[p] * tile
        return pl.CostEstimate(
            flops=2 * matmuls * rows * step, bytes_accessed=2 * mats * step, transcendentals=0
        )

    def partials(which, p, after=None, received=None):
        ins = held("tok", "cot", "wg", "wu", "wd")
        outs = {"send": trio_of(p, F32)}
        if after is not None:
            ins["after"] = (after, pl.BlockSpec(memory_space=pl.ANY))
        if received is not None:
            ins["received"] = (received, trio)
            outs = {"own": trio_of(p, F32), "send": trio_of(p, BF16)}
        return call(
            partial_kernel, "partials", place(which, p), (split[p],), ins, outs, cost=cost(p, 3, 0)
        )

    def activate(own, others, after):
        ins = {"own": (own, whole(own)), "after": (after, pl.BlockSpec(memory_space=pl.ANY))}
        ins.update({f"other{k}": (a, whole(a)) for k, a in enumerate(others)})
        shape = jax.ShapeDtypeStruct(own.shape, BF16)
        return call(act_kernel, "activate", none, (1,), ins, {"act": (shape, whole(shape))})["act"]

    def back(which, p, act, do_rows, do_grads, state, last=False):
        ins = {"act": (act, trio)}
        outs, aliases, scratch = {}, {}, {}
        if do_rows:
            ins.update(held("wg", "wu", "wd"))
            shape = jax.ShapeDtypeStruct((2, rows, width), F32)
            scratch["acc"] = pltpu.VMEM(shape.shape, F32)
            if "sums" in state:
                ins["sums"] = pinned(state["sums"])
            if last:
                n_out = n_grid if direct else 1
                shape = jax.ShapeDtypeStruct((2, rows // n_out, width), BF16 if direct else F32)
                outs.update({f"rows{k}": (shape, whole(shape)) for k in range(n_out)})
            else:
                outs["new_sums"] = pinned(shape)
        if do_grads:
            ins.update(held("tok_t", "cot", "mg", "mu", "md"))
            cols = pl.BlockSpec((width, tile), lambda i, first: (0, first[0] + i))
            downs = pl.BlockSpec((tile, width), lambda i, first: (first[0] + i, 0))
            outs["gg"] = (jax.ShapeDtypeStruct((width, units), F32), cols)
            outs["gu"] = (jax.ShapeDtypeStruct((width, units), F32), cols)
            outs["gd"] = (jax.ShapeDtypeStruct((units, width), F32), downs)
            for k in ("gg", "gu", "gd"):
                if k in state:
                    ins["old_" + k] = (state[k], pl.BlockSpec(memory_space=pl.ANY))
                    aliases["old_" + k] = k
            if "rows0" in state:
                ins["after"] = (state["rows0"], pl.BlockSpec(memory_space=pl.ANY))
        got = call(
            functools.partial(back_kernel, do_rows, do_grads, split[p]),
            "_".join(["back"] + ["rows"] * do_rows + ["grads"] * do_grads),
            place(which, p),
            (split[p],),
            ins,
            outs,
            scratch=scratch,
            aliases=aliases,
            cost=cost(p, 3 * do_rows + 3 * do_grads, 6 * do_grads),
        )
        return {**state, **{k.replace("new_", ""): v for k, v in got.items()}}

    n = len(split)
    sent, sums, theirs, after = [], [], [], None
    for p in range(n + 1):
        if p < n:
            after = partials(1, p, after)["send"]
            sent.append(swap(after))
        if p > 0:
            got = partials(0, p - 1, after, sent[p - 1])
            after = got["own"]
            sums.append(after)
            theirs.append(across(got["send"]))

    state = {}
    for p in range(n):
        last = p == n - 1
        act = activate(sums[p], theirs[p], state.get("sums", after))
        act_other = swap(act)
        state = back(0, p, act, True, not last, state)
        state = back(1, p, act_other, True, not last, state, last)
        if last:
            state = back(0, p, act, False, True, state)
            state = back(1, p, act_other, False, True, state)

    if direct:
        both = state["rows0"].astype(F32)
        for s in range(1, n_grid):
            both += trade(state[f"rows{s}"], s).astype(F32)
    else:
        both = lax.psum_scatter(state["rows0"], "grid", scatter_dimension=1, tiled=True)
    both = both.astype(BF16)
    return (both[0], both[1], state["gg"], state["gu"], state["gd"])


def solution(mesh):
    in_specs = (
        P(("groups", "grid"), "dp"),
        P("dp", "grid"),
        P("dp", "grid"),
        P("grid", "dp"),
        P(("groups", "dp"), "grid"),
        P(("groups", "dp"), "grid"),
        P(("groups", "grid"), "dp"),
        P(("groups", "grid"), "dp"),
    )
    out_specs = (
        P(("groups", "grid"), "dp"),
        P(("groups", "grid"), "dp"),
        P(("groups", "dp"), "grid"),
        P(("groups", "dp"), "grid"),
        P(("groups", "grid"), "dp"),
    )
    sizes = (mesh.shape["grid"], mesh.shape["dp"])
    return jax.shard_map(
        functools.partial(shards, sizes),
        mesh=mesh,
        in_specs=in_specs,
        out_specs=out_specs,
        check_vma=False,
    )
```

```python
import functools
import types

import jax
import jax.numpy as jnp
from jax import lax
from jax.experimental import pallas as pl
from jax.experimental.pallas import tpu as pltpu
from jax.sharding import PartitionSpec as P

BLK = 128
DEPTH = 256
ANY = pl.BlockSpec(memory_space=pl.ANY)
PIECES = [3, 3, 2]
AHEAD = [(1, 0), (1, 1), (1, 2)]
MIB = 1024 * 1024
F32 = jnp.float32
BF16 = jnp.bfloat16


def dot(left, right, dims=(1, 0)):
    return lax.dot_general(
        left, right, (((dims[0],), (dims[1],)), ((), ())), preferred_element_type=F32
    )


def pinned(array):
    spec = pl.BlockSpec(memory_space=pltpu.VMEM)
    if isinstance(array, jax.ShapeDtypeStruct):
        return (pltpu.VMEM(array.shape, array.dtype), spec)
    return (pltpu.with_memory_space_constraint(array, pltpu.VMEM), spec)


def call(kernel, name, scalars, grid, ins, outs, scratch=None, aliases=None, cost=None, vmem=4):
    scratch = scratch or {}
    names = ["place", *ins, *outs, *scratch]
    in_names, out_names = list(ins), list(outs)

    def body(*refs):
        kernel(types.SimpleNamespace(**dict(zip(names, refs))))

    results = pl.pallas_call(
        body,
        out_shape=[shape for shape, _ in outs.values()],
        grid_spec=pltpu.PrefetchScalarGridSpec(
            num_scalar_prefetch=1,
            grid=grid,
            in_specs=[spec for _, spec in ins.values()],
            out_specs=[spec for _, spec in outs.values()],
            scratch_shapes=list(scratch.values()),
        ),
        input_output_aliases={
            1 + in_names.index(i): out_names.index(o) for i, o in (aliases or {}).items()
        },
        compiler_params=pltpu.CompilerParams(vmem_limit_bytes=vmem * MIB),
        cost_estimate=cost,
        name=name,
    )(scalars, *[array for array, _ in ins.values()])
    return dict(zip(out_names, results))


def hbm(array):
    return pltpu.with_memory_space_constraint(array, pltpu.HBM)


def whole(array):
    return pl.BlockSpec(array.shape, lambda *_: (0,) * len(array.shape))


def stack(rows, bands):
    return max(1, min(bands, DEPTH // rows))


def spread_kernel(r):
    def pattern(blocks):
        at = lax.broadcasted_iota(jnp.int32, (blocks, blocks * BLK), 0) * BLK
        column = lax.broadcasted_iota(jnp.int32, (blocks, blocks * BLK), 1)
        return ((column >= at) & (column < at + BLK)).astype(F32).astype(BF16)

    def entries(mask):
        return mask[...].astype(F32).astype(BF16)

    wide = pattern(r.mask_gate.shape[1])
    gate, up = dot(entries(r.mask_gate), wide), dot(entries(r.mask_up), wide)
    down = dot(entries(r.mask_down_t), pattern(r.mask_down_t.shape[0]), (0, 0))
    for value, out in ((gate, r.mg), (up, r.mu), (down, r.md)):
        for b in range(out.shape[0]):
            out[b] = value[b : b + 1, :]


def assemble_kernel(r):
    blocks = [ref for name, ref in vars(r).items() if name.startswith("block")]
    rows = blocks[0].shape[1]
    for k, block in enumerate(blocks):
        r.tok[k * rows : (k + 1) * rows, :] = block[0]
        r.cot[k * rows : (k + 1) * rows, :] = block[1]
    r.tok_t[...] = r.tok[...].T


def tile_at(r, tile):
    return pl.ds(pl.multiple_of((r.place[0] + pl.program_id(0)) * tile, tile), tile)


def keep_masked(r):
    tile = r.wg.shape[1]
    step, at = pl.program_id(0), tile_at(r, tile)
    for w, mask, out in ((r.wg, r.mg, r.kg), (r.wu, r.mu, r.ku)):
        for b in range(w.shape[0] // BLK):
            band = slice(b * BLK, (b + 1) * BLK)
            out[step, band, :] = w[band, :] * mask[b, :, at].astype(BF16)
    for b in range(tile // BLK):
        band = slice(b * BLK, (b + 1) * BLK)
        keep = r.md[(r.place[0] + step) * (tile // BLK) + b].astype(BF16)
        r.kd[step, band, :] = r.wd[band, :] * keep


def partial_kernel(r):
    if hasattr(r, "wg"):
        keep_masked(r)
    step = pl.program_id(0)
    gate = dot(r.tok[...], r.kg[step])
    up = dot(r.tok[...], r.ku[step])
    back = dot(r.cot[...], r.kd[step], (1, 1))
    for k, value in enumerate((gate, up, back)):
        if hasattr(r, "received"):
            value = value + r.received[k]
            r.own[k] = value
        r.send[k] = value.astype(r.send.dtype)


def act_kernel(r):
    others = [ref for name, ref in vars(r).items() if name.startswith("other")]
    gate, up, back = (
        sum((other[k].astype(F32) for other in others), r.own[k]) for k in range(3)
    )
    sigma = 1.0 / (1.0 + jnp.exp(-gate))
    silu = gate * sigma
    slope = sigma * (1.0 + gate * (1.0 - sigma))
    r.act[0] = (silu * up).astype(BF16)
    r.act[1] = (back * up * slope).astype(BF16)
    r.act[2] = (back * silu).astype(BF16)


def add_rows(r, tiles):
    step = pl.program_id(0)

    @pl.when(step == 0)
    def _():
        r.acc[...] = r.sums[...] if hasattr(r, "sums") else jnp.zeros_like(r.acc)

    r.acc[0] += dot(r.act[0], r.kd[step])
    r.acc[1] += dot(r.act[1], r.kg[step], (1, 1)) + dot(r.act[2], r.ku[step], (1, 1))

    @pl.when(step == tiles - 1)
    def _():
        if hasattr(r, "new_sums"):
            r.new_sums[...] = r.acc[...]
        else:
            outs = [ref for name, ref in vars(r).items() if name.startswith("rows")]
            rows = outs[0].shape[1]
            for k, out in enumerate(outs):
                out[...] = r.acc[:, k * rows : (k + 1) * rows, :].astype(out.dtype)


def weight_grads(r):
    tile = r.act.shape[2]
    at = tile_at(r, tile)
    for out, k, mask in ((r.gg, 1, r.mg), (r.gu, 2, r.mu)):
        value = dot(r.tok_t[...], r.act[k])
        for b in range(out.shape[0] // BLK):
            band = slice(b * BLK, (b + 1) * BLK)
            out[band, :] = value[band, :] * mask[b, :, at]
    value = dot(r.act[0].T, r.cot[...])
    for b in range(tile // BLK):
        band = slice(b * BLK, (b + 1) * BLK)
        row = (r.place[0] + pl.program_id(0)) * (tile // BLK) + b
        r.gd[band, :] = value[band, :] * r.md[row]


def back_kernel(do_rows, do_grads, tiles, r):
    if do_rows:
        add_rows(r, tiles)
    if do_grads:
        weight_grads(r)


def shards(sizes, tokens, w_gate, w_up, w_down, mask_gate, mask_up, mask_down, grad_out):
    n_grid, n_dp = sizes
    width, units = w_gate.shape
    pairs = n_dp // 2
    half = units // 2
    tile = 256 if half % 256 == 0 and half >= 1024 else BLK
    split = PIECES if sum(PIECES) * tile == half else [half // tile]
    starts = [sum(split[:p]) for p in range(len(split))]
    direct = n_grid == 4
    grant = lambda mib: mib if n_grid * tokens.shape[0] <= 64 else min(8 * mib, 40)

    core = lax.axis_index("dp") % 2
    firsts = [
        jnp.stack([(half // tile) * h + start]).astype(jnp.int32)
        for h in (core, 1 - core)
        for start in starts
    ]
    place = lambda which, p: firsts[which * len(split) + p]
    none = jnp.zeros((1,), jnp.int32)

    def trade(array, s):
        return lax.ppermute(array, "grid", [(i, i ^ s) for i in range(n_grid)])

    def swap(array):
        return lax.ppermute(array, "dp", [(i, i ^ 1) for i in range(n_dp)])

    def across(array):
        return [
            lax.ppermute(
                array,
                "dp",
                [(i, ((i // 2 + s) % pairs) * 2 + i % 2) for i in range(n_dp)],
            )
            for s in range(1, pairs)
        ]

    block = jnp.stack([tokens, grad_out])
    if direct:
        blocks = [block] + [trade(block, s) for s in range(1, n_grid)]
    else:
        blocks = [lax.all_gather(block, "grid", axis=1, tiled=True)]
    rows = n_grid * tokens.shape[0]
    row_shape = jax.ShapeDtypeStruct((rows, width), BF16)
    deep_shape = jax.ShapeDtypeStruct((width, rows), BF16)
    def spread_of(blocks, across):
        return pinned(jax.ShapeDtypeStruct((blocks, 1, across * BLK), F32))

    spread = call(
        spread_kernel,
        "spread",
        none,
        (1,),
        {
            k: (mask, whole(mask))
            for k, mask in (
                ("mask_gate", mask_gate),
                ("mask_up", mask_up),
                ("mask_down_t", mask_down.T),
            )
        },
        {
            "mg": spread_of(*mask_gate.shape),
            "mu": spread_of(*mask_up.shape),
            "md": spread_of(*mask_down.shape),
        },
    )

    def cost(p, matmuls, mats):
        step = width * split[p] * tile
        return pl.CostEstimate(
            flops=2 * matmuls * rows * step, bytes_accessed=2 * mats * step, transcendentals=0
        )

    def masking(p):
        cols = pl.BlockSpec((width, tile), lambda i, first: (0, first[0] + i))
        downs = pl.BlockSpec((tile, width), lambda i, first: (first[0] + i, 0))
        by_cols = jax.ShapeDtypeStruct((split[p], width, tile), BF16)
        by_rows = jax.ShapeDtypeStruct((split[p], tile, width), BF16)
        ins = {"wg": (hbm(w_gate), cols), "wu": (hbm(w_up), cols), "wd": (hbm(w_down), downs)}
        ins.update({k: pinned(v) for k, v in spread.items()})
        return ins, {"kg": pinned(by_cols), "ku": pinned(by_cols), "kd": pinned(by_rows)}

    kept = {}
    for which, p in AHEAD if direct else []:
        kept[which, p] = call(
            keep_masked,
            "keep_masked",
            place(which, p),
            (split[p],),
            *masking(p),
            cost=cost(p, 0, 3),
            vmem=grant(8),
        )
    gathered = call(
        assemble_kernel,
        "assemble",
        none,
        (1,),
        {
            **{f"after{k}": (v["kg"], ANY) for k, v in enumerate(kept.values())},
            **{f"block{k}": (b, whole(b)) for k, b in enumerate(blocks)},
        },
        {"tok": pinned(row_shape), "cot": pinned(row_shape), "tok_t": pinned(deep_shape)},
    )

    def held(*names):
        return {k: pinned(spread[k] if k in spread else gathered[k]) for k in names}

    trio = pl.BlockSpec((3, rows, tile), lambda i, idx: (0, 0, i))

    def trio_of(p, kind):
        return (jax.ShapeDtypeStruct((3, rows, split[p] * tile), kind), trio)

    def partials(which, p, after=None, received=None):
        ins, outs = held("tok", "cot"), {"send": trio_of(p, F32)}
        if (which, p) in kept:
            ins.update({k: pinned(v) for k, v in kept[which, p].items()})
            masked = {}
        else:
            weights, masked = masking(p)
            ins.update(weights)
        if after is not None:
            ins["after"] = (after, ANY)
        if received is not None:
            ins["received"] = (received, trio)
            outs = {"own": trio_of(p, F32), "send": trio_of(p, BF16)}
        got = call(
            partial_kernel,
            "partials",
            place(which, p),
            (split[p],),
            ins,
            {**outs, **masked},
            cost=cost(p, 3, 3 if masked else 0),
            vmem=grant(8 if masked else 4),
        )
        if masked:
            kept[which, p] = {k: got[k] for k in masked}
        return got

    def activate(own, others, after):
        ins = {"own": (own, whole(own)), "after": (after, ANY)}
        ins.update({f"other{k}": (a, whole(a)) for k, a in enumerate(others)})
        shape = jax.ShapeDtypeStruct(own.shape, BF16)
        return call(act_kernel, "activate", none, (1,), ins, {"act": (shape, whole(shape))})["act"]

    def back(which, p, act, do_rows, do_grads, state, last=False):
        ins = {"act": (act, trio)}
        outs, aliases, scratch = {}, {}, {}
        if do_rows:
            ins.update({k: pinned(v) for k, v in kept[which, p].items()})
            shape = jax.ShapeDtypeStruct((2, rows, width), F32)
            scratch["acc"] = pltpu.VMEM(shape.shape, F32)
            if "sums" in state:
                ins["sums"] = pinned(state["sums"])
            if last:
                n_out = n_grid if direct else 1
                shape = jax.ShapeDtypeStruct((2, rows // n_out, width), BF16 if direct else F32)
                outs.update({f"rows{k}": (shape, whole(shape)) for k in range(n_out)})
            else:
                outs["new_sums"] = pinned(shape)
        if do_grads:
            ins.update(held("tok_t", "cot", "mg", "mu", "md"))
            cols = pl.BlockSpec((width, tile), lambda i, first: (0, first[0] + i))
            downs = pl.BlockSpec((tile, width), lambda i, first: (first[0] + i, 0))
            outs["gg"] = (jax.ShapeDtypeStruct((width, units), F32), cols)
            outs["gu"] = (jax.ShapeDtypeStruct((width, units), F32), cols)
            outs["gd"] = (jax.ShapeDtypeStruct((units, width), F32), downs)
            for k in ("gg", "gu", "gd"):
                if k in state:
                    ins["old_" + k] = (state[k], ANY)
                    aliases["old_" + k] = k
            if "rows0" in state:
                ins["after"] = (state["rows0"], ANY)
        got = call(
            functools.partial(back_kernel, do_rows, do_grads, split[p]),
            "_".join(["back"] + ["rows"] * do_rows + ["grads"] * do_grads),
            place(which, p),
            (split[p],),
            ins,
            outs,
            scratch=scratch,
            aliases=aliases,
            cost=cost(p, 3 * do_rows + 3 * do_grads, 6 * do_grads),
            vmem=grant(9 if do_grads else 4),
        )
        return {**state, **{k.replace("new_", ""): v for k, v in got.items()}}

    n = len(split)
    sent, sums, theirs, after = [], [], [], None
    for p in range(n + 1):
        if p < n:
            after = partials(1, p, after)["send"]
            sent.append(swap(after))
        if p > 0:
            got = partials(0, p - 1, after, sent[p - 1])
            after = got["own"]
            sums.append(after)
            theirs.append(across(got["send"]))

    state = {}
    for p in range(n):
        last = p == n - 1
        act = activate(sums[p], theirs[p], state.get("sums", after))
        act_other = swap(act)
        state = back(0, p, act, True, not last, state)
        state = back(1, p, act_other, True, not last, state, last)
        if last:
            state = back(0, p, act, False, True, state)
            state = back(1, p, act_other, False, True, state)

    if direct:
        both = state["rows0"].astype(F32)
        for s in range(1, n_grid):
            both += trade(state[f"rows{s}"], s).astype(F32)
    else:
        both = lax.psum_scatter(state["rows0"], "grid", scatter_dimension=1, tiled=True)
    both = both.astype(BF16)
    return (both[0], both[1], state["gg"], state["gu"], state["gd"])


def solution(mesh):
    in_specs = (
        P(("groups", "grid"), "dp"),
        P("dp", "grid"),
        P("dp", "grid"),
        P("grid", "dp"),
        P(("groups", "dp"), "grid"),
        P(("groups", "dp"), "grid"),
        P(("groups", "grid"), "dp"),
        P(("groups", "grid"), "dp"),
    )
    out_specs = (
        P(("groups", "grid"), "dp"),
        P(("groups", "grid"), "dp"),
        P(("groups", "dp"), "grid"),
        P(("groups", "dp"), "grid"),
        P(("groups", "grid"), "dp"),
    )
    sizes = (mesh.shape["grid"], mesh.shape["dp"])
    return jax.shard_map(
        functools.partial(shards, sizes),
        mesh=mesh,
        in_specs=in_specs,
        out_specs=out_specs,
        check_vma=False,
    )
```

```python
import functools
import types

import jax
import jax.numpy as jnp
from jax import lax
from jax.experimental import pallas as pl
from jax.experimental.pallas import tpu as pltpu
from jax.sharding import PartitionSpec as P

BLK = 128
MIB = 1024 * 1024
DEPTH = 256
ANY = pl.BlockSpec(memory_space=pl.ANY)
PIECES = [3, 3, 2]
F32 = jnp.float32
BF16 = jnp.bfloat16


def dot(left, right, dims=(1, 0)):
    return lax.dot_general(
        left, right, (((dims[0],), (dims[1],)), ((), ())), preferred_element_type=F32
    )


def pinned(array):
    spec = pl.BlockSpec(memory_space=pltpu.VMEM)
    if isinstance(array, jax.ShapeDtypeStruct):
        return (pltpu.VMEM(array.shape, array.dtype), spec)
    return (pltpu.with_memory_space_constraint(array, pltpu.VMEM), spec)


def call(kernel, name, scalars, grid, ins, outs, scratch=None, aliases=None, cost=None, vmem=4):
    scratch = scratch or {}
    names = ["place", *ins, *outs, *scratch]
    in_names, out_names = list(ins), list(outs)

    def body(*refs):
        kernel(types.SimpleNamespace(**dict(zip(names, refs))))

    results = pl.pallas_call(
        body,
        out_shape=[shape for shape, _ in outs.values()],
        grid_spec=pltpu.PrefetchScalarGridSpec(
            num_scalar_prefetch=1,
            grid=grid,
            in_specs=[spec for _, spec in ins.values()],
            out_specs=[spec for _, spec in outs.values()],
            scratch_shapes=list(scratch.values()),
        ),
        input_output_aliases={
            1 + in_names.index(i): out_names.index(o) for i, o in (aliases or {}).items()
        },
        compiler_params=pltpu.CompilerParams(vmem_limit_bytes=vmem * MIB),
        cost_estimate=cost,
        name=name,
    )(scalars, *[array for array, _ in ins.values()])
    return dict(zip(out_names, results))


def hbm(array):
    return pltpu.with_memory_space_constraint(array, pltpu.HBM)


def whole(array):
    return pl.BlockSpec(array.shape, lambda *_: (0,) * len(array.shape))


def stack(rows, bands):
    return max(1, min(bands, DEPTH // rows))


def spread_kernel(r):
    def pattern(blocks):
        at = lax.broadcasted_iota(jnp.int32, (blocks, blocks * BLK), 0) * BLK
        column = lax.broadcasted_iota(jnp.int32, (blocks, blocks * BLK), 1)
        return ((column >= at) & (column < at + BLK)).astype(F32).astype(BF16)

    across, along = r.mask_gate.shape
    units, features = pattern(along), pattern(across)
    for mask, by_units, by_features in (
        (r.mask_gate, r.mg, r.mgt),
        (r.mask_up, r.mu, r.mut),
        (r.mask_down_t, r.mdt, r.md),
    ):
        entries = mask[...].astype(F32).astype(BF16)
        value = dot(entries, units)
        for b in range(across):
            by_units[b] = value[b : b + 1, :]
        value = dot(entries, features, (0, 0))
        for b in range(along):
            by_features[b] = value[b : b + 1, :]


def diagonal(out, value, start=0):
    rows, size = value.shape
    for b in range(size // BLK):
        band = slice(b * BLK, (b + 1) * BLK)
        out[start + b * rows : start + (b + 1) * rows, band] = value[:, band]


def assemble_kernel(r):
    blocks = [ref for name, ref in vars(r).items() if name.startswith("block")]
    rows = blocks[0].shape[1]
    tok = jnp.concatenate([block[0] for block in blocks], axis=0)
    cot = jnp.concatenate([block[1] for block in blocks], axis=0)
    r.cot[...] = cot
    rows, width = cot.shape
    pair = r.tok_d.shape[2] // BLK
    r.tok_d[...] = jnp.zeros_like(r.tok_d)
    r.cot_d[...] = jnp.zeros_like(r.cot_d)
    for p in range(width // (pair * BLK)):
        part = slice(p * pair * BLK, (p + 1) * pair * BLK)
        diagonal(r.tok_d.at[p], tok[:, part])
        diagonal(r.cot_d.at[p], cot[:, part])
    deep = stack(rows, width // BLK)
    r.bands[...] = jnp.zeros_like(r.bands)
    for b in range(width // BLK):
        band = slice(b * BLK, (b + 1) * BLK)
        slot = slice((b % deep) * rows, (b % deep + 1) * rows)
        r.bands[slot, band] = tok[:, band]
    r.tok_t[...] = r.bands[...].T


def tile_at(r, tile):
    return pl.ds(pl.multiple_of((r.place[0] + pl.program_id(0)) * tile, tile), tile)


def masked_sum(left, right, masks, dims=(1, 0)):
    value = dot(left, right, dims)
    rows = value.shape[0] // len(masks)
    return sum(value[b * rows : (b + 1) * rows, :] * m for b, m in enumerate(masks))


def partial_kernel(r):
    at = tile_at(r, r.send.shape[2])
    pairs, _, size = r.tok_d.shape
    totals = [0.0, 0.0, 0.0]
    for p in range(pairs):
        part = slice(p * size, (p + 1) * size)
        bands = range(p * size // BLK, (p + 1) * size // BLK)
        for k, (left, right, mask, dims) in enumerate(
            (
                (r.tok_d[p], r.wg[part, :], r.mg, (1, 0)),
                (r.tok_d[p], r.wu[part, :], r.mu, (1, 0)),
                (r.cot_d[p], r.wd[:, part], r.mdt, (1, 1)),
            )
        ):
            totals[k] += masked_sum(left, right, [mask[b, :, at] for b in bands], dims)
    for k, value in enumerate(totals):
        if hasattr(r, "received"):
            value = value + r.received[k]
            r.own[k] = value
        r.send[k] = value.astype(r.send.dtype)


def act_kernel(r):
    others = [ref for name, ref in vars(r).items() if name.startswith("other")]
    gate, up, back = (
        sum((other[k].astype(F32) for other in others), r.own[k]) for k in range(3)
    )
    sigma = 1.0 / (1.0 + jnp.exp(-gate))
    silu = gate * sigma
    slope = sigma * (1.0 + gate * (1.0 - sigma))
    r.act[0] = (silu * up).astype(BF16)
    r.act[1] = (back * up * slope).astype(BF16)
    r.act[2] = (back * silu).astype(BF16)


def add_rows(r, tiles):
    step = pl.program_id(0)
    width = r.acc.shape[2]
    tile = r.act.shape[2]

    @pl.when(step == 0)
    def _():
        r.acc[...] = r.sums[...] if hasattr(r, "sums") else jnp.zeros_like(r.acc)

    first = (r.place[0] + step) * (tile // BLK)
    size = min(DEPTH, width)
    for f in range(0, width, size):
        part = slice(f, f + size)

        def masks(mask):
            return [mask[first + b][:, part] for b in range(tile // BLK)]

        r.acc[0, :, part] += masked_sum(r.act_d[0], r.wd[:, part], masks(r.md))
        r.acc[1, :, part] += masked_sum(
            r.act_d[1], r.wg[part, :], masks(r.mgt), (1, 1)
        ) + masked_sum(r.act_d[2], r.wu[part, :], masks(r.mut), (1, 1))

    @pl.when(step == tiles - 1)
    def _():
        if hasattr(r, "new_sums"):
            r.new_sums[...] = r.acc[...]
        else:
            outs = [ref for name, ref in vars(r).items() if name.startswith("rows")]
            rows = outs[0].shape[1]
            for k, out in enumerate(outs):
                out[...] = r.acc[:, k * rows : (k + 1) * rows, :].astype(out.dtype)


def weight_grads(r):
    _, rows, tile = r.act.shape
    at = tile_at(r, tile)
    deep = r.tok_t.shape[1] // rows
    for out, k, mask in ((r.gg, 1, r.mg), (r.gu, 2, r.mu)):
        for g in range(out.shape[0] // (deep * BLK)):
            right = r.masked_act.at[k - 1, g]
            for j in range(deep):
                keep = mask[g * deep + j, :, at].astype(BF16)
                right[j * rows : (j + 1) * rows, :] = r.act[k] * keep
            group = slice(g * deep * BLK, (g + 1) * deep * BLK)
            out[group, :] = dot(r.tok_t[group, :], right[...])
    first = (r.place[0] + pl.program_id(0)) * (tile // BLK)
    for b in range(tile // BLK):
        r.masked_cot[b * rows : (b + 1) * rows, :] = r.cot[...] * r.md[first + b].astype(BF16)
    r.gd[...] = dot(r.act_d[0].T, r.masked_cot[...])


def back_kernel(do_rows, do_grads, tiles, r):
    @pl.when(pl.program_id(0) == 0)
    def _():
        r.act_d[...] = jnp.zeros_like(r.act_d)

    for k in range(3 if do_rows else 1):
        diagonal(r.act_d.at[k], r.act[k])
    if do_rows:
        add_rows(r, tiles)
    if do_grads:
        weight_grads(r)


def shards(sizes, tokens, w_gate, w_up, w_down, mask_gate, mask_up, mask_down, grad_out):
    n_grid, n_dp = sizes
    width, units = w_gate.shape
    pairs = n_dp // 2
    half = units // 2
    tile = 256 if half % 256 == 0 and half >= 1024 else BLK
    split = PIECES if sum(PIECES) * tile == half else [half // tile]
    starts = [sum(split[:p]) for p in range(len(split))]
    direct = n_grid == 4
    grant = lambda mib: mib if n_grid * tokens.shape[0] <= 64 else min(8 * mib, 40)

    core = lax.axis_index("dp") % 2
    firsts = [
        jnp.stack([(half // tile) * h + start]).astype(jnp.int32)
        for h in (core, 1 - core)
        for start in starts
    ]
    place = lambda which, p: firsts[which * len(split) + p]
    none = jnp.zeros((1,), jnp.int32)

    def trade(array, s):
        return lax.ppermute(array, "grid", [(i, i ^ s) for i in range(n_grid)])

    def swap(array):
        return lax.ppermute(array, "dp", [(i, i ^ 1) for i in range(n_dp)])

    def across(array):
        return [
            lax.ppermute(
                array,
                "dp",
                [(i, ((i // 2 + s) % pairs) * 2 + i % 2) for i in range(n_dp)],
            )
            for s in range(1, pairs)
        ]

    block = jnp.stack([tokens, grad_out])
    if direct:
        blocks = [block] + [trade(block, s) for s in range(1, n_grid)]
    else:
        blocks = [lax.all_gather(block, "grid", axis=1, tiled=True)]
    rows = n_grid * tokens.shape[0]
    pair = min(2, width // BLK)
    deep = stack(rows, width // BLK)
    row_shape = jax.ShapeDtypeStruct((rows, width), BF16)
    pair_shape = jax.ShapeDtypeStruct((width // (pair * BLK), pair * rows, pair * BLK), BF16)
    deep_shape = jax.ShapeDtypeStruct((width, deep * rows), BF16)

    def spread_of(blocks, across):
        return pinned(jax.ShapeDtypeStruct((blocks, 1, across * BLK), F32))

    spread = call(
        spread_kernel,
        "spread",
        none,
        (1,),
        {
            k: (mask, whole(mask))
            for k, mask in (
                ("mask_gate", mask_gate),
                ("mask_up", mask_up),
                ("mask_down_t", mask_down.T),
            )
        },
        {
            "mg": spread_of(width // BLK, units // BLK),
            "mu": spread_of(width // BLK, units // BLK),
            "mdt": spread_of(width // BLK, units // BLK),
            "mgt": spread_of(units // BLK, width // BLK),
            "mut": spread_of(units // BLK, width // BLK),
            "md": spread_of(units // BLK, width // BLK),
        },
        vmem=grant(4),
    )

    def cost(p, matmuls, mats):
        step = width * split[p] * tile
        return pl.CostEstimate(
            flops=2 * matmuls * rows * step, bytes_accessed=2 * mats * step, transcendentals=0
        )

    def weights():
        cols = pl.BlockSpec((width, tile), lambda i, first: (0, first[0] + i))
        downs = pl.BlockSpec((tile, width), lambda i, first: (first[0] + i, 0))
        return {"wg": (hbm(w_gate), cols), "wu": (hbm(w_up), cols), "wd": (hbm(w_down), downs)}

    gathered = call(
        assemble_kernel,
        "assemble",
        none,
        (1,),
        {
            "after": (spread["mg"], ANY),
            **{f"block{k}": (b, whole(b)) for k, b in enumerate(blocks)},
        },
        {
            "cot": pinned(row_shape),
            "tok_d": pinned(pair_shape),
            "cot_d": pinned(pair_shape),
            "tok_t": pinned(deep_shape),
        },
        scratch={"bands": pltpu.VMEM(deep_shape.shape[::-1], BF16)},
        vmem=grant(4),
    )

    def held(*names):
        return {k: pinned(spread[k] if k in spread else gathered[k]) for k in names}

    trio = pl.BlockSpec((3, rows, tile), lambda i, idx: (0, 0, i))

    def trio_of(p, kind):
        return (jax.ShapeDtypeStruct((3, rows, split[p] * tile), kind), trio)

    def partials(which, p, after=None, received=None):
        ins = {**held("tok_d", "cot_d", "mg", "mu", "mdt"), **weights()}
        outs = {"send": trio_of(p, F32)}
        if after is not None:
            ins["after"] = (after, ANY)
        if received is not None:
            ins["received"] = (received, trio)
            outs = {"own": trio_of(p, F32), "send": trio_of(p, BF16)}
        return call(
            partial_kernel,
            "partials",
            place(which, p),
            (split[p],),
            ins,
            outs,
            cost=cost(p, 3, 3),
            vmem=grant(6),
        )

    def activate(own, others, after):
        ins = {"own": (own, whole(own)), "after": (after, ANY)}
        ins.update({f"other{k}": (a, whole(a)) for k, a in enumerate(others)})
        shape = jax.ShapeDtypeStruct(own.shape, BF16)
        return call(act_kernel, "activate", none, (1,), ins, {"act": (shape, whole(shape))})["act"]

    def back(which, p, act, do_rows, do_grads, state, last=False):
        ins = {"act": (act, trio)}
        outs, aliases = {}, {}
        spots = tile // BLK
        scratch = {"act_d": pltpu.VMEM((3, spots * rows, tile), BF16)}
        if do_rows:
            ins.update({**weights(), **held("md", "mgt", "mut")})
            shape = jax.ShapeDtypeStruct((2, rows, width), F32)
            scratch["acc"] = pltpu.VMEM(shape.shape, F32)
            if "sums" in state:
                ins["sums"] = pinned(state["sums"])
            if last:
                n_out = n_grid if direct else 1
                shape = jax.ShapeDtypeStruct((2, rows // n_out, width), BF16 if direct else F32)
                outs.update({f"rows{k}": (shape, whole(shape)) for k in range(n_out)})
            else:
                outs["new_sums"] = pinned(shape)
        if do_grads:
            ins.update(held("tok_t", "cot", "mg", "mu", "md"))
            cols = pl.BlockSpec((width, tile), lambda i, first: (0, first[0] + i))
            downs = pl.BlockSpec((tile, width), lambda i, first: (first[0] + i, 0))
            outs["gg"] = (jax.ShapeDtypeStruct((width, units), F32), cols)
            outs["gu"] = (jax.ShapeDtypeStruct((width, units), F32), cols)
            outs["gd"] = (jax.ShapeDtypeStruct((units, width), F32), downs)
            scratch["masked_act"] = pltpu.VMEM((2, width // (deep * BLK), deep * rows, tile), BF16)
            scratch["masked_cot"] = pltpu.VMEM((spots * rows, width), BF16)
            for k in ("gg", "gu", "gd"):
                if k in state:
                    ins["old_" + k] = (state[k], ANY)
                    aliases["old_" + k] = k
            if "rows0" in state:
                ins["after"] = (state["rows0"], ANY)
        got = call(
            functools.partial(back_kernel, do_rows, do_grads, split[p]),
            "_".join(["back"] + ["rows"] * do_rows + ["grads"] * do_grads),
            place(which, p),
            (split[p],),
            ins,
            outs,
            scratch=scratch,
            aliases=aliases,
            cost=cost(p, 3 * do_rows + 3 * do_grads, 3 * do_rows + 6 * do_grads),
            vmem=grant(14 if do_rows and do_grads else 10),
        )
        return {**state, **{k.replace("new_", ""): v for k, v in got.items()}}

    n = len(split)
    sent, sums, theirs, after = [], [], [], None
    for p in range(n + 1):
        if p < n:
            after = partials(1, p, after)["send"]
            sent.append(swap(after))
        if p > 0:
            got = partials(0, p - 1, after, sent[p - 1])
            after = got["own"]
            sums.append(after)
            theirs.append(across(got["send"]))

    state = {}
    for p in range(n):
        last = p == n - 1
        act = activate(sums[p], theirs[p], state.get("sums", after))
        act_other = swap(act)
        state = back(0, p, act, True, not last, state)
        state = back(1, p, act_other, True, not last, state, last)
        if last:
            state = back(0, p, act, False, True, state)
            state = back(1, p, act_other, False, True, state)

    if direct:
        both = state["rows0"].astype(F32)
        for s in range(1, n_grid):
            both += trade(state[f"rows{s}"], s).astype(F32)
    else:
        both = lax.psum_scatter(state["rows0"], "grid", scatter_dimension=1, tiled=True)
    both = both.astype(BF16)
    return (both[0], both[1], state["gg"], state["gu"], state["gd"])


def solution(mesh):
    in_specs = (
        P(("groups", "grid"), "dp"),
        P("dp", "grid"),
        P("dp", "grid"),
        P("grid", "dp"),
        P(("groups", "dp"), "grid"),
        P(("groups", "dp"), "grid"),
        P(("groups", "grid"), "dp"),
        P(("groups", "grid"), "dp"),
    )
    out_specs = (
        P(("groups", "grid"), "dp"),
        P(("groups", "grid"), "dp"),
        P(("groups", "dp"), "grid"),
        P(("groups", "dp"), "grid"),
        P(("groups", "grid"), "dp"),
    )
    sizes = (mesh.shape["grid"], mesh.shape["dp"])
    return jax.shard_map(
        functools.partial(shards, sizes),
        mesh=mesh,
        in_specs=in_specs,
        out_specs=out_specs,
        check_vma=False,
    )
```

```python
import functools
import types

import jax
import jax.numpy as jnp
from jax import lax
from jax.experimental import pallas as pl
from jax.experimental.pallas import tpu as pltpu
from jax.sharding import PartitionSpec as P

BLK = 128
MIB = 1024 * 1024
DEPTH = 256
ANY = pl.BlockSpec(memory_space=pl.ANY)
PIECES = [3, 3, 2]
KEPT = ("kg", "ku", "kd")
F32 = jnp.float32
BF16 = jnp.bfloat16


def dot(left, right, dims=(1, 0)):
    return lax.dot_general(
        left, right, (((dims[0],), (dims[1],)), ((), ())), preferred_element_type=F32
    )


def pinned(array):
    spec = pl.BlockSpec(memory_space=pltpu.VMEM)
    if isinstance(array, jax.ShapeDtypeStruct):
        return (pltpu.VMEM(array.shape, array.dtype), spec)
    return (pltpu.with_memory_space_constraint(array, pltpu.VMEM), spec)


def call(kernel, name, scalars, ins, outs, scratch=None, aliases=None, cost=None, vmem=2):
    scratch = scratch or {}
    names = ["place", *ins, *outs, *scratch]
    in_names, out_names = list(ins), list(outs)

    def body(*refs):
        kernel(types.SimpleNamespace(**dict(zip(names, refs))))

    results = pl.pallas_call(
        body,
        out_shape=[shape for shape, _ in outs.values()],
        grid_spec=pltpu.PrefetchScalarGridSpec(
            num_scalar_prefetch=1,
            grid=(1,),
            in_specs=[spec for _, spec in ins.values()],
            out_specs=[spec for _, spec in outs.values()],
            scratch_shapes=list(scratch.values()),
        ),
        input_output_aliases={
            1 + in_names.index(i): out_names.index(o) for i, o in (aliases or {}).items()
        },
        compiler_params=pltpu.CompilerParams(vmem_limit_bytes=vmem * MIB),
        cost_estimate=cost,
        name=name,
    )(scalars, *[array for array, _ in ins.values()])
    return dict(zip(out_names, results))


def hbm(array):
    return pltpu.with_memory_space_constraint(array, pltpu.HBM)


def whole(array):
    return pl.BlockSpec(array.shape, lambda *_: (0,) * len(array.shape))


def spread(r):
    def pattern(blocks):
        at = lax.broadcasted_iota(jnp.int32, (blocks, blocks * BLK), 0) * BLK
        column = lax.broadcasted_iota(jnp.int32, (blocks, blocks * BLK), 1)
        return ((column >= at) & (column < at + BLK)).astype(F32).astype(BF16)

    across, along = r.mask_gate.shape
    units, features = pattern(along), pattern(across)
    for mask, by_units, by_features in (
        (r.mask_gate, r.mg, r.mgt),
        (r.mask_up, r.mu, r.mut),
        (r.mask_down_t, r.mdt, r.md),
    ):
        entries = mask[...].astype(F32).astype(BF16)
        value = dot(entries, units)
        for b in range(across):
            by_units[b] = value[b : b + 1, :]
        value = dot(entries, features, (0, 0))
        for b in range(along):
            by_features[b] = value[b : b + 1, :]


def span(start, size):
    return pl.ds(pl.multiple_of(start, BLK), size)


def fetch(r, which, starts, into, sems):
    copies = []
    for start, (gate, up, down) in zip(starts, into):
        at = span(r.place[which] + start, down.shape[0])
        for source, target in (
            (r.w_gate.at[:, at], gate),
            (r.w_up.at[:, at], up),
            (r.w_down.at[at, :], down),
        ):
            copies.append(pltpu.make_async_copy(source, target, sems.at[len(copies)]))
            copies[-1].start()
    return copies


def fetch_kernel(starts, r):
    into = [[getattr(r, f"{k}{p}") for k in KEPT] for p in range(len(starts))]
    copies = fetch(r, 1, starts, into, r.sems)
    spread(r)
    for copy in copies:
        copy.wait()


def diagonal(out, value):
    rows, size = value.shape
    for b in range(size // BLK):
        band = slice(b * BLK, (b + 1) * BLK)
        out[b * rows : (b + 1) * rows, band] = value[:, band]


def assemble_kernel(r):
    blocks = [ref for name, ref in vars(r).items() if name.startswith("block")]
    tok = jnp.concatenate([block[0] for block in blocks], axis=0)
    cot = jnp.concatenate([block[1] for block in blocks], axis=0)
    r.cot[...] = cot
    size = r.tok_d.shape[2]
    r.tok_d[...] = jnp.zeros_like(r.tok_d)
    r.cot_d[...] = jnp.zeros_like(r.cot_d)
    for p in range(r.tok_d.shape[0]):
        part = slice(p * size, (p + 1) * size)
        diagonal(r.tok_d.at[p], tok[:, part])
        diagonal(r.cot_d.at[p], cot[:, part])
    for p in range(r.tok_d.shape[0]):
        r.tok_t[p] = r.tok_d[p].T


def masked_sum(left, right, masks, dims=(1, 0)):
    value = dot(left, right, dims)
    rows = value.shape[0] // len(masks)
    return sum(value[b * rows : (b + 1) * rows, :] * m for b, m in enumerate(masks))


def partial_kernel(which, start, tile, r):
    copies = []
    if hasattr(r, "sems"):
        copies = fetch(r, 0, [start], [(r.new_kg, r.new_ku, r.new_kd)], r.sems)
    pairs, _, size = r.tok_d.shape
    for first in range(0, r.send.shape[2], tile):
        at = span(r.place[which] + start + first, tile)
        local = slice(first, first + tile)
        totals = [0.0, 0.0, 0.0]
        for p in range(pairs):
            part = slice(p * size, (p + 1) * size)
            bands = range(p * size // BLK, (p + 1) * size // BLK)
            for k, (left, right, mask, dims) in enumerate(
                (
                    (r.tok_d[p], r.kg[part, local], r.mg, (1, 0)),
                    (r.tok_d[p], r.ku[part, local], r.mu, (1, 0)),
                    (r.cot_d[p], r.kd[local, part], r.mdt, (1, 1)),
                )
            ):
                totals[k] += masked_sum(left, right, [mask[b, :, at] for b in bands], dims)
        for k, value in enumerate(totals):
            if hasattr(r, "received"):
                value = value + r.received[k, :, local]
                r.own[k, :, local] = value
            r.send[k, :, local] = value.astype(r.send.dtype)
    for copy in copies:
        copy.wait()


def act_kernel(r):
    others = [ref for name, ref in vars(r).items() if name.startswith("other")]
    gate, up, back = (
        sum((other[k].astype(F32) for other in others), r.own[k]) for k in range(3)
    )
    sigma = 1.0 / (1.0 + jnp.exp(-gate))
    silu = gate * sigma
    slope = sigma * (1.0 + gate * (1.0 - sigma))
    r.act[0] = (silu * up).astype(BF16)
    r.act[1] = (back * up * slope).astype(BF16)
    r.act[2] = (back * silu).astype(BF16)


def add_rows(r, block, local):
    width, tile = r.acc.shape[2], r.act_d.shape[2]
    size = min(DEPTH, width)
    for f in range(0, width, size):
        part = slice(f, f + size)

        def masks(mask):
            return [mask[block + b][:, part] for b in range(tile // BLK)]

        r.acc[0, :, part] += masked_sum(r.act_d[0], r.kd[local, part], masks(r.md))
        r.acc[1, :, part] += masked_sum(
            r.act_d[1], r.kg[part, local], masks(r.mgt), (1, 1)
        ) + masked_sum(r.act_d[2], r.ku[part, local], masks(r.mut), (1, 1))


class Outbox:
    def __init__(self, slots, sems):
        self.slots, self.sems = slots, sems
        self.flying, self.count = [None] * slots.shape[0], 0

    def put(self, value, target):
        k = self.count % len(self.flying)
        self.count += 1
        if self.flying[k] is not None:
            self.flying[k].wait()
        self.slots[k] = value
        self.flying[k] = pltpu.make_async_copy(self.slots.at[k], target, self.sems.at[k])
        self.flying[k].start()

    def close(self):
        for copy in self.flying:
            if copy is not None:
                copy.wait()


def back_kernel(which, start, do_rows, do_grads, r):
    _, rows, size = r.act.shape
    tile = r.act_d.shape[2]
    base = r.place[which] + start
    at = span(base, size)
    r.act_d[...] = jnp.zeros_like(r.act_d)
    groups = 0
    if do_rows:
        r.acc[...] = r.sums[...] if hasattr(r, "sums") else jnp.zeros_like(r.acc)
    if do_grads:
        groups, height, _ = r.tok_t.shape
        by_cols, by_rows = Outbox(r.col_slots, r.col_sems), Outbox(r.row_slots, r.row_sems)
    for i in range(max(groups, size // tile)):
        if i < groups:
            band = slice(i * height, (i + 1) * height)
            for out, k, mask in ((r.gg, 1, r.mg), (r.gu, 2, r.mu)):
                right = r.masked_act.at[k - 1]
                for j in range(height // BLK):
                    keep = mask[i * (height // BLK) + j, :, at].astype(BF16)
                    right[j * rows : (j + 1) * rows, :] = r.act[k] * keep
                by_cols.put(dot(r.tok_t[i], right[...]), out.at[band, at])
        if i < size // tile:
            local = slice(i * tile, (i + 1) * tile)
            for k in range(3 if do_rows else 1):
                diagonal(r.act_d.at[k], r.act[k, :, local])
            block = lax.div(base, BLK) + i * (tile // BLK)
            if do_grads:
                for b in range(tile // BLK):
                    keep = r.md[block + b].astype(BF16)
                    r.masked_cot[b * rows : (b + 1) * rows, :] = r.cot[...] * keep
                value = dot(r.act_d[0].T, r.masked_cot[...])
                by_rows.put(value, r.gd.at[span(base + i * tile, tile), :])
            if do_rows:
                add_rows(r, block, local)
    if do_rows:
        if hasattr(r, "new_sums"):
            r.new_sums[...] = r.acc[...]
        else:
            outs = [ref for name, ref in vars(r).items() if name.startswith("rows")]
            count = outs[0].shape[1]
            for k, out in enumerate(outs):
                out[...] = r.acc[:, k * count : (k + 1) * count, :].astype(out.dtype)
    if do_grads:
        by_cols.close()
        by_rows.close()


def shards(sizes, tokens, w_gate, w_up, w_down, mask_gate, mask_up, mask_down, grad_out):
    n_grid, n_dp = sizes
    width, units = w_gate.shape
    rows = n_grid * tokens.shape[0]
    pairs = n_dp // 2
    half = units // 2
    tile = min(DEPTH, half)
    split = PIECES if sum(PIECES) * tile == half else [half // tile]
    split = [tile * count for count in split]
    starts = [sum(split[:p]) for p in range(len(split))]
    n = len(split)
    direct = n_grid == 4
    grant = lambda mib: mib if rows <= 64 else 32

    core = lax.axis_index("dp") % 2
    place = jnp.stack([core * half, (1 - core) * half]).astype(jnp.int32)

    def trade(array, s):
        return lax.ppermute(array, "grid", [(i, i ^ s) for i in range(n_grid)])

    def swap(array):
        return lax.ppermute(array, "dp", [(i, i ^ 1) for i in range(n_dp)])

    def across(array):
        return [
            lax.ppermute(
                array,
                "dp",
                [(i, ((i // 2 + s) % pairs) * 2 + i % 2) for i in range(n_dp)],
            )
            for s in range(1, pairs)
        ]

    def cost(p, matmuls, mats):
        step = width * split[p]
        return pl.CostEstimate(
            flops=2 * matmuls * rows * step, bytes_accessed=2 * mats * step, transcendentals=0
        )

    def shape(*dims, kind=BF16):
        return jax.ShapeDtypeStruct(dims, kind)

    weights = {"w_gate": (w_gate, ANY), "w_up": (w_up, ANY), "w_down": (w_down, ANY)}
    weights = {k: (hbm(w), spec) for k, (w, spec) in weights.items()}

    def kept_shapes(p):
        return [shape(width, split[p]), shape(width, split[p]), shape(split[p], width)]

    block = jnp.stack([tokens, grad_out])
    if direct:
        blocks = [block] + [trade(block, s) for s in range(1, n_grid)]
    else:
        blocks = [lax.all_gather(block, "grid", axis=1, tiled=True)]

    across_shape = shape(width // BLK, 1, units, kind=F32)
    along_shape = shape(units // BLK, 1, width, kind=F32)
    masks = {"mask_gate": mask_gate, "mask_up": mask_up, "mask_down_t": mask_down.T}
    got = call(
        functools.partial(fetch_kernel, starts),
        "fetch",
        place,
        {**weights, **{k: (hbm(m), whole(m)) for k, m in masks.items()}},
        {
            **{k: pinned(across_shape) for k in ("mg", "mu", "mdt")},
            **{k: pinned(along_shape) for k in ("mgt", "mut", "md")},
            **{f"{k}{p}": pinned(s) for p in range(n) for k, s in zip(KEPT, kept_shapes(p))},
        },
        scratch={"sems": pltpu.SemaphoreType.DMA((3 * n,))},
        cost=pl.CostEstimate(flops=0, bytes_accessed=6 * width * half, transcendentals=0),
        vmem=grant(4),
    )
    values = {k: got[k] for k in ("mg", "mu", "mdt", "mgt", "mut", "md")}
    kept = {(1, p): {k: got[f"{k}{p}"] for k in KEPT} for p in range(n)}

    pair = min(DEPTH, width) // BLK
    pair_shape = shape(width // (pair * BLK), pair * rows, pair * BLK)
    values |= call(
        assemble_kernel,
        "assemble",
        place,
        {
            "after": (values["mg"], ANY),
            **{f"block{k}": (b, whole(b)) for k, b in enumerate(blocks)},
        },
        {
            "cot": pinned(shape(rows, width)),
            "tok_d": pinned(pair_shape),
            "cot_d": pinned(pair_shape),
            "tok_t": pinned(shape(pair_shape.shape[0], pair * BLK, pair * rows)),
        },
        vmem=grant(4),
    )

    def held(*names):
        return {k: pinned(values[k]) for k in names}

    def partials(which, p, after=None, received=None):
        trio = (3, rows, split[p])
        ins = held("tok_d", "cot_d", "mg", "mu", "mdt")
        ins.update({k: pinned(v) for k, v in kept[which, p].items()})
        outs, scratch = {"send": pinned(shape(*trio, kind=F32))}, {}
        if after is not None:
            ins["after"] = (after, ANY)
        if received is None:
            ins.update(weights)
            outs.update({"new_" + k: pinned(s) for k, s in zip(KEPT, kept_shapes(p))})
            scratch["sems"] = pltpu.SemaphoreType.DMA((3,))
        else:
            ins["received"] = pinned(received)
            outs = {"own": pinned(shape(*trio, kind=F32)), "send": pinned(shape(*trio))}
        got = call(
            functools.partial(partial_kernel, which, starts[p], tile),
            "partials",
            place,
            ins,
            outs,
            scratch=scratch,
            cost=cost(p, 3, 3),
            vmem=grant(2),
        )
        if received is None:
            kept[0, p] = {k: got["new_" + k] for k in KEPT}
        return got

    def activate(own, others, after):
        ins = {"own": pinned(own), "after": (after, ANY)}
        ins.update({f"other{k}": pinned(a) for k, a in enumerate(others)})
        outs = {"act": pinned(shape(*own.shape))}
        return call(act_kernel, "activate", place, ins, outs, vmem=grant(2))["act"]

    def back(which, p, act, do_rows, do_grads, state, last=False):
        ins = {"act": pinned(act), **held("md")}
        outs, aliases = {}, {}
        spots, size = tile // BLK, split[p]
        scratch = {"act_d": pltpu.VMEM((3, spots * rows, tile), BF16)}
        if do_rows:
            ins.update({k: pinned(v) for k, v in kept[which, p].items()})
            ins.update(held("mgt", "mut"))
            scratch["acc"] = pltpu.VMEM((2, rows, width), F32)
            if "sums" in state:
                ins["sums"] = pinned(state["sums"])
            if last:
                n_out = n_grid if direct else 1
                out = shape(2, rows // n_out, width, kind=BF16 if direct else F32)
                outs.update({f"rows{k}": pinned(out) for k in range(n_out)})
            else:
                outs["new_sums"] = pinned(shape(2, rows, width, kind=F32))
        if do_grads:
            ins.update(held("tok_t", "cot", "mg", "mu"))
            outs["gg"] = (shape(width, units, kind=F32), ANY)
            outs["gu"] = (shape(width, units, kind=F32), ANY)
            outs["gd"] = (shape(units, width, kind=F32), ANY)
            scratch["masked_act"] = pltpu.VMEM((2, pair * rows, size), BF16)
            scratch["masked_cot"] = pltpu.VMEM((spots * rows, width), BF16)
            scratch["col_slots"] = pltpu.VMEM((4, pair * BLK, size), F32)
            scratch["row_slots"] = pltpu.VMEM((2, tile, width), F32)
            scratch["col_sems"] = pltpu.SemaphoreType.DMA((4,))
            scratch["row_sems"] = pltpu.SemaphoreType.DMA((2,))
            for k in ("gg", "gu", "gd"):
                if k in state:
                    ins["old_" + k] = (state[k], ANY)
                    aliases["old_" + k] = k
            if "rows0" in state:
                ins["after"] = (state["rows0"], ANY)
        got = call(
            functools.partial(back_kernel, which, starts[p], do_rows, do_grads),
            "_".join(["back"] + ["rows"] * do_rows + ["grads"] * do_grads),
            place,
            ins,
            outs,
            scratch=scratch,
            aliases=aliases,
            cost=cost(p, 3 * do_rows + 3 * do_grads, 6 * do_grads),
            vmem=grant(9 if do_grads else 3),
        )
        return {**state, **{k.replace("new_", ""): v for k, v in got.items()}}

    sent, sums, theirs, after = [], [], [], None
    for p in range(n + 1):
        if p < n:
            after = partials(1, p, after)["send"]
            sent.append(swap(after))
        if p > 0:
            got = partials(0, p - 1, after, sent[p - 1])
            after = got["own"]
            sums.append(after)
            theirs.append(across(got["send"]))

    state = {}
    for p in range(n):
        last = p == n - 1
        act = activate(sums[p], theirs[p], state.get("sums", after))
        act_other = swap(act)
        state = back(0, p, act, True, not last, state)
        state = back(1, p, act_other, True, not last, state, last)
        if last:
            state = back(0, p, act, False, True, state)
            state = back(1, p, act_other, False, True, state)

    if direct:
        both = state["rows0"].astype(F32)
        for s in range(1, n_grid):
            both += trade(state[f"rows{s}"], s).astype(F32)
    else:
        both = lax.psum_scatter(state["rows0"], "grid", scatter_dimension=1, tiled=True)
    both = both.astype(BF16)
    return (both[0], both[1], state["gg"], state["gu"], state["gd"])


def solution(mesh):
    in_specs = (
        P(("groups", "grid"), "dp"),
        P("dp", "grid"),
        P("dp", "grid"),
        P("grid", "dp"),
        P(("groups", "dp"), "grid"),
        P(("groups", "dp"), "grid"),
        P(("groups", "grid"), "dp"),
        P(("groups", "grid"), "dp"),
    )
    out_specs = (
        P(("groups", "grid"), "dp"),
        P(("groups", "grid"), "dp"),
        P(("groups", "dp"), "grid"),
        P(("groups", "dp"), "grid"),
        P(("groups", "grid"), "dp"),
    )
    sizes = (mesh.shape["grid"], mesh.shape["dp"])
    return jax.shard_map(
        functools.partial(shards, sizes),
        mesh=mesh,
        in_specs=in_specs,
        out_specs=out_specs,
        check_vma=False,
    )
```

```python
import functools
import types

import jax
import jax.numpy as jnp
from jax import lax
from jax.experimental import pallas as pl
from jax.experimental.pallas import tpu as pltpu
from jax.sharding import PartitionSpec as P

BLK = 128
MIB = 1024 * 1024
DEPTH = 256
ANY = pl.BlockSpec(memory_space=pl.ANY)
PIECES = [2, 3, 3]
SPLIT = 4
KEPT = ("kg", "ku", "kd")
F32 = jnp.float32
BF16 = jnp.bfloat16


def dot(left, right, dims=(1, 0)):
    return lax.dot_general(
        left, right, (((dims[0],), (dims[1],)), ((), ())), preferred_element_type=F32
    )


def pinned(array):
    spec = pl.BlockSpec(memory_space=pltpu.VMEM)
    if isinstance(array, jax.ShapeDtypeStruct):
        return (pltpu.VMEM(array.shape, array.dtype), spec)
    return (pltpu.with_memory_space_constraint(array, pltpu.VMEM), spec)


def call(kernel, name, scalars, ins, outs, scratch=None, aliases=None, vmem=2):
    scratch = scratch or {}
    names = ["place", *ins, *outs, *scratch]
    in_names, out_names = list(ins), list(outs)

    def body(*refs):
        kernel(types.SimpleNamespace(**dict(zip(names, refs))))

    results = pl.pallas_call(
        body,
        out_shape=[shape for shape, _ in outs.values()],
        grid_spec=pltpu.PrefetchScalarGridSpec(
            num_scalar_prefetch=1,
            grid=(1,),
            in_specs=[spec for _, spec in ins.values()],
            out_specs=[spec for _, spec in outs.values()],
            scratch_shapes=list(scratch.values()),
        ),
        input_output_aliases={
            1 + in_names.index(i): out_names.index(o) for i, o in (aliases or {}).items()
        },
        compiler_params=pltpu.CompilerParams(vmem_limit_bytes=vmem * MIB),
        cost_estimate=pl.CostEstimate(flops=1, bytes_accessed=1, transcendentals=0),
        name=name,
    )(scalars, *[array for array, _ in ins.values()])
    return dict(zip(out_names, results))


def hbm(array):
    return pltpu.with_memory_space_constraint(array, pltpu.HBM)


def whole(array):
    return pl.BlockSpec(array.shape, lambda *_: (0,) * len(array.shape))


def spread(r):
    def pattern(blocks):
        at = lax.broadcasted_iota(jnp.int32, (blocks, blocks * BLK), 0) * BLK
        column = lax.broadcasted_iota(jnp.int32, (blocks, blocks * BLK), 1)
        return ((column >= at) & (column < at + BLK)).astype(F32).astype(BF16)

    across, along = r.mask_gate.shape
    units, features = pattern(along), pattern(across)
    for mask, by_units, by_features in (
        (r.mask_gate, r.mg, r.mgt),
        (r.mask_up, r.mu, r.mut),
        (r.mask_down_t, r.mdt, r.md),
    ):
        entries = mask[...].astype(F32).astype(BF16)
        value = dot(entries, units)
        for b in range(across):
            by_units[b] = value[b : b + 1, :]
        value = dot(entries, features, (0, 0))
        for b in range(along):
            by_features[b] = value[b : b + 1, :]


def span(start, size):
    return pl.ds(pl.multiple_of(start, BLK), size)


def fetch(r, loads, sems):
    copies = []

    for which, first, targets in loads:
        gate, up, down = (getattr(r, name) for name in targets)
        size, width = down.shape
        base = r.place[which] + first
        for source, target in ((r.w_gate, gate), (r.w_up, up)):
            for row in range(0, width, width // SPLIT):
                rows = slice(row, row + width // SPLIT)
                copies.append((source.at[rows, span(base, size)], target.at[rows, :]))
        for row in range(0, size, BLK):
            copies.append((r.w_down.at[span(base + row, BLK), :], down.at[row : row + BLK, :]))
    copies = [pltpu.make_async_copy(a, b, sems.at[k]) for k, (a, b) in enumerate(copies)]
    for copy in copies:
        copy.start()
    return copies


def count_copies(sizes):
    return sum(2 * SPLIT + size // BLK for size in sizes)


def fetch_kernel(loads, r):
    copies = fetch(r, loads, r.sems)
    spread(r)
    for copy in copies:
        copy.wait()


def diagonal(out, value):
    rows, size = value.shape
    for b in range(size // BLK):
        band = slice(b * BLK, (b + 1) * BLK)
        out[b * rows : (b + 1) * rows, band] = value[:, band]


def assemble_kernel(r):
    blocks = [ref for name, ref in vars(r).items() if name.startswith("block")]
    tok = jnp.concatenate([block[0] for block in blocks], axis=0)
    cot = jnp.concatenate([block[1] for block in blocks], axis=0)
    r.cot[...] = cot
    size = r.tok_d.shape[2]
    r.tok_d[...] = jnp.zeros_like(r.tok_d)
    r.cot_d[...] = jnp.zeros_like(r.cot_d)
    for p in range(r.tok_d.shape[0]):
        part = slice(p * size, (p + 1) * size)
        diagonal(r.tok_d.at[p], tok[:, part])
        diagonal(r.cot_d.at[p], cot[:, part])
    for p in range(r.tok_d.shape[0]):
        r.tok_t[p] = r.tok_d[p].T


def masked_sum(left, right, masks, dims=(1, 0)):
    value = dot(left, right, dims)
    rows = value.shape[0] // len(masks)
    return sum(value[b * rows : (b + 1) * rows, :] * m for b, m in enumerate(masks))


def partial_kernel(which, start, tile, loads, r):
    copies = fetch(r, loads, r.sems) if loads else []
    pairs, _, size = r.tok_d.shape
    for first in range(0, r.send.shape[2], tile):
        at = span(r.place[which] + start + first, tile)
        local = slice(first, first + tile)
        totals = [0.0, 0.0, 0.0]
        for p in range(pairs):
            part = slice(p * size, (p + 1) * size)
            bands = range(p * size // BLK, (p + 1) * size // BLK)
            for k, (left, right, mask, dims) in enumerate(
                (
                    (r.tok_d[p], r.kg[part, local], r.mg, (1, 0)),
                    (r.tok_d[p], r.ku[part, local], r.mu, (1, 0)),
                    (r.cot_d[p], r.kd[local, part], r.mdt, (1, 1)),
                )
            ):
                totals[k] += masked_sum(left, right, [mask[b, :, at] for b in bands], dims)
        for k, value in enumerate(totals):
            if hasattr(r, "received"):
                value = value + r.received[k, :, local]
                r.own[k, :, local] = value
            r.send[k, :, local] = value.astype(r.send.dtype)
    for copy in copies:
        copy.wait()


def act_kernel(r):
    others = [ref for name, ref in vars(r).items() if name.startswith("other")]
    gate, up, back = (
        sum((other[k].astype(F32) for other in others), r.own[k]) for k in range(3)
    )
    sigma = 1.0 / (1.0 + jnp.exp(-gate))
    silu = gate * sigma
    slope = sigma * (1.0 + gate * (1.0 - sigma))
    r.act[0] = (silu * up).astype(BF16)
    r.act[1] = (back * up * slope).astype(BF16)
    r.act[2] = (back * silu).astype(BF16)


def add_rows(r, i, block, local):
    width, tile = r.acc.shape[2], r.act_d.shape[3]
    size = min(DEPTH, width)
    for f in range(0, width, size):
        part = slice(f, f + size)

        def masks(mask):
            return [mask[block + b][:, part] for b in range(tile // BLK)]

        r.acc[0, :, part] += masked_sum(r.act_d[i, 0], r.kd[local, part], masks(r.md))
        r.acc[1, :, part] += masked_sum(
            r.act_d[i, 1], r.kg[part, local], masks(r.mgt), (1, 1)
        ) + masked_sum(r.act_d[i, 2], r.ku[part, local], masks(r.mut), (1, 1))


class Outbox:
    def __init__(self, slots, sems):
        self.slots, self.sems = slots, sems
        self.flying, self.count = [None] * slots.shape[0], 0

    def put(self, value, target):
        k = self.count % len(self.flying)
        self.count += 1
        if self.flying[k] is not None:
            self.flying[k].wait()
        self.slots[k] = value
        self.flying[k] = pltpu.make_async_copy(self.slots.at[k], target, self.sems.at[k])
        self.flying[k].start()

    def close(self):
        for copy in self.flying:
            if copy is not None:
                copy.wait()


def back_kernel(which, start, do_rows, do_grads, r):
    _, rows, size = r.act.shape
    tile = r.act_d.shape[3]
    base = r.place[which] + start
    at = span(base, size)
    r.act_d[...] = jnp.zeros_like(r.act_d)
    groups = 0
    if do_rows:
        r.acc[...] = r.sums[...] if hasattr(r, "sums") else jnp.zeros_like(r.acc)
    if do_grads:
        groups, height, _ = r.tok_t.shape
        by_cols, by_rows = Outbox(r.col_slots, r.col_sems), Outbox(r.row_slots, r.row_sems)
    tiles = [slice(i * tile, (i + 1) * tile) for i in range(size // tile)]
    block = lax.div(base, BLK)
    spots = tile // BLK
    for i, local in enumerate(tiles):
        for k in range(3 if do_rows else 1):
            diagonal(r.act_d.at[i, k], r.act[k, :, local])
    for i in range(max(groups, len(tiles)) if do_grads else 0):
        if i < groups:
            band = slice(i * height, (i + 1) * height)
            for out, k, mask in ((r.gg, 1, r.mg), (r.gu, 2, r.mu)):
                right = r.masked_act.at[k - 1]
                for j in range(height // BLK):
                    keep = mask[i * (height // BLK) + j, :, at].astype(BF16)
                    right[j * rows : (j + 1) * rows, :] = r.act[k] * keep
                by_cols.put(dot(r.tok_t[i], right[...]), out.at[band, at])
        if i < len(tiles):
            for b in range(spots):
                keep = r.md[block + i * spots + b].astype(BF16)
                r.masked_cot[b * rows : (b + 1) * rows, :] = r.cot[...] * keep
            value = dot(r.act_d[i, 0].T, r.masked_cot[...])
            by_rows.put(value, r.gd.at[span(base + i * tile, tile), :])
    for i, local in enumerate(tiles if do_rows else []):
        add_rows(r, i, block + i * spots, local)
    if do_rows:
        if hasattr(r, "new_sums"):
            r.new_sums[...] = r.acc[...]
        else:
            outs = [ref for name, ref in vars(r).items() if name.startswith("rows")]
            count = outs[0].shape[1]
            for k, out in enumerate(outs):
                out[...] = r.acc[:, k * count : (k + 1) * count, :].astype(out.dtype)
    if do_grads:
        by_cols.close()
        by_rows.close()


def shards(sizes, tokens, w_gate, w_up, w_down, mask_gate, mask_up, mask_down, grad_out):
    n_grid, n_dp = sizes
    width, units = w_gate.shape
    rows = n_grid * tokens.shape[0]
    pairs = n_dp // 2
    half = units // 2
    tile = min(DEPTH, half)
    split = PIECES if sum(PIECES) * tile == half else [half // tile]
    split = [tile * count for count in split]
    starts = [sum(split[:p]) for p in range(len(split))]
    n = len(split)
    direct = n_grid == 4
    grant = lambda mib: mib if rows <= 64 else 32

    core = lax.axis_index("dp") % 2
    place = jnp.stack([core * half, (1 - core) * half]).astype(jnp.int32)

    def trade(array, s):
        return lax.ppermute(array, "grid", [(i, i ^ s) for i in range(n_grid)])

    def swap(array):
        return lax.ppermute(array, "dp", [(i, i ^ 1) for i in range(n_dp)])

    def across(array):
        return [
            lax.ppermute(
                array,
                "dp",
                [(i, ((i // 2 + s) % pairs) * 2 + i % 2) for i in range(n_dp)],
            )
            for s in range(1, pairs)
        ]

    def shape(*dims, kind=BF16):
        return jax.ShapeDtypeStruct(dims, kind)

    weights = {"w_gate": (w_gate, ANY), "w_up": (w_up, ANY), "w_down": (w_down, ANY)}
    weights = {k: (hbm(w), spec) for k, (w, spec) in weights.items()}

    def kept_shapes(p):
        return [shape(width, split[p]), shape(width, split[p]), shape(split[p], width)]

    block = jnp.stack([tokens, grad_out])
    if direct:
        blocks = [block] + [trade(block, s) for s in range(1, n_grid)]
    else:
        blocks = [lax.all_gather(block, "grid", axis=1, tiled=True)]

    across_shape = shape(width // BLK, 1, units, kind=F32)
    along_shape = shape(units // BLK, 1, width, kind=F32)
    masks = {"mask_gate": mask_gate, "mask_up": mask_up, "mask_down_t": mask_down.T}
    kept = {}

    def loading(pieces):
        loads, outs = [], {}
        for which, p in pieces:
            names = [f"{k}_{which}_{p}" for k in KEPT]
            loads.append((which, starts[p], names))
            outs.update({k: pinned(s) for k, s in zip(names, kept_shapes(p))})
        count = count_copies([split[p] for _, p in pieces])
        return loads, outs, {"sems": pltpu.SemaphoreType.DMA((count,))} if pieces else {}

    def keep(got, pieces):
        for which, p in pieces:
            kept[which, p] = {k: got[f"{k}_{which}_{p}"] for k in KEPT}

    first = [(1, p) for p in range(min(n, 2))]
    loads, outs, scratch = loading(first)
    got = call(
        functools.partial(fetch_kernel, loads),
        "fetch",
        place,
        {**weights, **{k: (hbm(m), whole(m)) for k, m in masks.items()}},
        {
            **{k: pinned(across_shape) for k in ("mg", "mu", "mdt")},
            **{k: pinned(along_shape) for k in ("mgt", "mut", "md")},
            **outs,
        },
        scratch=scratch,
        vmem=grant(4),
    )
    values = {k: got[k] for k in ("mg", "mu", "mdt", "mgt", "mut", "md")}
    keep(got, first)

    pair = min(DEPTH, width) // BLK
    pair_shape = shape(width // (pair * BLK), pair * rows, pair * BLK)
    values |= call(
        assemble_kernel,
        "assemble",
        place,
        {
            "after": (values["mg"], ANY),
            **{f"block{k}": (b, whole(b)) for k, b in enumerate(blocks)},
        },
        {
            "cot": pinned(shape(rows, width)),
            "tok_d": pinned(pair_shape),
            "cot_d": pinned(pair_shape),
            "tok_t": pinned(shape(pair_shape.shape[0], pair * BLK, pair * rows)),
        },
        vmem=grant(4),
    )

    def held(*names):
        return {k: pinned(values[k]) for k in names}

    def partials(which, p, pieces, after=None, received=None):
        trio = (3, rows, split[p])
        ins = held("tok_d", "cot_d", "mg", "mu", "mdt")
        ins.update({k: pinned(v) for k, v in kept[which, p].items()})
        outs = {"send": pinned(shape(*trio, kind=F32))}
        if after is not None:
            ins["after"] = (after, ANY)
        if received is not None:
            ins["received"] = pinned(received)
            outs = {"own": pinned(shape(*trio, kind=F32)), "send": pinned(shape(*trio))}
        loads, fetched, scratch = loading(pieces)
        got = call(
            functools.partial(partial_kernel, which, starts[p], tile, loads),
            "partials",
            place,
            {**ins, **(weights if loads else {})},
            {**outs, **fetched},
            scratch=scratch,
            vmem=grant(2),
        )
        keep(got, pieces)
        return got

    def activate(own, others, after):
        ins = {"own": pinned(own), "after": (after, ANY)}
        ins.update({f"other{k}": pinned(a) for k, a in enumerate(others)})
        outs = {"act": pinned(shape(*own.shape))}
        return call(act_kernel, "activate", place, ins, outs, vmem=grant(2))["act"]

    def back(which, p, act, do_rows, do_grads, state, last=False):
        ins = {"act": pinned(act), **held("md")}
        outs, aliases = {}, {}
        spots, size = tile // BLK, split[p]
        scratch = {"act_d": pltpu.VMEM((size // tile, 3, spots * rows, tile), BF16)}
        if do_rows:
            ins.update({k: pinned(v) for k, v in kept[which, p].items()})
            ins.update(held("mgt", "mut"))
            scratch["acc"] = pltpu.VMEM((2, rows, width), F32)
            if "sums" in state:
                ins["sums"] = pinned(state["sums"])
            if last:
                n_out = n_grid if direct else 1
                out = shape(2, rows // n_out, width, kind=BF16 if direct else F32)
                outs.update({f"rows{k}": pinned(out) for k in range(n_out)})
            else:
                outs["new_sums"] = pinned(shape(2, rows, width, kind=F32))
        if do_grads:
            ins.update(held("tok_t", "cot", "mg", "mu"))
            outs["gg"] = (shape(width, units, kind=F32), ANY)
            outs["gu"] = (shape(width, units, kind=F32), ANY)
            outs["gd"] = (shape(units, width, kind=F32), ANY)
            scratch["masked_act"] = pltpu.VMEM((2, pair * rows, size), BF16)
            scratch["masked_cot"] = pltpu.VMEM((spots * rows, width), BF16)
            by_cols, by_rows = 2 * width // (pair * BLK), size // tile
            scratch["col_slots"] = pltpu.VMEM((by_cols, pair * BLK, size), F32)
            scratch["row_slots"] = pltpu.VMEM((by_rows, tile, width), F32)
            scratch["col_sems"] = pltpu.SemaphoreType.DMA((by_cols,))
            scratch["row_sems"] = pltpu.SemaphoreType.DMA((by_rows,))
            for k in ("gg", "gu", "gd"):
                if k in state:
                    ins["old_" + k] = (state[k], ANY)
                    aliases["old_" + k] = k
            if "rows0" in state:
                ins["after"] = (state["rows0"], ANY)
        got = call(
            functools.partial(back_kernel, which, starts[p], do_rows, do_grads),
            "_".join(["back"] + ["rows"] * do_rows + ["grads"] * do_grads),
            place,
            ins,
            outs,
            scratch=scratch,
            aliases=aliases,
            vmem=grant(12 if do_grads else 3),
        )
        return {**state, **{k.replace("new_", ""): v for k, v in got.items()}}

    sent, sums, theirs, after = [], [], [], None
    for p in range(n + 1):
        if p < n:
            after = partials(1, p, [(0, p)], after)["send"]
            sent.append(swap(after))
        if p > 0:
            ahead = [(1, p + 1)] if p + 1 < n else []
            got = partials(0, p - 1, ahead, after, sent[p - 1])
            after = got["own"]
            sums.append(after)
            theirs.append(across(got["send"]))

    state = {}
    for p in range(n):
        last = p == n - 1
        act = activate(sums[p], theirs[p], state.get("sums", after))
        act_other = swap(act)
        state = back(0, p, act, True, not last, state)
        state = back(1, p, act_other, True, not last, state, last)
        if last:
            state = back(0, p, act, False, True, state)
            state = back(1, p, act_other, False, True, state)

    if direct:
        both = state["rows0"].astype(F32)
        for s in range(1, n_grid):
            both += trade(state[f"rows{s}"], s).astype(F32)
    else:
        both = lax.psum_scatter(state["rows0"], "grid", scatter_dimension=1, tiled=True)
    both = both.astype(BF16)
    return (both[0], both[1], state["gg"], state["gu"], state["gd"])


def solution(mesh):
    in_specs = (
        P(("groups", "grid"), "dp"),
        P("dp", "grid"),
        P("dp", "grid"),
        P("grid", "dp"),
        P(("groups", "dp"), "grid"),
        P(("groups", "dp"), "grid"),
        P(("groups", "grid"), "dp"),
        P(("groups", "grid"), "dp"),
    )
    out_specs = (
        P(("groups", "grid"), "dp"),
        P(("groups", "grid"), "dp"),
        P(("groups", "dp"), "grid"),
        P(("groups", "dp"), "grid"),
        P(("groups", "grid"), "dp"),
    )
    sizes = (mesh.shape["grid"], mesh.shape["dp"])
    return jax.shard_map(
        functools.partial(shards, sizes),
        mesh=mesh,
        in_specs=in_specs,
        out_specs=out_specs,
        check_vma=False,
    )
```

```python
import functools
import types

import jax
import jax.numpy as jnp
from jax import lax
from jax.experimental import pallas as pl
from jax.experimental.pallas import tpu as pltpu
from jax.sharding import PartitionSpec as P

BLK = 128
MIB = 1024 * 1024
DEPTH = 256
ANY = pl.BlockSpec(memory_space=pl.ANY)
PIECES = [2, 3, 3]
SPLIT = 4
KEPT = ("kg", "ku", "kd")
MASKS = ("mask_gate", "mask_up", "mask_down_t")
F32 = jnp.float32
BF16 = jnp.bfloat16


def dot(left, right, dims=(1, 0)):
    return lax.dot_general(
        left, right, (((dims[0],), (dims[1],)), ((), ())), preferred_element_type=F32
    )


def pinned(array):
    spec = pl.BlockSpec(memory_space=pltpu.VMEM)
    if isinstance(array, jax.ShapeDtypeStruct):
        return (pltpu.VMEM(array.shape, array.dtype), spec)
    return (pltpu.with_memory_space_constraint(array, pltpu.VMEM), spec)


def call(kernel, name, scalars, ins, outs, scratch=None, aliases=None, vmem=2):
    scratch = scratch or {}
    names = ["place", *ins, *outs, *scratch]
    in_names, out_names = list(ins), list(outs)

    def body(*refs):
        kernel(types.SimpleNamespace(**dict(zip(names, refs))))

    results = pl.pallas_call(
        body,
        out_shape=[shape for shape, _ in outs.values()],
        grid_spec=pltpu.PrefetchScalarGridSpec(
            num_scalar_prefetch=1,
            grid=(1,),
            in_specs=[spec for _, spec in ins.values()],
            out_specs=[spec for _, spec in outs.values()],
            scratch_shapes=list(scratch.values()),
        ),
        input_output_aliases={
            1 + in_names.index(i): out_names.index(o) for i, o in (aliases or {}).items()
        },
        compiler_params=pltpu.CompilerParams(vmem_limit_bytes=vmem * MIB),
        cost_estimate=pl.CostEstimate(flops=1, bytes_accessed=1, transcendentals=0),
        name=name,
    )(scalars, *[array for array, _ in ins.values()])
    return dict(zip(out_names, results))


def hbm(array):
    return pltpu.with_memory_space_constraint(array, pltpu.HBM)


def whole(array):
    return pl.BlockSpec(array.shape, lambda *_: (0,) * len(array.shape))


def spread(r):
    def pattern(blocks):
        at = lax.broadcasted_iota(jnp.int32, (blocks, blocks * BLK), 0) * BLK
        column = lax.broadcasted_iota(jnp.int32, (blocks, blocks * BLK), 1)
        return ((column >= at) & (column < at + BLK)).astype(F32).astype(BF16)

    across, along = r.mask_gate.shape
    units, features = pattern(along), pattern(across)
    for mask, by_units, by_features in (
        (r.mask_gate, r.mg, r.mgt),
        (r.mask_up, r.mu, r.mut),
        (r.mask_down_t, r.mdt, r.md),
    ):
        entries = mask[...].astype(F32).astype(BF16)
        value = dot(entries, units)
        for b in range(across):
            by_units[b] = value[b : b + 1, :]
        value = dot(entries, features, (0, 0))
        for b in range(along):
            by_features[b] = value[b : b + 1, :]


def span(start, size):
    return pl.ds(pl.multiple_of(start, BLK), size)


def fetch_kernel(r):
    copies = []
    for source, target in ((r.w_gate, r.kg), (r.w_up, r.ku), (r.w_down, r.kd)):
        height = source.shape[0] // SPLIT
        for k in range(SPLIT):
            rows = slice(k * height, (k + 1) * height)
            copies.append((source.at[rows, :], target.at[rows, :]))
    for k in MASKS:
        copies.append((getattr(r, "hbm_" + k), getattr(r, k)))
    copies = [pltpu.make_async_copy(a, b, r.sems.at[k]) for k, (a, b) in enumerate(copies)]
    for copy in copies[-len(MASKS) :] + copies[: -len(MASKS)]:
        copy.start()
    for copy in copies[-len(MASKS) :]:
        copy.wait()
    spread(r)
    for copy in copies[: -len(MASKS)]:
        copy.wait()


def diagonal(out, value):
    rows, size = value.shape
    for b in range(size // BLK):
        band = slice(b * BLK, (b + 1) * BLK)
        out[b * rows : (b + 1) * rows, band] = value[:, band]


def assemble_kernel(r):
    blocks = [ref for name, ref in sorted(vars(r).items()) if name.startswith("block")]
    tok = jnp.concatenate([block[0] for block in blocks], axis=0)
    cot = jnp.concatenate([block[1] for block in blocks], axis=0)
    r.cot[...] = cot
    size = r.tok_d.shape[2]
    r.tok_d[...] = jnp.zeros_like(r.tok_d)
    r.cot_d[...] = jnp.zeros_like(r.cot_d)
    for p in range(r.tok_d.shape[0]):
        part = slice(p * size, (p + 1) * size)
        diagonal(r.tok_d.at[p], tok[:, part])
        diagonal(r.cot_d.at[p], cot[:, part])
    for p in range(r.tok_d.shape[0]):
        r.tok_t[p] = r.tok_d[p].T


def masked_sum(left, right, masks, dims=(1, 0)):
    value = dot(left, right, dims)
    rows = value.shape[0] // len(masks)
    return sum(value[b * rows : (b + 1) * rows, :] * m for b, m in enumerate(masks))


def partial_kernel(which, start, tile, r):
    pairs, _, size = r.tok_d.shape
    for first in range(0, r.send.shape[2], tile):
        at = span(r.place[which] + start + first, tile)
        local = slice(first, first + tile)
        totals = [0.0, 0.0, 0.0]
        for p in range(pairs):
            part = slice(p * size, (p + 1) * size)
            bands = range(p * size // BLK, (p + 1) * size // BLK)
            for k, (left, right, mask, dims) in enumerate(
                (
                    (r.tok_d[p], r.kg[part, at], r.mg, (1, 0)),
                    (r.tok_d[p], r.ku[part, at], r.mu, (1, 0)),
                    (r.cot_d[p], r.kd[at, part], r.mdt, (1, 1)),
                )
            ):
                totals[k] += masked_sum(left, right, [mask[b, :, at] for b in bands], dims)
        for k, value in enumerate(totals):
            if hasattr(r, "received"):
                value = value + r.received[k, :, local]
                r.own[k, :, local] = value
            r.send[k, :, local] = value.astype(r.send.dtype)


def act_kernel(r):
    others = [ref for name, ref in vars(r).items() if name.startswith("other")]
    gate, up, back = (
        sum((other[k].astype(F32) for other in others), r.own[k]) for k in range(3)
    )
    sigma = 1.0 / (1.0 + jnp.exp(-gate))
    silu = gate * sigma
    slope = sigma * (1.0 + gate * (1.0 - sigma))
    r.act[0] = (silu * up).astype(BF16)
    r.act[1] = (back * up * slope).astype(BF16)
    r.act[2] = (back * silu).astype(BF16)


def add_rows(r, i, block, at):
    width, tile = r.acc.shape[2], r.act_d.shape[3]
    size = min(DEPTH, width)
    for f in range(0, width, size):
        part = slice(f, f + size)

        def masks(mask):
            return [mask[block + b][:, part] for b in range(tile // BLK)]

        r.acc[0, :, part] += masked_sum(r.act_d[i, 0], r.kd[at, part], masks(r.md))
        r.acc[1, :, part] += masked_sum(
            r.act_d[i, 1], r.kg[part, at], masks(r.mgt), (1, 1)
        ) + masked_sum(r.act_d[i, 2], r.ku[part, at], masks(r.mut), (1, 1))


class Outbox:
    def __init__(self, slots, sems):
        self.slots, self.sems = slots, sems
        self.flying, self.count = [None] * slots.shape[0], 0

    def put(self, value, target):
        k = self.count % len(self.flying)
        self.count += 1
        if self.flying[k] is not None:
            self.flying[k].wait()
        self.slots[k] = value
        self.flying[k] = pltpu.make_async_copy(self.slots.at[k], target, self.sems.at[k])
        self.flying[k].start()

    def close(self):
        for copy in self.flying:
            if copy is not None:
                copy.wait()


def back_kernel(items, do_rows, do_grads, r):
    tile = r.act_d.shape[3]
    spots = tile // BLK
    r.act_d[...] = jnp.zeros_like(r.act_d)
    if do_rows:
        r.acc[...] = r.sums[...] if hasattr(r, "sums") else jnp.zeros_like(r.acc)
    if do_grads:
        groups, height, _ = r.tok_t.shape
        by_cols, by_rows = Outbox(r.col_slots, r.col_sems), Outbox(r.row_slots, r.row_sems)
    for act, which, start in items:
        act = getattr(r, act)
        _, rows, size = act.shape
        base = r.place[which] + start
        at, block = span(base, size), lax.div(base, BLK)
        tiles = [slice(i * tile, (i + 1) * tile) for i in range(size // tile)]
        for i, local in enumerate(tiles):
            for k in range(3 if do_rows else 1):
                diagonal(r.act_d.at[i, k], act[k, :, local])
        for i in range(max(groups, len(tiles)) if do_grads else 0):
            if i < groups:
                band = slice(i * height, (i + 1) * height)
                for out, k, mask in ((r.gg, 1, r.mg), (r.gu, 2, r.mu)):
                    right = r.masked_act.at[k - 1]
                    for j in range(height // BLK):
                        keep = mask[i * (height // BLK) + j, :, at].astype(BF16)
                        right[j * rows : (j + 1) * rows, :] = act[k] * keep
                    by_cols.put(dot(r.tok_t[i], right[...]), out.at[band, at])
            if i < len(tiles):
                for b in range(spots):
                    keep = r.md[block + i * spots + b].astype(BF16)
                    r.masked_cot[b * rows : (b + 1) * rows, :] = r.cot[...] * keep
                value = dot(r.act_d[i, 0].T, r.masked_cot[...])
                by_rows.put(value, r.gd.at[span(base + i * tile, tile), :])
        for i in range(len(tiles) if do_rows else 0):
            add_rows(r, i, block + i * spots, span(base + i * tile, tile))
    if do_rows:
        if hasattr(r, "new_sums"):
            r.new_sums[...] = r.acc[...]
        else:
            outs = [ref for name, ref in vars(r).items() if name.startswith("rows")]
            count = outs[0].shape[1]
            for k, out in enumerate(outs):
                out[...] = r.acc[:, k * count : (k + 1) * count, :].astype(out.dtype)
    if do_grads:
        by_cols.close()
        by_rows.close()


def shards(sizes, tokens, w_gate, w_up, w_down, mask_gate, mask_up, mask_down, grad_out):
    n_grid, n_dp = sizes
    width, units = w_gate.shape
    rows = n_grid * tokens.shape[0]
    pairs = n_dp // 2
    half = units // 2
    tile = min(DEPTH, half)
    split = PIECES if sum(PIECES) * tile == half else [half // tile]
    split = [tile * count for count in split]
    starts = [sum(split[:p]) for p in range(len(split))]
    n = len(split)
    direct = n_grid == 4
    grant = lambda mib: mib if rows <= 64 else 32

    core = lax.axis_index("dp") % 2
    place = jnp.stack([core * half, (1 - core) * half]).astype(jnp.int32)

    def trade(array, s):
        return lax.ppermute(array, "grid", [(i, i ^ s) for i in range(n_grid)])

    def swap(array):
        return lax.ppermute(array, "dp", [(i, i ^ 1) for i in range(n_dp)])

    def across(array):
        return [
            lax.ppermute(
                array,
                "dp",
                [(i, ((i // 2 + s) % pairs) * 2 + i % 2) for i in range(n_dp)],
            )
            for s in range(1, pairs)
        ]

    def shape(*dims, kind=BF16):
        return jax.ShapeDtypeStruct(dims, kind)

    weights = {"w_gate": (w_gate, ANY), "w_up": (w_up, ANY), "w_down": (w_down, ANY)}
    weights = {k: (hbm(w), spec) for k, (w, spec) in weights.items()}

    block = jnp.stack([tokens, grad_out])
    if direct:
        blocks = [block] + [trade(block, s) for s in range(1, n_grid)]
    else:
        blocks = [lax.all_gather(block, "grid", axis=1, tiled=True)]

    across_shape = shape(width // BLK, 1, units, kind=F32)
    along_shape = shape(units // BLK, 1, width, kind=F32)
    masks = dict(zip(MASKS, (mask_gate, mask_up, mask_down.T)))
    values = call(
        fetch_kernel,
        "fetch",
        place,
        {**weights, **{"hbm_" + k: (hbm(m), ANY) for k, m in masks.items()}},
        {
            **{k: pinned(across_shape) for k in ("mg", "mu", "mdt")},
            **{k: pinned(along_shape) for k in ("mgt", "mut", "md")},
            **{k: pinned(shape(*w.shape)) for k, w in zip(KEPT, (w_gate, w_up, w_down))},
        },
        scratch={
            **{k: pltpu.VMEM(m.shape, m.dtype) for k, m in masks.items()},
            "sems": pltpu.SemaphoreType.DMA((3 * SPLIT + len(masks),)),
        },
        vmem=grant(4),
    )

    pair = min(DEPTH, width) // BLK
    pair_shape = shape(width // (pair * BLK), pair * rows, pair * BLK)
    values |= call(
        assemble_kernel,
        "assemble",
        place,
        {
            "after": (values["mg"], ANY),
            **{f"block{k}": (b, whole(b)) for k, b in reversed(list(enumerate(blocks)))},
        },
        {
            "cot": pinned(shape(rows, width)),
            "tok_d": pinned(pair_shape),
            "cot_d": pinned(pair_shape),
            "tok_t": pinned(shape(pair_shape.shape[0], pair * BLK, pair * rows)),
        },
        vmem=grant(4),
    )

    def held(*names):
        return {k: pinned(values[k]) for k in names}

    def partials(which, p, after=None, received=None):
        trio = (3, rows, split[p])
        ins = held("tok_d", "cot_d", "mg", "mu", "mdt", *KEPT)
        outs = {"send": pinned(shape(*trio, kind=F32))}
        if after is not None:
            ins["after"] = (after, ANY)
        if received is not None:
            ins["received"] = pinned(received)
            outs = {"own": pinned(shape(*trio, kind=F32)), "send": pinned(shape(*trio))}
        kernel = functools.partial(partial_kernel, which, starts[p], tile)
        return call(kernel, "partials", place, ins, outs, vmem=grant(2))

    def activate(own, others, after):
        ins = {"own": pinned(own), "after": (after, ANY)}
        ins.update({f"other{k}": pinned(a) for k, a in enumerate(others)})
        outs = {"act": pinned(shape(*own.shape))}
        return call(act_kernel, "activate", place, ins, outs, vmem=grant(2))["act"]

    def back(pieces, do_rows, do_grads, state, last=False):
        items = [(f"act{k}", which, starts[p]) for k, (which, p, _) in enumerate(pieces)]
        ins = {f"act{k}": pinned(act) for k, (_, _, act) in enumerate(pieces)}
        ins.update(held("md"))
        outs, aliases = {}, {}
        spots, size = tile // BLK, split[pieces[0][1]]
        scratch = {"act_d": pltpu.VMEM((size // tile, 3, spots * rows, tile), BF16)}
        if do_rows:
            ins.update(held("mgt", "mut", *KEPT))
            scratch["acc"] = pltpu.VMEM((2, rows, width), F32)
            if "sums" in state:
                ins["sums"] = pinned(state["sums"])
            if last:
                n_out = n_grid if direct else 1
                out = shape(2, rows // n_out, width, kind=BF16 if direct else F32)
                outs.update({f"rows{k}": pinned(out) for k in range(n_out)})
            else:
                outs["new_sums"] = pinned(shape(2, rows, width, kind=F32))
        if do_grads:
            ins.update(held("tok_t", "cot", "mg", "mu"))
            outs["gg"] = (shape(width, units, kind=F32), ANY)
            outs["gu"] = (shape(width, units, kind=F32), ANY)
            outs["gd"] = (shape(units, width, kind=F32), ANY)
            scratch["masked_act"] = pltpu.VMEM((2, pair * rows, size), BF16)
            scratch["masked_cot"] = pltpu.VMEM((spots * rows, width), BF16)
            by_cols, by_rows = 2 * width // (pair * BLK), size // tile
            scratch["col_slots"] = pltpu.VMEM((by_cols, pair * BLK, size), F32)
            scratch["row_slots"] = pltpu.VMEM((by_rows, tile, width), F32)
            scratch["col_sems"] = pltpu.SemaphoreType.DMA((by_cols,))
            scratch["row_sems"] = pltpu.SemaphoreType.DMA((by_rows,))
            for k in ("gg", "gu", "gd"):
                if k in state:
                    ins["old_" + k] = (state[k], ANY)
                    aliases["old_" + k] = k
            if "rows0" in state:
                ins["after"] = (state["rows0"], ANY)
        got = call(
            functools.partial(back_kernel, items, do_rows, do_grads),
            "_".join(["back"] + ["rows"] * do_rows + ["grads"] * do_grads),
            place,
            ins,
            outs,
            scratch=scratch,
            aliases=aliases,
            vmem=grant(12 if do_grads else 3),
        )
        return {**state, **{k.replace("new_", ""): v for k, v in got.items()}}

    sent, sums, theirs, after = [], [], [], None
    for p in range(n + 1):
        if p < n:
            after = partials(1, p, after)["send"]
            sent.append(swap(after))
        if p > 0:
            got = partials(0, p - 1, after, sent[p - 1])
            after = got["own"]
            sums.append(after)
            theirs.append(across(got["send"]))

    state = {}
    for p in range(n):
        last = p == n - 1
        act = activate(sums[p], theirs[p], state.get("sums", after))
        act_other = swap(act)
        state = back([(0, p, act)], True, not last, state)
        state = back([(1, p, act_other)], True, not last, state, last)
        if last:
            state = back([(0, p, act), (1, p, act_other)], False, True, state)

    if direct:
        both = state["rows0"].astype(F32)
        for s in range(1, n_grid):
            both += trade(state[f"rows{s}"], s).astype(F32)
    else:
        both = lax.psum_scatter(state["rows0"], "grid", scatter_dimension=1, tiled=True)
    both = both.astype(BF16)
    return (both[0], both[1], state["gg"], state["gu"], state["gd"])


def solution(mesh):
    in_specs = (
        P(("groups", "grid"), "dp"),
        P("dp", "grid"),
        P("dp", "grid"),
        P("grid", "dp"),
        P(("groups", "dp"), "grid"),
        P(("groups", "dp"), "grid"),
        P(("groups", "grid"), "dp"),
        P(("groups", "grid"), "dp"),
    )
    out_specs = (
        P(("groups", "grid"), "dp"),
        P(("groups", "grid"), "dp"),
        P(("groups", "dp"), "grid"),
        P(("groups", "dp"), "grid"),
        P(("groups", "grid"), "dp"),
    )
    sizes = (mesh.shape["grid"], mesh.shape["dp"])
    return jax.shard_map(
        functools.partial(shards, sizes),
        mesh=mesh,
        in_specs=in_specs,
        out_specs=out_specs,
        check_vma=False,
    )
```

```python
import functools
import types

import jax
import jax.numpy as jnp
from jax import lax
from jax.experimental import pallas as pl
from jax.experimental.pallas import tpu as pltpu
from jax.sharding import PartitionSpec as P

BLK = 128
MIB = 1024 * 1024
DEPTH = 256
ANY = pl.BlockSpec(memory_space=pl.ANY)
PIECES = [2, 3, 3]
SPLIT = 4
KEPT = ("kg", "ku", "kd")
MASKS = ("mask_gate", "mask_up", "mask_down_t")
F32 = jnp.float32
BF16 = jnp.bfloat16


def dot(left, right, dims=(1, 0)):
    return lax.dot_general(
        left, right, (((dims[0],), (dims[1],)), ((), ())), preferred_element_type=F32
    )


def pinned(array):
    spec = pl.BlockSpec(memory_space=pltpu.VMEM)
    if isinstance(array, jax.ShapeDtypeStruct):
        return (pltpu.VMEM(array.shape, array.dtype), spec)
    return (pltpu.with_memory_space_constraint(array, pltpu.VMEM), spec)


def call(kernel, name, ins, outs, scratch=None, aliases=None, vmem=2):
    scratch = scratch or {}
    names = [*ins, *outs, *scratch]
    in_names, out_names = list(ins), list(outs)

    def body(*refs):
        kernel(types.SimpleNamespace(**dict(zip(names, refs))))

    results = pl.pallas_call(
        body,
        out_shape=[shape for shape, _ in outs.values()],
        in_specs=[spec for _, spec in ins.values()],
        out_specs=[spec for _, spec in outs.values()],
        scratch_shapes=list(scratch.values()),
        input_output_aliases={
            in_names.index(i): out_names.index(o) for i, o in (aliases or {}).items()
        },
        compiler_params=pltpu.CompilerParams(vmem_limit_bytes=vmem * MIB),
        cost_estimate=pl.CostEstimate(flops=1, bytes_accessed=1, transcendentals=0),
        name=name,
    )(*[array for array, _ in ins.values()])
    return dict(zip(out_names, results))


def hbm(array):
    return pltpu.with_memory_space_constraint(array, pltpu.HBM)


def whole(array):
    return pl.BlockSpec(array.shape, lambda *_: (0,) * len(array.shape))


def spread(r):
    def pattern(blocks):
        at = lax.broadcasted_iota(jnp.int32, (blocks, blocks * BLK), 0) * BLK
        column = lax.broadcasted_iota(jnp.int32, (blocks, blocks * BLK), 1)
        return ((column >= at) & (column < at + BLK)).astype(F32).astype(BF16)

    across, along = r.mask_gate.shape
    units, features = pattern(along), pattern(across)
    for mask, by_units, by_features in (
        (r.mask_gate, r.mg, r.mgt),
        (r.mask_up, r.mu, r.mut),
        (r.mask_down_t, r.mdt, r.md),
    ):
        entries = mask[...].astype(F32).astype(BF16)
        value = dot(entries, units)
        for b in range(across):
            by_units[b] = value[b : b + 1, :]
        value = dot(entries, features, (0, 0))
        for b in range(along):
            by_features[b] = value[b : b + 1, :]


def first_unit(which, half):
    core = lax.rem(lax.axis_index("dp"), 2)
    return (core if which == 0 else 1 - core) * half


def span(start, size):
    return pl.ds(pl.multiple_of(start, BLK), size)


def fetch_kernel(r):
    copies = []
    for source, target in ((r.w_gate, r.kg), (r.w_up, r.ku), (r.w_down, r.kd)):
        height = source.shape[0] // SPLIT
        for k in range(SPLIT):
            rows = slice(k * height, (k + 1) * height)
            copies.append((source.at[rows, :], target.at[rows, :]))
    for k in MASKS:
        copies.append((getattr(r, "hbm_" + k), getattr(r, k)))
    copies = [pltpu.make_async_copy(a, b, r.sems.at[k]) for k, (a, b) in enumerate(copies)]
    for copy in copies[-len(MASKS) :] + copies[: -len(MASKS)]:
        copy.start()
    for copy in copies[-len(MASKS) :]:
        copy.wait()
    spread(r)
    for copy in copies[: -len(MASKS)]:
        copy.wait()


def diagonal(out, value):
    rows, size = value.shape
    for b in range(size // BLK):
        band = slice(b * BLK, (b + 1) * BLK)
        out[b * rows : (b + 1) * rows, band] = value[:, band]


def assemble_kernel(r):
    blocks = [ref for name, ref in sorted(vars(r).items()) if name.startswith("block")]
    tok = jnp.concatenate([block[0] for block in blocks], axis=0)
    cot = jnp.concatenate([block[1] for block in blocks], axis=0)
    r.cot[...] = cot
    size = r.tok_d.shape[2]
    r.tok_d[...] = jnp.zeros_like(r.tok_d)
    r.cot_d[...] = jnp.zeros_like(r.cot_d)
    for p in range(r.tok_d.shape[0]):
        part = slice(p * size, (p + 1) * size)
        diagonal(r.tok_d.at[p], tok[:, part])
        diagonal(r.cot_d.at[p], cot[:, part])
    for p in range(r.tok_d.shape[0]):
        r.tok_t[p] = r.tok_d[p].T


def masked_sum(left, right, masks, dims=(1, 0)):
    value = dot(left, right, dims)
    rows = value.shape[0] // len(masks)
    return sum(value[b * rows : (b + 1) * rows, :] * m for b, m in enumerate(masks))


def partial_kernel(which, start, half, tile, r):
    pairs, _, size = r.tok_d.shape
    base = first_unit(which, half) + start
    for first in range(0, r.send.shape[2], tile):
        at = span(base + first, tile)
        local = slice(first, first + tile)
        totals = [0.0, 0.0, 0.0]
        for p in range(pairs):
            part = slice(p * size, (p + 1) * size)
            bands = range(p * size // BLK, (p + 1) * size // BLK)
            for k, (left, right, mask, dims) in enumerate(
                (
                    (r.tok_d[p], r.kg[part, at], r.mg, (1, 0)),
                    (r.tok_d[p], r.ku[part, at], r.mu, (1, 0)),
                    (r.cot_d[p], r.kd[at, part], r.mdt, (1, 1)),
                )
            ):
                totals[k] += masked_sum(left, right, [mask[b, :, at] for b in bands], dims)
        for k, value in enumerate(totals):
            if hasattr(r, "received"):
                value = value + r.received[k, :, local]
                r.own[k, :, local] = value
            r.send[k, :, local] = value.astype(r.send.dtype)


def act_kernel(r):
    others = [ref for name, ref in vars(r).items() if name.startswith("other")]
    gate, up, back = (
        sum((other[k].astype(F32) for other in others), r.own[k]) for k in range(3)
    )
    sigma = 1.0 / (1.0 + jnp.exp(-gate))
    silu = gate * sigma
    slope = sigma * (1.0 + gate * (1.0 - sigma))
    r.act[0] = (silu * up).astype(BF16)
    r.act[1] = (back * up * slope).astype(BF16)
    r.act[2] = (back * silu).astype(BF16)


def add_rows(r, i, block, at):
    width, tile = r.acc.shape[2], r.act_d.shape[3]
    size = min(DEPTH, width)
    for f in range(0, width, size):
        part = slice(f, f + size)

        def masks(mask):
            return [mask[block + b][:, part] for b in range(tile // BLK)]

        r.acc[0, :, part] += masked_sum(r.act_d[i, 0], r.kd[at, part], masks(r.md))
        r.acc[1, :, part] += masked_sum(
            r.act_d[i, 1], r.kg[part, at], masks(r.mgt), (1, 1)
        ) + masked_sum(r.act_d[i, 2], r.ku[part, at], masks(r.mut), (1, 1))


class Outbox:
    def __init__(self, slots, sems):
        self.slots, self.sems = slots, sems
        self.flying, self.count = [None] * slots.shape[0], 0

    def put(self, value, target):
        k = self.count % len(self.flying)
        self.count += 1
        if self.flying[k] is not None:
            self.flying[k].wait()
        self.slots[k] = value
        self.flying[k] = pltpu.make_async_copy(self.slots.at[k], target, self.sems.at[k])
        self.flying[k].start()

    def close(self):
        for copy in self.flying:
            if copy is not None:
                copy.wait()


def back_kernel(items, half, do_rows, do_grads, r):
    tile = r.act_d.shape[3]
    spots = tile // BLK
    r.act_d[...] = jnp.zeros_like(r.act_d)
    if do_rows:
        r.acc[...] = r.sums[...] if hasattr(r, "sums") else jnp.zeros_like(r.acc)
    if do_grads:
        groups, height, _ = r.tok_t.shape
        by_cols, by_rows = Outbox(r.col_slots, r.col_sems), Outbox(r.row_slots, r.row_sems)
    for act, which, start in items:
        act = getattr(r, act)
        _, rows, size = act.shape
        base = first_unit(which, half) + start
        at, block = span(base, size), lax.div(base, BLK)
        tiles = [slice(i * tile, (i + 1) * tile) for i in range(size // tile)]
        for i, local in enumerate(tiles):
            for k in range(3 if do_rows else 1):
                diagonal(r.act_d.at[i, k], act[k, :, local])
        for i in range(max(groups, len(tiles)) if do_grads else 0):
            if i < groups:
                band = slice(i * height, (i + 1) * height)
                for out, k, mask in ((r.gg, 1, r.mg), (r.gu, 2, r.mu)):
                    right = r.masked_act.at[k - 1]
                    for j in range(height // BLK):
                        keep = mask[i * (height // BLK) + j, :, at].astype(BF16)
                        right[j * rows : (j + 1) * rows, :] = act[k] * keep
                    by_cols.put(dot(r.tok_t[i], right[...]), out.at[band, at])
            if i < len(tiles):
                for b in range(spots):
                    keep = r.md[block + i * spots + b].astype(BF16)
                    r.masked_cot[b * rows : (b + 1) * rows, :] = r.cot[...] * keep
                value = dot(r.act_d[i, 0].T, r.masked_cot[...])
                by_rows.put(value, r.gd.at[span(base + i * tile, tile), :])
        for i in range(len(tiles) if do_rows else 0):
            add_rows(r, i, block + i * spots, span(base + i * tile, tile))
    if do_rows:
        if hasattr(r, "new_sums"):
            r.new_sums[...] = r.acc[...]
        else:
            outs = [ref for name, ref in vars(r).items() if name.startswith("rows")]
            count = outs[0].shape[1]
            for k, out in enumerate(outs):
                out[...] = r.acc[:, k * count : (k + 1) * count, :].astype(out.dtype)
    if do_grads:
        by_cols.close()
        by_rows.close()


def shards(sizes, tokens, w_gate, w_up, w_down, mask_gate, mask_up, mask_down, grad_out):
    n_grid, n_dp = sizes
    width, units = w_gate.shape
    rows = n_grid * tokens.shape[0]
    pairs = n_dp // 2
    half = units // 2
    tile = min(DEPTH, half)
    split = PIECES if sum(PIECES) * tile == half else [half // tile]
    split = [tile * count for count in split]
    starts = [sum(split[:p]) for p in range(len(split))]
    n = len(split)
    direct = n_grid == 4
    grant = lambda mib: mib if rows <= 64 else 32

    def trade(array, s):
        return lax.ppermute(array, "grid", [(i, i ^ s) for i in range(n_grid)])

    def swap(array):
        return lax.ppermute(array, "dp", [(i, i ^ 1) for i in range(n_dp)])

    def across(array):
        return [
            lax.ppermute(
                array,
                "dp",
                [(i, ((i // 2 + s) % pairs) * 2 + i % 2) for i in range(n_dp)],
            )
            for s in range(1, pairs)
        ]

    def shape(*dims, kind=BF16):
        return jax.ShapeDtypeStruct(dims, kind)

    weights = {"w_gate": (w_gate, ANY), "w_up": (w_up, ANY), "w_down": (w_down, ANY)}
    weights = {k: (hbm(w), spec) for k, (w, spec) in weights.items()}

    block = jnp.stack([tokens, grad_out])
    if direct:
        blocks = [block] + [trade(block, s) for s in range(1, n_grid)]
    else:
        blocks = [lax.all_gather(block, "grid", axis=1, tiled=True)]

    across_shape = shape(width // BLK, 1, units, kind=F32)
    along_shape = shape(units // BLK, 1, width, kind=F32)
    masks = dict(zip(MASKS, (mask_gate, mask_up, mask_down.T)))
    values = call(
        fetch_kernel,
        "fetch",
        {**weights, **{"hbm_" + k: (hbm(m), ANY) for k, m in masks.items()}},
        {
            **{k: pinned(across_shape) for k in ("mg", "mu", "mdt")},
            **{k: pinned(along_shape) for k in ("mgt", "mut", "md")},
            **{k: pinned(shape(*w.shape)) for k, w in zip(KEPT, (w_gate, w_up, w_down))},
        },
        scratch={
            **{k: pltpu.VMEM(m.shape, m.dtype) for k, m in masks.items()},
            "sems": pltpu.SemaphoreType.DMA((3 * SPLIT + len(masks),)),
        },
        vmem=grant(4),
    )

    pair = min(DEPTH, width) // BLK
    pair_shape = shape(width // (pair * BLK), pair * rows, pair * BLK)
    values |= call(
        assemble_kernel,
        "assemble",
        {
            "after": (values["mg"], ANY),
            **{f"block{k}": (b, whole(b)) for k, b in reversed(list(enumerate(blocks)))},
        },
        {
            "cot": pinned(shape(rows, width)),
            "tok_d": pinned(pair_shape),
            "cot_d": pinned(pair_shape),
            "tok_t": pinned(shape(pair_shape.shape[0], pair * BLK, pair * rows)),
        },
        vmem=grant(4),
    )

    def held(*names):
        return {k: pinned(values[k]) for k in names}

    def partials(which, p, after=None, received=None):
        trio = (3, rows, split[p])
        ins = held("tok_d", "cot_d", "mg", "mu", "mdt", *KEPT)
        outs = {"send": pinned(shape(*trio, kind=F32))}
        if after is not None:
            ins["after"] = (after, ANY)
        if received is not None:
            ins["received"] = pinned(received)
            outs = {"own": pinned(shape(*trio, kind=F32)), "send": pinned(shape(*trio))}
        kernel = functools.partial(partial_kernel, which, starts[p], half, tile)
        return call(kernel, "partials", ins, outs, vmem=grant(2))

    def activate(own, others, after):
        ins = {"own": pinned(own), "after": (after, ANY)}
        ins.update({f"other{k}": pinned(a) for k, a in enumerate(others)})
        outs = {"act": pinned(shape(*own.shape))}
        return call(act_kernel, "activate", ins, outs, vmem=grant(2))["act"]

    def back(pieces, do_rows, do_grads, state, last=False):
        items = [(f"act{k}", which, starts[p]) for k, (which, p, _) in enumerate(pieces)]
        ins = {f"act{k}": pinned(act) for k, (_, _, act) in enumerate(pieces)}
        ins.update(held("md"))
        outs, aliases = {}, {}
        spots, size = tile // BLK, split[pieces[0][1]]
        scratch = {"act_d": pltpu.VMEM((size // tile, 3, spots * rows, tile), BF16)}
        if do_rows:
            ins.update(held("mgt", "mut", *KEPT))
            scratch["acc"] = pltpu.VMEM((2, rows, width), F32)
            if "sums" in state:
                ins["sums"] = pinned(state["sums"])
            if last:
                n_out = n_grid if direct else 1
                out = shape(2, rows // n_out, width, kind=BF16 if direct else F32)
                outs.update({f"rows{k}": pinned(out) for k in range(n_out)})
            else:
                outs["new_sums"] = pinned(shape(2, rows, width, kind=F32))
        if do_grads:
            ins.update(held("tok_t", "cot", "mg", "mu"))
            outs["gg"] = (shape(width, units, kind=F32), ANY)
            outs["gu"] = (shape(width, units, kind=F32), ANY)
            outs["gd"] = (shape(units, width, kind=F32), ANY)
            scratch["masked_act"] = pltpu.VMEM((2, pair * rows, size), BF16)
            scratch["masked_cot"] = pltpu.VMEM((spots * rows, width), BF16)
            by_cols, by_rows = 2 * width // (pair * BLK), size // tile
            scratch["col_slots"] = pltpu.VMEM((by_cols, pair * BLK, size), F32)
            scratch["row_slots"] = pltpu.VMEM((by_rows, tile, width), F32)
            scratch["col_sems"] = pltpu.SemaphoreType.DMA((by_cols,))
            scratch["row_sems"] = pltpu.SemaphoreType.DMA((by_rows,))
            for k in ("gg", "gu", "gd"):
                if k in state:
                    ins["old_" + k] = (state[k], ANY)
                    aliases["old_" + k] = k
            if "rows0" in state:
                ins["after"] = (state["rows0"], ANY)
        got = call(
            functools.partial(back_kernel, items, half, do_rows, do_grads),
            "_".join(["back"] + ["rows"] * do_rows + ["grads"] * do_grads),
            ins,
            outs,
            scratch=scratch,
            aliases=aliases,
            vmem=grant(12 if do_grads else 3),
        )
        return {**state, **{k.replace("new_", ""): v for k, v in got.items()}}

    sent, sums, theirs, after = [], [], [], None
    for p in range(n + 1):
        if p < n:
            after = partials(1, p, after)["send"]
            sent.append(swap(after))
        if p > 0:
            got = partials(0, p - 1, after, sent[p - 1])
            after = got["own"]
            sums.append(after)
            theirs.append(across(got["send"]))

    state = {}
    for p in range(n):
        last = p == n - 1
        act = activate(sums[p], theirs[p], state.get("sums", after))
        act_other = swap(act)
        state = back([(0, p, act)], True, not last, state)
        state = back([(1, p, act_other)], True, not last, state, last)
        if last:
            state = back([(0, p, act), (1, p, act_other)], False, True, state)

    if direct:
        both = state["rows0"].astype(F32)
        for s in range(1, n_grid):
            both += trade(state[f"rows{s}"], s).astype(F32)
    else:
        both = lax.psum_scatter(state["rows0"], "grid", scatter_dimension=1, tiled=True)
    both = both.astype(BF16)
    return (both[0], both[1], state["gg"], state["gu"], state["gd"])


def solution(mesh):
    in_specs = (
        P(("groups", "grid"), "dp"),
        P("dp", "grid"),
        P("dp", "grid"),
        P("grid", "dp"),
        P(("groups", "dp"), "grid"),
        P(("groups", "dp"), "grid"),
        P(("groups", "grid"), "dp"),
        P(("groups", "grid"), "dp"),
    )
    out_specs = (
        P(("groups", "grid"), "dp"),
        P(("groups", "grid"), "dp"),
        P(("groups", "dp"), "grid"),
        P(("groups", "dp"), "grid"),
        P(("groups", "grid"), "dp"),
    )
    sizes = (mesh.shape["grid"], mesh.shape["dp"])
    return jax.shard_map(
        functools.partial(shards, sizes),
        mesh=mesh,
        in_specs=in_specs,
        out_specs=out_specs,
        check_vma=False,
    )
```

```python
import functools
import types

import jax
import jax.numpy as jnp
from jax import lax
from jax.experimental import pallas as pl
from jax.experimental.pallas import tpu as pltpu
from jax.sharding import PartitionSpec as P

BLK = 128
MIB = 1024 * 1024
DEPTH = 256
ANY = pl.BlockSpec(memory_space=pl.ANY)
PIECES = [2, 3, 3]
SPLIT = 4
KEPT = ("kg", "ku", "kd")
MASKS = ("mask_gate", "mask_up", "mask_down_t")
F32 = jnp.float32
BF16 = jnp.bfloat16


def dot(left, right, dims=(1, 0)):
    return lax.dot_general(
        left, right, (((dims[0],), (dims[1],)), ((), ())), preferred_element_type=F32
    )


def pinned(array):
    spec = pl.BlockSpec(memory_space=pltpu.VMEM)
    if isinstance(array, jax.ShapeDtypeStruct):
        return (pltpu.VMEM(array.shape, array.dtype), spec)
    return (pltpu.with_memory_space_constraint(array, pltpu.VMEM), spec)


def call(kernel, name, ins, outs, scratch=None, aliases=None, vmem=2):
    scratch = scratch or {}
    names = [*ins, *outs, *scratch]
    in_names, out_names = list(ins), list(outs)

    def body(*refs):
        kernel(types.SimpleNamespace(**dict(zip(names, refs))))

    results = pl.pallas_call(
        body,
        out_shape=[shape for shape, _ in outs.values()],
        in_specs=[spec for _, spec in ins.values()],
        out_specs=[spec for _, spec in outs.values()],
        scratch_shapes=list(scratch.values()),
        input_output_aliases={
            in_names.index(i): out_names.index(o) for i, o in (aliases or {}).items()
        },
        compiler_params=pltpu.CompilerParams(vmem_limit_bytes=vmem * MIB),
        cost_estimate=pl.CostEstimate(flops=1, bytes_accessed=1, transcendentals=0),
        name=name,
    )(*[array for array, _ in ins.values()])
    return dict(zip(out_names, results))


def hbm(array):
    return pltpu.with_memory_space_constraint(array, pltpu.HBM)


def whole(array):
    return pl.BlockSpec(array.shape, lambda *_: (0,) * len(array.shape))


def spread(r):
    def pattern(blocks):
        at = lax.broadcasted_iota(jnp.int32, (blocks, blocks * BLK), 0) * BLK
        column = lax.broadcasted_iota(jnp.int32, (blocks, blocks * BLK), 1)
        return ((column >= at) & (column < at + BLK)).astype(F32).astype(BF16)

    across, along = r.mask_gate.shape
    units, features = pattern(along), pattern(across)
    for mask, by_units, by_features in (
        (r.mask_gate, r.mg, r.mgt),
        (r.mask_up, r.mu, r.mut),
        (r.mask_down_t, r.mdt, r.md),
    ):
        entries = mask[...].astype(F32).astype(BF16)
        value = dot(entries, units)
        for b in range(across):
            by_units[b] = value[b : b + 1, :]
        value = dot(entries, features, (0, 0))
        for b in range(along):
            by_features[b] = value[b : b + 1, :]


def first_unit(which, half):
    core = lax.rem(lax.axis_index("dp"), 2)
    return (core if which == 0 else 1 - core) * half


def span(start, size):
    return pl.ds(pl.multiple_of(start, BLK), size)


def copy_all(pairs, sems, first=0):
    copies = [pltpu.make_async_copy(a, b, sems.at[first + k]) for k, (a, b) in enumerate(pairs)]
    for copy in copies:
        copy.start()
    return copies


def in_bands(source, target):
    height = source.shape[0] // SPLIT
    bands = [slice(k * height, (k + 1) * height) for k in range(SPLIT)]
    return [(source.at[band, :], target.at[band, :]) for band in bands]


def first_kernel(r):
    small = [(getattr(r, "hbm_" + k), getattr(r, k)) for k in MASKS]
    small += [(r.tokens, r.block.at[0]), (r.grad_out, r.block.at[1])]
    small = copy_all(small, r.sems)
    large = copy_all(in_bands(r.w_down, r.kd), r.sems, len(small))
    for copy in small:
        copy.wait()
    spread(r)
    for copy in large:
        copy.wait()


def fetch_kernel(r):
    for copy in copy_all(in_bands(r.w_gate, r.kg) + in_bands(r.w_up, r.ku), r.sems):
        copy.wait()


def diagonal(out, value):
    rows, size = value.shape
    for b in range(size // BLK):
        band = slice(b * BLK, (b + 1) * BLK)
        out[b * rows : (b + 1) * rows, band] = value[:, band]


def assemble_kernel(r):
    blocks = [ref for name, ref in sorted(vars(r).items()) if name.startswith("block")]
    tok = jnp.concatenate([block[0] for block in blocks], axis=0)
    cot = jnp.concatenate([block[1] for block in blocks], axis=0)
    r.cot[...] = cot
    size = r.tok_d.shape[2]
    r.tok_d[...] = jnp.zeros_like(r.tok_d)
    r.cot_d[...] = jnp.zeros_like(r.cot_d)
    for p in range(r.tok_d.shape[0]):
        part = slice(p * size, (p + 1) * size)
        diagonal(r.tok_d.at[p], tok[:, part])
        diagonal(r.cot_d.at[p], cot[:, part])
    for p in range(r.tok_d.shape[0]):
        r.tok_t[p] = r.tok_d[p].T


def masked_sum(left, right, masks, dims=(1, 0)):
    value = dot(left, right, dims)
    rows = value.shape[0] // len(masks)
    return sum(value[b * rows : (b + 1) * rows, :] * m for b, m in enumerate(masks))


def partial_kernel(which, start, half, tile, r):
    pairs, _, size = r.tok_d.shape
    base = first_unit(which, half) + start
    for first in range(0, r.send.shape[2], tile):
        at = span(base + first, tile)
        local = slice(first, first + tile)
        totals = [0.0, 0.0, 0.0]
        for p in range(pairs):
            part = slice(p * size, (p + 1) * size)
            bands = range(p * size // BLK, (p + 1) * size // BLK)
            for k, (left, right, mask, dims) in enumerate(
                (
                    (r.tok_d[p], r.kg[part, at], r.mg, (1, 0)),
                    (r.tok_d[p], r.ku[part, at], r.mu, (1, 0)),
                    (r.cot_d[p], r.kd[at, part], r.mdt, (1, 1)),
                )
            ):
                totals[k] += masked_sum(left, right, [mask[b, :, at] for b in bands], dims)
        for k, value in enumerate(totals):
            if hasattr(r, "received"):
                value = value + r.received[k, :, local]
                r.own[k, :, local] = value
            r.send[k, :, local] = value.astype(r.send.dtype)


def act_kernel(r):
    others = [ref for name, ref in vars(r).items() if name.startswith("other")]
    gate, up, back = (
        sum((other[k].astype(F32) for other in others), r.own[k]) for k in range(3)
    )
    sigma = 1.0 / (1.0 + jnp.exp(-gate))
    silu = gate * sigma
    slope = sigma * (1.0 + gate * (1.0 - sigma))
    r.act[0] = (silu * up).astype(BF16)
    r.act[1] = (back * up * slope).astype(BF16)
    r.act[2] = (back * silu).astype(BF16)


def add_rows(r, i, block, at):
    width, tile = r.acc.shape[2], r.act_d.shape[3]
    size = min(DEPTH, width)
    for f in range(0, width, size):
        part = slice(f, f + size)

        def masks(mask):
            return [mask[block + b][:, part] for b in range(tile // BLK)]

        r.acc[0, :, part] += masked_sum(r.act_d[i, 0], r.kd[at, part], masks(r.md))
        r.acc[1, :, part] += masked_sum(
            r.act_d[i, 1], r.kg[part, at], masks(r.mgt), (1, 1)
        ) + masked_sum(r.act_d[i, 2], r.ku[part, at], masks(r.mut), (1, 1))


class Outbox:
    def __init__(self, slots, sems):
        self.slots, self.sems = slots, sems
        self.flying, self.count = [None] * slots.shape[0], 0

    def put(self, value, target):
        k = self.count % len(self.flying)
        self.count += 1
        if self.flying[k] is not None:
            self.flying[k].wait()
        self.slots[k] = value
        self.flying[k] = pltpu.make_async_copy(self.slots.at[k], target, self.sems.at[k])
        self.flying[k].start()

    def close(self):
        for copy in self.flying:
            if copy is not None:
                copy.wait()


def back_kernel(items, half, do_rows, do_grads, r):
    tile = r.act_d.shape[3]
    spots = tile // BLK
    if do_rows:
        r.acc[...] = r.sums[...] if hasattr(r, "sums") else jnp.zeros_like(r.acc)
    if do_grads:
        groups, height, _ = r.tok_t.shape
        by_cols, by_rows = Outbox(r.col_slots, r.col_sems), Outbox(r.row_slots, r.row_sems)
    for act, which, start in items:
        act = getattr(r, act)
        _, rows, size = act.shape
        base = first_unit(which, half) + start
        at, block = span(base, size), lax.div(base, BLK)
        tiles = [slice(i * tile, (i + 1) * tile) for i in range(size // tile)]
        for i in range(groups if do_grads else 0):
            band = slice(i * height, (i + 1) * height)
            for out, k, mask in ((r.gg, 1, r.mg), (r.gu, 2, r.mu)):
                right = r.masked_act.at[k - 1]
                for j in range(height // BLK):
                    keep = mask[i * (height // BLK) + j, :, at].astype(BF16)
                    right[j * rows : (j + 1) * rows, :] = act[k] * keep
                by_cols.put(dot(r.tok_t[i], right[...]), out.at[band, at])
        if act is r.act0:
            r.act_d[...] = jnp.zeros_like(r.act_d)
        for i, local in enumerate(tiles):
            for k in range(3 if do_rows else 1):
                diagonal(r.act_d.at[i, k], act[k, :, local])
            if do_grads:
                for b in range(spots):
                    keep = r.md[block + i * spots + b].astype(BF16)
                    r.masked_cot[b * rows : (b + 1) * rows, :] = r.cot[...] * keep
                value = dot(r.act_d[i, 0].T, r.masked_cot[...])
                by_rows.put(value, r.gd.at[span(base + i * tile, tile), :])
        for i in range(len(tiles) if do_rows else 0):
            add_rows(r, i, block + i * spots, span(base + i * tile, tile))
    if do_rows:
        if hasattr(r, "new_sums"):
            r.new_sums[...] = r.acc[...]
        else:
            outs = [ref for name, ref in vars(r).items() if name.startswith("rows")]
            count = outs[0].shape[1]
            for k, out in enumerate(outs):
                out[...] = r.acc[:, k * count : (k + 1) * count, :].astype(out.dtype)
    if do_grads:
        by_cols.close()
        by_rows.close()


def shards(sizes, tokens, w_gate, w_up, w_down, mask_gate, mask_up, mask_down, grad_out):
    n_grid, n_dp = sizes
    width, units = w_gate.shape
    rows = n_grid * tokens.shape[0]
    pairs = n_dp // 2
    half = units // 2
    tile = min(DEPTH, half)
    split = PIECES if sum(PIECES) * tile == half else [half // tile]
    split = [tile * count for count in split]
    starts = [sum(split[:p]) for p in range(len(split))]
    n = len(split)
    direct = n_grid == 4
    grant = lambda mib: mib if rows <= 64 else 32

    def trade(array, s):
        return lax.ppermute(array, "grid", [(i, i ^ s) for i in range(n_grid)])

    def swap(array):
        return lax.ppermute(array, "dp", [(i, i ^ 1) for i in range(n_dp)])

    def across(array):
        return [
            lax.ppermute(
                array,
                "dp",
                [(i, ((i // 2 + s) % pairs) * 2 + i % 2) for i in range(n_dp)],
            )
            for s in range(1, pairs)
        ]

    def shape(*dims, kind=BF16):
        return jax.ShapeDtypeStruct(dims, kind)

    weights = {"w_gate": (w_gate, ANY), "w_up": (w_up, ANY), "w_down": (w_down, ANY)}
    weights = {k: (hbm(w), spec) for k, (w, spec) in weights.items()}

    across_shape = shape(width // BLK, 1, units, kind=F32)
    along_shape = shape(units // BLK, 1, width, kind=F32)
    masks = dict(zip(MASKS, (mask_gate, mask_up, mask_down.T)))
    values = call(
        first_kernel,
        "first",
        {
            "w_down": weights["w_down"],
            **{"hbm_" + k: (hbm(m), ANY) for k, m in masks.items()},
            "tokens": (hbm(tokens), ANY),
            "grad_out": (hbm(grad_out), ANY),
        },
        {
            "block": pinned(shape(2, *tokens.shape)),
            **{k: pinned(across_shape) for k in ("mg", "mu", "mdt")},
            **{k: pinned(along_shape) for k in ("mgt", "mut", "md")},
            "kd": pinned(shape(*w_down.shape)),
        },
        scratch={
            **{k: pltpu.VMEM(m.shape, m.dtype) for k, m in masks.items()},
            "sems": pltpu.SemaphoreType.DMA((SPLIT + len(masks) + 2,)),
        },
        vmem=grant(4),
    )
    block = values["block"]
    if direct:
        blocks = [block] + [trade(block, s) for s in range(1, n_grid)]
    else:
        blocks = [lax.all_gather(block, "grid", axis=1, tiled=True)]
    values |= call(
        fetch_kernel,
        "fetch",
        {"w_gate": weights["w_gate"], "w_up": weights["w_up"], "after": (values["mg"], ANY)},
        {"kg": pinned(shape(*w_gate.shape)), "ku": pinned(shape(*w_up.shape))},
        scratch={"sems": pltpu.SemaphoreType.DMA((2 * SPLIT,))},
        vmem=grant(2),
    )

    pair = min(DEPTH, width) // BLK
    pair_shape = shape(width // (pair * BLK), pair * rows, pair * BLK)
    values |= call(
        assemble_kernel,
        "assemble",
        {
            "after": (values["kg"], ANY),
            **{f"block{k}": (b, whole(b)) for k, b in reversed(list(enumerate(blocks)))},
        },
        {
            "cot": pinned(shape(rows, width)),
            "tok_d": pinned(pair_shape),
            "cot_d": pinned(pair_shape),
            "tok_t": pinned(shape(pair_shape.shape[0], pair * BLK, pair * rows)),
        },
        vmem=grant(4),
    )

    def held(*names):
        return {k: pinned(values[k]) for k in names}

    def partials(which, p, after=None, received=None):
        trio = (3, rows, split[p])
        ins = held("tok_d", "cot_d", "mg", "mu", "mdt", *KEPT)
        outs = {"send": pinned(shape(*trio, kind=F32))}
        if after is not None:
            ins["after"] = (after, ANY)
        if received is not None:
            ins["received"] = pinned(received)
            outs = {"own": pinned(shape(*trio, kind=F32)), "send": pinned(shape(*trio))}
        kernel = functools.partial(partial_kernel, which, starts[p], half, tile)
        return call(kernel, "partials", ins, outs, vmem=grant(2))

    def activate(own, others, after):
        ins = {"own": pinned(own), "after": (after, ANY)}
        ins.update({f"other{k}": pinned(a) for k, a in enumerate(others)})
        outs = {"act": pinned(shape(*own.shape))}
        return call(act_kernel, "activate", ins, outs, vmem=grant(2))["act"]

    def back(pieces, do_rows, do_grads, state, last=False):
        items = [(f"act{k}", which, starts[p]) for k, (which, p, _) in enumerate(pieces)]
        ins = {f"act{k}": pinned(act) for k, (_, _, act) in enumerate(pieces)}
        ins.update(held("md"))
        outs, aliases = {}, {}
        spots, size = tile // BLK, split[pieces[0][1]]
        scratch = {"act_d": pltpu.VMEM((size // tile, 3, spots * rows, tile), BF16)}
        if do_rows:
            ins.update(held("mgt", "mut", *KEPT))
            scratch["acc"] = pltpu.VMEM((2, rows, width), F32)
            if "sums" in state:
                ins["sums"] = pinned(state["sums"])
            if last:
                n_out = n_grid if direct else 1
                out = shape(2, rows // n_out, width, kind=BF16 if direct else F32)
                outs.update({f"rows{k}": pinned(out) for k in range(n_out)})
            else:
                outs["new_sums"] = pinned(shape(2, rows, width, kind=F32))
        if do_grads:
            ins.update(held("tok_t", "cot", "mg", "mu"))
            outs["gg"] = (shape(width, units, kind=F32), ANY)
            outs["gu"] = (shape(width, units, kind=F32), ANY)
            outs["gd"] = (shape(units, width, kind=F32), ANY)
            scratch["masked_act"] = pltpu.VMEM((2, pair * rows, size), BF16)
            scratch["masked_cot"] = pltpu.VMEM((spots * rows, width), BF16)
            by_cols, by_rows = 2 * width // (pair * BLK), size // tile
            scratch["col_slots"] = pltpu.VMEM((by_cols, pair * BLK, size), F32)
            scratch["row_slots"] = pltpu.VMEM((by_rows, tile, width), F32)
            scratch["col_sems"] = pltpu.SemaphoreType.DMA((by_cols,))
            scratch["row_sems"] = pltpu.SemaphoreType.DMA((by_rows,))
            for k in ("gg", "gu", "gd"):
                if k in state:
                    ins["old_" + k] = (state[k], ANY)
                    aliases["old_" + k] = k
            if "rows0" in state:
                ins["after"] = (state["rows0"], ANY)
        got = call(
            functools.partial(back_kernel, items, half, do_rows, do_grads),
            "_".join(["back"] + ["rows"] * do_rows + ["grads"] * do_grads),
            ins,
            outs,
            scratch=scratch,
            aliases=aliases,
            vmem=grant(12 if do_grads else 3),
        )
        return {**state, **{k.replace("new_", ""): v for k, v in got.items()}}

    sent, sums, theirs, after = [], [], [], None
    for which, p in [(1, p) for p in range(n)] + [(0, p) for p in range(n)]:
        if which == 1:
            after = partials(1, p, after)["send"]
            sent.append(swap(after))
        else:
            got = partials(0, p, after, sent[p])
            after = got["own"]
            sums.append(after)
            theirs.append(across(got["send"]))

    state = {}
    for p in range(n):
        last = p == n - 1
        act = activate(sums[p], theirs[p], state.get("sums", after))
        act_other = swap(act)
        state = back([(0, p, act)], True, True, state)
        state = back([(1, p, act_other)], True, not last, state, last)
        if last:
            state = back([(1, p, act_other)], False, True, state)

    if direct:
        both = state["rows0"].astype(F32)
        for s in range(1, n_grid):
            both += trade(state[f"rows{s}"], s).astype(F32)
    else:
        both = lax.psum_scatter(state["rows0"], "grid", scatter_dimension=1, tiled=True)
    both = both.astype(BF16)
    return (both[0], both[1], state["gg"], state["gu"], state["gd"])


def solution(mesh):
    in_specs = (
        P(("groups", "grid"), "dp"),
        P("dp", "grid"),
        P("dp", "grid"),
        P("grid", "dp"),
        P(("groups", "dp"), "grid"),
        P(("groups", "dp"), "grid"),
        P(("groups", "grid"), "dp"),
        P(("groups", "grid"), "dp"),
    )
    out_specs = (
        P(("groups", "grid"), "dp"),
        P(("groups", "grid"), "dp"),
        P(("groups", "dp"), "grid"),
        P(("groups", "dp"), "grid"),
        P(("groups", "grid"), "dp"),
    )
    sizes = (mesh.shape["grid"], mesh.shape["dp"])
    return jax.shard_map(
        functools.partial(shards, sizes),
        mesh=mesh,
        in_specs=in_specs,
        out_specs=out_specs,
        check_vma=False,
    )
```

```python
import functools
import types

import jax
import jax.numpy as jnp
from jax import lax
from jax.experimental import pallas as pl
from jax.experimental.pallas import tpu as pltpu
from jax.sharding import PartitionSpec as P

BLK = 128
MIB = 1024 * 1024
DEPTH = 256
ANY = pl.BlockSpec(memory_space=pl.ANY)
PIECES = [2, 3, 3]
SPLIT = 4
KEPT = ("kg", "ku", "kd")
MASKS = ("mask_gate", "mask_up", "mask_down_t")
F32 = jnp.float32
BF16 = jnp.bfloat16


def dot(left, right, dims=(1, 0)):
    return lax.dot_general(
        left, right, (((dims[0],), (dims[1],)), ((), ())), preferred_element_type=F32
    )


def pinned(array):
    spec = pl.BlockSpec(memory_space=pltpu.VMEM)
    if isinstance(array, jax.ShapeDtypeStruct):
        return (pltpu.VMEM(array.shape, array.dtype), spec)
    return (pltpu.with_memory_space_constraint(array, pltpu.VMEM), spec)


def call(kernel, name, ins, outs, scratch=None, aliases=None, vmem=2):
    scratch = scratch or {}
    names = [*ins, *outs, *scratch]
    in_names, out_names = list(ins), list(outs)

    def body(*refs):
        kernel(types.SimpleNamespace(**dict(zip(names, refs))))

    results = pl.pallas_call(
        body,
        out_shape=[shape for shape, _ in outs.values()],
        in_specs=[spec for _, spec in ins.values()],
        out_specs=[spec for _, spec in outs.values()],
        scratch_shapes=list(scratch.values()),
        input_output_aliases={
            in_names.index(i): out_names.index(o) for i, o in (aliases or {}).items()
        },
        compiler_params=pltpu.CompilerParams(vmem_limit_bytes=vmem * MIB),
        cost_estimate=pl.CostEstimate(flops=1, bytes_accessed=1, transcendentals=0),
        name=name,
    )(*[array for array, _ in ins.values()])
    return dict(zip(out_names, results))


def hbm(array):
    return pltpu.with_memory_space_constraint(array, pltpu.HBM)


def whole(array):
    return pl.BlockSpec(array.shape, lambda *_: (0,) * len(array.shape))


def spread(r):
    def pattern(blocks):
        at = lax.broadcasted_iota(jnp.int32, (blocks, blocks * BLK), 0) * BLK
        column = lax.broadcasted_iota(jnp.int32, (blocks, blocks * BLK), 1)
        return ((column >= at) & (column < at + BLK)).astype(F32).astype(BF16)

    across, along = r.mask_gate.shape
    units, features = pattern(along), pattern(across)
    for mask, by_units, by_features in (
        (r.mask_gate, r.mg, r.mgt),
        (r.mask_up, r.mu, r.mut),
        (r.mask_down_t, r.mdt, r.md),
    ):
        entries = mask[...].astype(F32).astype(BF16)
        value = dot(entries, units)
        for b in range(across):
            by_units[b] = value[b : b + 1, :]
        value = dot(entries, features, (0, 0))
        for b in range(along):
            by_features[b] = value[b : b + 1, :]


def first_unit(which, half):
    core = lax.rem(lax.axis_index("dp"), 2)
    return (core if which == 0 else 1 - core) * half


def span(start, size):
    return pl.ds(pl.multiple_of(start, BLK), size)


def fetch_kernel(r):
    copies = []
    for source, target in ((r.w_gate, r.kg), (r.w_up, r.ku), (r.w_down, r.kd)):
        height = source.shape[0] // SPLIT
        for k in range(SPLIT):
            rows = slice(k * height, (k + 1) * height)
            copies.append((source.at[rows, :], target.at[rows, :]))
    for k in MASKS:
        copies.append((getattr(r, "hbm_" + k), getattr(r, k)))
    copies = [pltpu.make_async_copy(a, b, r.sems.at[k]) for k, (a, b) in enumerate(copies)]
    for copy in copies[-len(MASKS) :] + copies[: -len(MASKS)]:
        copy.start()
    for copy in copies[-len(MASKS) :]:
        copy.wait()
    spread(r)
    for copy in copies[: -len(MASKS)]:
        copy.wait()


def diagonal(out, value):
    rows, size = value.shape
    for b in range(size // BLK):
        band = slice(b * BLK, (b + 1) * BLK)
        out[b * rows : (b + 1) * rows, band] = value[:, band]


def assemble_kernel(r):
    blocks = [ref for name, ref in sorted(vars(r).items()) if name.startswith("block")]
    tok = jnp.concatenate([block[0] for block in blocks], axis=0)
    cot = jnp.concatenate([block[1] for block in blocks], axis=0)
    r.cot[...] = cot
    size = r.tok_d.shape[2]
    r.tok_d[...] = jnp.zeros_like(r.tok_d)
    r.cot_d[...] = jnp.zeros_like(r.cot_d)
    for p in range(r.tok_d.shape[0]):
        part = slice(p * size, (p + 1) * size)
        diagonal(r.tok_d.at[p], tok[:, part])
        diagonal(r.cot_d.at[p], cot[:, part])
    for p in range(r.tok_d.shape[0]):
        r.tok_t[p] = r.tok_d[p].T


def masked_sum(left, right, masks, dims=(1, 0)):
    value = dot(left, right, dims)
    rows = value.shape[0] // len(masks)
    return sum(value[b * rows : (b + 1) * rows, :] * m for b, m in enumerate(masks))


def partial_kernel(which, start, half, tile, r):
    pairs, _, size = r.tok_d.shape
    base = first_unit(which, half) + start
    for first in range(0, r.send.shape[2], tile):
        at = span(base + first, tile)
        local = slice(first, first + tile)
        totals = [0.0, 0.0, 0.0]
        for p in range(pairs):
            part = slice(p * size, (p + 1) * size)
            bands = range(p * size // BLK, (p + 1) * size // BLK)
            for k, (left, right, mask, dims) in enumerate(
                (
                    (r.tok_d[p], r.kg[part, at], r.mg, (1, 0)),
                    (r.tok_d[p], r.ku[part, at], r.mu, (1, 0)),
                    (r.cot_d[p], r.kd[at, part], r.mdt, (1, 1)),
                )
            ):
                totals[k] += masked_sum(left, right, [mask[b, :, at] for b in bands], dims)
        for k, value in enumerate(totals):
            if hasattr(r, "received"):
                value = value + r.received[k, :, local]
                r.own[k, :, local] = value
            r.send[k, :, local] = value.astype(r.send.dtype)


def act_kernel(r):
    others = [ref for name, ref in vars(r).items() if name.startswith("other")]
    gate, up, back = (
        sum((other[k].astype(F32) for other in others), r.own[k]) for k in range(3)
    )
    sigma = 1.0 / (1.0 + jnp.exp(-gate))
    silu = gate * sigma
    slope = sigma * (1.0 + gate * (1.0 - sigma))
    r.act[0] = (silu * up).astype(BF16)
    r.act[1] = (back * up * slope).astype(BF16)
    r.act[2] = (back * silu).astype(BF16)


def add_rows(r, i, block, at):
    width, tile = r.acc.shape[2], r.act_d.shape[3]
    size = min(DEPTH, width)
    for f in range(0, width, size):
        part = slice(f, f + size)

        def masks(mask):
            return [mask[block + b][:, part] for b in range(tile // BLK)]

        r.acc[0, :, part] += masked_sum(r.act_d[i, 0], r.kd[at, part], masks(r.md))
        r.acc[1, :, part] += masked_sum(
            r.act_d[i, 1], r.kg[part, at], masks(r.mgt), (1, 1)
        ) + masked_sum(r.act_d[i, 2], r.ku[part, at], masks(r.mut), (1, 1))


class Outbox:
    def __init__(self, slots, sems):
        self.slots, self.sems = slots, sems
        self.flying, self.count = [None] * slots.shape[0], 0

    def put(self, value, target):
        k = self.count % len(self.flying)
        self.count += 1
        if self.flying[k] is not None:
            self.flying[k].wait()
        self.slots[k] = value
        self.flying[k] = pltpu.make_async_copy(self.slots.at[k], target, self.sems.at[k])
        self.flying[k].start()

    def close(self):
        for copy in self.flying:
            if copy is not None:
                copy.wait()


def back_kernel(items, half, do_rows, do_grads, r):
    tile = r.act_d.shape[3]
    spots = tile // BLK
    if do_rows:
        r.acc[...] = r.sums[...] if hasattr(r, "sums") else jnp.zeros_like(r.acc)
    if do_grads:
        groups, height, _ = r.tok_t.shape
        by_cols, by_rows = Outbox(r.col_slots, r.col_sems), Outbox(r.row_slots, r.row_sems)
    for act, which, start in items:
        act = getattr(r, act)
        _, rows, size = act.shape
        base = first_unit(which, half) + start
        at, block = span(base, size), lax.div(base, BLK)
        tiles = [slice(i * tile, (i + 1) * tile) for i in range(size // tile)]
        for i in range(groups if do_grads else 0):
            band = slice(i * height, (i + 1) * height)
            for out, k, mask in ((r.gg, 1, r.mg), (r.gu, 2, r.mu)):
                right = r.masked_act.at[k - 1]
                for j in range(height // BLK):
                    keep = mask[i * (height // BLK) + j, :, at].astype(BF16)
                    right[j * rows : (j + 1) * rows, :] = act[k] * keep
                by_cols.put(dot(r.tok_t[i], right[...]), out.at[band, at])
        if act is r.act0:
            r.act_d[...] = jnp.zeros_like(r.act_d)
        for i, local in enumerate(tiles):
            for k in range(3 if do_rows else 1):
                diagonal(r.act_d.at[i, k], act[k, :, local])
            if do_grads:
                for b in range(spots):
                    keep = r.md[block + i * spots + b].astype(BF16)
                    r.masked_cot[b * rows : (b + 1) * rows, :] = r.cot[...] * keep
                value = dot(r.act_d[i, 0].T, r.masked_cot[...])
                by_rows.put(value, r.gd.at[span(base + i * tile, tile), :])
        for i in range(len(tiles) if do_rows else 0):
            add_rows(r, i, block + i * spots, span(base + i * tile, tile))
    if do_rows:
        if hasattr(r, "new_sums"):
            r.new_sums[...] = r.acc[...]
        else:
            outs = [ref for name, ref in vars(r).items() if name.startswith("rows")]
            count = outs[0].shape[1]
            for k, out in enumerate(outs):
                out[...] = r.acc[:, k * count : (k + 1) * count, :].astype(out.dtype)
    if do_grads:
        by_cols.close()
        by_rows.close()


def shards(sizes, tokens, w_gate, w_up, w_down, mask_gate, mask_up, mask_down, grad_out):
    n_grid, n_dp = sizes
    width, units = w_gate.shape
    rows = n_grid * tokens.shape[0]
    pairs = n_dp // 2
    half = units // 2
    tile = min(DEPTH, half)
    split = PIECES if sum(PIECES) * tile == half else [half // tile]
    split = [tile * count for count in split]
    starts = [sum(split[:p]) for p in range(len(split))]
    n = len(split)
    direct = n_grid == 4
    grant = lambda mib: mib if rows <= 64 else 32

    def trade(array, s):
        return lax.ppermute(array, "grid", [(i, i ^ s) for i in range(n_grid)])

    def swap(array):
        return lax.ppermute(array, "dp", [(i, i ^ 1) for i in range(n_dp)])

    def across(array):
        return [
            lax.ppermute(
                array,
                "dp",
                [(i, ((i // 2 + s) % pairs) * 2 + i % 2) for i in range(n_dp)],
            )
            for s in range(1, pairs)
        ]

    def shape(*dims, kind=BF16):
        return jax.ShapeDtypeStruct(dims, kind)

    weights = {"w_gate": (w_gate, ANY), "w_up": (w_up, ANY), "w_down": (w_down, ANY)}
    weights = {k: (hbm(w), spec) for k, (w, spec) in weights.items()}

    block = jnp.stack([tokens, grad_out])
    if direct:
        blocks = [block] + [trade(block, s) for s in range(1, n_grid)]
    else:
        blocks = [lax.all_gather(block, "grid", axis=1, tiled=True)]

    across_shape = shape(width // BLK, 1, units, kind=F32)
    along_shape = shape(units // BLK, 1, width, kind=F32)
    masks = dict(zip(MASKS, (mask_gate, mask_up, mask_down.T)))
    values = call(
        fetch_kernel,
        "fetch",
        {**weights, **{"hbm_" + k: (hbm(m), ANY) for k, m in masks.items()}},
        {
            **{k: pinned(across_shape) for k in ("mg", "mu", "mdt")},
            **{k: pinned(along_shape) for k in ("mgt", "mut", "md")},
            **{k: pinned(shape(*w.shape)) for k, w in zip(KEPT, (w_gate, w_up, w_down))},
        },
        scratch={
            **{k: pltpu.VMEM(m.shape, m.dtype) for k, m in masks.items()},
            "sems": pltpu.SemaphoreType.DMA((3 * SPLIT + len(masks),)),
        },
        vmem=grant(4),
    )

    pair = min(DEPTH, width) // BLK
    pair_shape = shape(width // (pair * BLK), pair * rows, pair * BLK)
    values |= call(
        assemble_kernel,
        "assemble",
        {
            "after": (values["mg"], ANY),
            **{f"block{k}": (b, whole(b)) for k, b in reversed(list(enumerate(blocks)))},
        },
        {
            "cot": pinned(shape(rows, width)),
            "tok_d": pinned(pair_shape),
            "cot_d": pinned(pair_shape),
            "tok_t": pinned(shape(pair_shape.shape[0], pair * BLK, pair * rows)),
        },
        vmem=grant(4),
    )

    def held(*names):
        return {k: pinned(values[k]) for k in names}

    def partials(which, p, after=None, received=None):
        trio = (3, rows, split[p])
        ins = held("tok_d", "cot_d", "mg", "mu", "mdt", *KEPT)
        outs = {"send": pinned(shape(*trio, kind=F32))}
        if after is not None:
            ins["after"] = (after, ANY)
        if received is not None:
            ins["received"] = pinned(received)
            outs = {"own": pinned(shape(*trio, kind=F32)), "send": pinned(shape(*trio))}
        kernel = functools.partial(partial_kernel, which, starts[p], half, tile)
        return call(kernel, "partials", ins, outs, vmem=grant(2))

    def activate(own, others, after):
        ins = {"own": pinned(own), "after": (after, ANY)}
        ins.update({f"other{k}": pinned(a) for k, a in enumerate(others)})
        outs = {"act": pinned(shape(*own.shape))}
        return call(act_kernel, "activate", ins, outs, vmem=grant(2))["act"]

    def back(pieces, do_rows, do_grads, state, last=False):
        items = [(f"act{k}", which, starts[p]) for k, (which, p, _) in enumerate(pieces)]
        ins = {f"act{k}": pinned(act) for k, (_, _, act) in enumerate(pieces)}
        ins.update(held("md"))
        outs, aliases = {}, {}
        spots, size = tile // BLK, split[pieces[0][1]]
        scratch = {"act_d": pltpu.VMEM((size // tile, 3, spots * rows, tile), BF16)}
        if do_rows:
            ins.update(held("mgt", "mut", *KEPT))
            scratch["acc"] = pltpu.VMEM((2, rows, width), F32)
            if "sums" in state:
                ins["sums"] = pinned(state["sums"])
            if last:
                n_out = n_grid if direct else 1
                out = shape(2, rows // n_out, width, kind=BF16 if direct else F32)
                outs.update({f"rows{k}": pinned(out) for k in range(n_out)})
            else:
                outs["new_sums"] = pinned(shape(2, rows, width, kind=F32))
        if do_grads:
            ins.update(held("tok_t", "cot", "mg", "mu"))
            outs["gg"] = (shape(width, units, kind=F32), ANY)
            outs["gu"] = (shape(width, units, kind=F32), ANY)
            outs["gd"] = (shape(units, width, kind=F32), ANY)
            scratch["masked_act"] = pltpu.VMEM((2, pair * rows, size), BF16)
            scratch["masked_cot"] = pltpu.VMEM((spots * rows, width), BF16)
            by_cols, by_rows = 2 * width // (pair * BLK), size // tile
            scratch["col_slots"] = pltpu.VMEM((by_cols, pair * BLK, size), F32)
            scratch["row_slots"] = pltpu.VMEM((by_rows, tile, width), F32)
            scratch["col_sems"] = pltpu.SemaphoreType.DMA((by_cols,))
            scratch["row_sems"] = pltpu.SemaphoreType.DMA((by_rows,))
            for k in ("gg", "gu", "gd"):
                if k in state:
                    ins["old_" + k] = (state[k], ANY)
                    aliases["old_" + k] = k
            if "rows0" in state:
                ins["after"] = (state["rows0"], ANY)
        got = call(
            functools.partial(back_kernel, items, half, do_rows, do_grads),
            "_".join(["back"] + ["rows"] * do_rows + ["grads"] * do_grads),
            ins,
            outs,
            scratch=scratch,
            aliases=aliases,
            vmem=grant(12 if do_grads else 3),
        )
        return {**state, **{k.replace("new_", ""): v for k, v in got.items()}}

    sent, sums, theirs, after = [], [], [], None
    for p in range(n + 1):
        if p < n:
            after = partials(1, p, after)["send"]
            sent.append(swap(after))
        if p > 0:
            got = partials(0, p - 1, after, sent[p - 1])
            after = got["own"]
            sums.append(after)
            theirs.append(across(got["send"]))

    state = {}
    for p in range(n):
        last = p == n - 1
        act = activate(sums[p], theirs[p], state.get("sums", after))
        act_other = swap(act)
        both_halves = [(0, p, act), (1, p, act_other)]
        if last:
            state = back(both_halves[:1], True, False, state)
            state = back(both_halves[1:], True, False, state, last)
            state = back(both_halves, False, True, state)
        else:
            state = back(both_halves, True, True, state)

    if direct:
        both = state["rows0"].astype(F32)
        for s in range(1, n_grid):
            both += trade(state[f"rows{s}"], s).astype(F32)
    else:
        both = lax.psum_scatter(state["rows0"], "grid", scatter_dimension=1, tiled=True)
    both = both.astype(BF16)
    return (both[0], both[1], state["gg"], state["gu"], state["gd"])


def solution(mesh):
    in_specs = (
        P(("groups", "grid"), "dp"),
        P("dp", "grid"),
        P("dp", "grid"),
        P("grid", "dp"),
        P(("groups", "dp"), "grid"),
        P(("groups", "dp"), "grid"),
        P(("groups", "grid"), "dp"),
        P(("groups", "grid"), "dp"),
    )
    out_specs = (
        P(("groups", "grid"), "dp"),
        P(("groups", "grid"), "dp"),
        P(("groups", "dp"), "grid"),
        P(("groups", "dp"), "grid"),
        P(("groups", "grid"), "dp"),
    )
    sizes = (mesh.shape["grid"], mesh.shape["dp"])
    return jax.shard_map(
        functools.partial(shards, sizes),
        mesh=mesh,
        in_specs=in_specs,
        out_specs=out_specs,
        check_vma=False,
    )
```

```python
import functools
import types

import jax
import jax.numpy as jnp
from jax import lax
from jax.experimental import pallas as pl
from jax.experimental.pallas import tpu as pltpu
from jax.sharding import PartitionSpec as P

BLK = 128
MIB = 1024 * 1024
DEPTH = 256
ANY = pl.BlockSpec(memory_space=pl.ANY)
PIECES = [2, 3, 3]
SPLIT = 4
KEPT = ("kg", "ku", "kd")
MASKS = ("mask_gate", "mask_up", "mask_down_t")
F32 = jnp.float32
BF16 = jnp.bfloat16


def dot(left, right, dims=(1, 0)):
    return lax.dot_general(
        left, right, (((dims[0],), (dims[1],)), ((), ())), preferred_element_type=F32
    )


def pinned(array):
    spec = pl.BlockSpec(memory_space=pltpu.VMEM)
    if isinstance(array, jax.ShapeDtypeStruct):
        return (pltpu.VMEM(array.shape, array.dtype), spec)
    return (pltpu.with_memory_space_constraint(array, pltpu.VMEM), spec)


def call(kernel, name, ins, outs, scratch=None, aliases=None, vmem=2):
    scratch = scratch or {}
    names = [*ins, *outs, *scratch]
    in_names, out_names = list(ins), list(outs)

    def body(*refs):
        kernel(types.SimpleNamespace(**dict(zip(names, refs))))

    results = pl.pallas_call(
        body,
        out_shape=[shape for shape, _ in outs.values()],
        in_specs=[spec for _, spec in ins.values()],
        out_specs=[spec for _, spec in outs.values()],
        scratch_shapes=list(scratch.values()),
        input_output_aliases={
            in_names.index(i): out_names.index(o) for i, o in (aliases or {}).items()
        },
        compiler_params=pltpu.CompilerParams(vmem_limit_bytes=vmem * MIB),
        cost_estimate=pl.CostEstimate(flops=1, bytes_accessed=1, transcendentals=0),
        name=name,
    )(*[array for array, _ in ins.values()])
    return dict(zip(out_names, results))


def hbm(array):
    return pltpu.with_memory_space_constraint(array, pltpu.HBM)


def whole(array):
    return pl.BlockSpec(array.shape, lambda *_: (0,) * len(array.shape))


def spread(r):
    def pattern(blocks):
        at = lax.broadcasted_iota(jnp.int32, (blocks, blocks * BLK), 0) * BLK
        column = lax.broadcasted_iota(jnp.int32, (blocks, blocks * BLK), 1)
        return ((column >= at) & (column < at + BLK)).astype(F32).astype(BF16)

    across, along = r.mask_gate.shape
    units, features = pattern(along), pattern(across)
    for mask, by_units, by_features in (
        (r.mask_gate, r.mg, r.mgt),
        (r.mask_up, r.mu, r.mut),
        (r.mask_down_t, r.mdt, r.md),
    ):
        entries = mask[...].astype(F32).astype(BF16)
        value = dot(entries, units)
        for b in range(across):
            by_units[b] = value[b : b + 1, :]
        value = dot(entries, features, (0, 0))
        for b in range(along):
            by_features[b] = value[b : b + 1, :]


def first_unit(which, half):
    core = lax.rem(lax.axis_index("dp"), 2)
    return (core if which == 0 else 1 - core) * half


def span(start, size):
    return pl.ds(pl.multiple_of(start, BLK), size)


def fetch_kernel(r):
    copies = []
    for k in MASKS:
        copies.append((getattr(r, "hbm_" + k), getattr(r, k)))
    copies = [pltpu.make_async_copy(a, b, r.sems.at[k]) for k, (a, b) in enumerate(copies)]
    for copy in copies[-len(MASKS) :] + copies[: -len(MASKS)]:
        copy.start()
    for copy in copies[-len(MASKS) :]:
        copy.wait()
    spread(r)
    for copy in copies[: -len(MASKS)]:
        copy.wait()


def diagonal(out, value):
    rows, size = value.shape
    for b in range(size // BLK):
        band = slice(b * BLK, (b + 1) * BLK)
        out[b * rows : (b + 1) * rows, band] = value[:, band]


def assemble_kernel(r):
    blocks = [ref for name, ref in sorted(vars(r).items()) if name.startswith("block")]
    tok = jnp.concatenate([block[0] for block in blocks], axis=0)
    cot = jnp.concatenate([block[1] for block in blocks], axis=0)
    r.cot[...] = cot
    size = r.tok_d.shape[2]
    r.tok_d[...] = jnp.zeros_like(r.tok_d)
    r.cot_d[...] = jnp.zeros_like(r.cot_d)
    for p in range(r.tok_d.shape[0]):
        part = slice(p * size, (p + 1) * size)
        diagonal(r.tok_d.at[p], tok[:, part])
        diagonal(r.cot_d.at[p], cot[:, part])
    for p in range(r.tok_d.shape[0]):
        r.tok_t[p] = r.tok_d[p].T


def masked_sum(left, right, masks, dims=(1, 0)):
    value = dot(left, right, dims)
    rows = value.shape[0] // len(masks)
    return sum(value[b * rows : (b + 1) * rows, :] * m for b, m in enumerate(masks))


def partial_kernel(which, start, half, tile, r):
    pairs, _, size = r.tok_d.shape
    base = first_unit(which, half) + start
    for first in range(0, r.send.shape[2], tile):
        at = span(base + first, tile)
        local = slice(first, first + tile)
        totals = [0.0, 0.0, 0.0]
        for p in range(pairs):
            part = slice(p * size, (p + 1) * size)
            bands = range(p * size // BLK, (p + 1) * size // BLK)
            for k, (left, right, mask, dims) in enumerate(
                (
                    (r.tok_d[p], r.kg[part, at], r.mg, (1, 0)),
                    (r.tok_d[p], r.ku[part, at], r.mu, (1, 0)),
                    (r.cot_d[p], r.kd[at, part], r.mdt, (1, 1)),
                )
            ):
                totals[k] += masked_sum(left, right, [mask[b, :, at] for b in bands], dims)
        for k, value in enumerate(totals):
            if hasattr(r, "received"):
                value = value + r.received[k, :, local]
                r.own[k, :, local] = value
            r.send[k, :, local] = value.astype(r.send.dtype)


def act_kernel(r):
    others = [ref for name, ref in vars(r).items() if name.startswith("other")]
    gate, up, back = (
        sum((other[k].astype(F32) for other in others), r.own[k]) for k in range(3)
    )
    sigma = 1.0 / (1.0 + jnp.exp(-gate))
    silu = gate * sigma
    slope = sigma * (1.0 + gate * (1.0 - sigma))
    r.act[0] = (silu * up).astype(BF16)
    r.act[1] = (back * up * slope).astype(BF16)
    r.act[2] = (back * silu).astype(BF16)


def add_rows(r, i, block, at):
    width, tile = r.acc.shape[2], r.act_d.shape[3]
    size = min(DEPTH, width)
    for f in range(0, width, size):
        part = slice(f, f + size)

        def masks(mask):
            return [mask[block + b][:, part] for b in range(tile // BLK)]

        r.acc[0, :, part] += masked_sum(r.act_d[i, 0], r.kd[at, part], masks(r.md))
        r.acc[1, :, part] += masked_sum(
            r.act_d[i, 1], r.kg[part, at], masks(r.mgt), (1, 1)
        ) + masked_sum(r.act_d[i, 2], r.ku[part, at], masks(r.mut), (1, 1))


class Outbox:
    def __init__(self, slots, sems):
        self.slots, self.sems = slots, sems
        self.flying, self.count = [None] * slots.shape[0], 0

    def put(self, value, target):
        k = self.count % len(self.flying)
        self.count += 1
        if self.flying[k] is not None:
            self.flying[k].wait()
        self.slots[k] = value
        self.flying[k] = pltpu.make_async_copy(self.slots.at[k], target, self.sems.at[k])
        self.flying[k].start()

    def close(self):
        for copy in self.flying:
            if copy is not None:
                copy.wait()


def back_kernel(items, half, do_rows, do_grads, r):
    tile = r.act_d.shape[3]
    spots = tile // BLK
    r.act_d[...] = jnp.zeros_like(r.act_d)
    if do_rows:
        r.acc[...] = r.sums[...] if hasattr(r, "sums") else jnp.zeros_like(r.acc)
    if do_grads:
        groups, height, _ = r.tok_t.shape
        by_cols, by_rows = Outbox(r.col_slots, r.col_sems), Outbox(r.row_slots, r.row_sems)
    for act, which, start in items:
        act = getattr(r, act)
        _, rows, size = act.shape
        base = first_unit(which, half) + start
        at, block = span(base, size), lax.div(base, BLK)
        tiles = [slice(i * tile, (i + 1) * tile) for i in range(size // tile)]
        for i, local in enumerate(tiles):
            for k in range(3 if do_rows else 1):
                diagonal(r.act_d.at[i, k], act[k, :, local])
        for i in range(max(groups, len(tiles)) if do_grads else 0):
            if i < groups:
                band = slice(i * height, (i + 1) * height)
                for out, k, mask in ((r.gg, 1, r.mg), (r.gu, 2, r.mu)):
                    right = r.masked_act.at[k - 1]
                    for j in range(height // BLK):
                        keep = mask[i * (height // BLK) + j, :, at].astype(BF16)
                        right[j * rows : (j + 1) * rows, :] = act[k] * keep
                    by_cols.put(dot(r.tok_t[i], right[...]), out.at[band, at])
            if i < len(tiles):
                for b in range(spots):
                    keep = r.md[block + i * spots + b].astype(BF16)
                    r.masked_cot[b * rows : (b + 1) * rows, :] = r.cot[...] * keep
                value = dot(r.act_d[i, 0].T, r.masked_cot[...])
                by_rows.put(value, r.gd.at[span(base + i * tile, tile), :])
        for i in range(len(tiles) if do_rows else 0):
            add_rows(r, i, block + i * spots, span(base + i * tile, tile))
    if do_rows:
        if hasattr(r, "new_sums"):
            r.new_sums[...] = r.acc[...]
        else:
            outs = [ref for name, ref in vars(r).items() if name.startswith("rows")]
            count = outs[0].shape[1]
            for k, out in enumerate(outs):
                out[...] = r.acc[:, k * count : (k + 1) * count, :].astype(out.dtype)
    if do_grads:
        by_cols.close()
        by_rows.close()


def shards(sizes, tokens, w_gate, w_up, w_down, mask_gate, mask_up, mask_down, grad_out):
    n_grid, n_dp = sizes
    width, units = w_gate.shape
    rows = n_grid * tokens.shape[0]
    pairs = n_dp // 2
    half = units // 2
    tile = min(DEPTH, half)
    split = PIECES if sum(PIECES) * tile == half else [half // tile]
    split = [tile * count for count in split]
    starts = [sum(split[:p]) for p in range(len(split))]
    n = len(split)
    direct = n_grid == 4
    grant = lambda mib: mib if rows <= 64 else 32

    def trade(array, s):
        return lax.ppermute(array, "grid", [(i, i ^ s) for i in range(n_grid)])

    def swap(array):
        return lax.ppermute(array, "dp", [(i, i ^ 1) for i in range(n_dp)])

    def across(array):
        return [
            lax.ppermute(
                array,
                "dp",
                [(i, ((i // 2 + s) % pairs) * 2 + i % 2) for i in range(n_dp)],
            )
            for s in range(1, pairs)
        ]

    def shape(*dims, kind=BF16):
        return jax.ShapeDtypeStruct(dims, kind)

    weights = {"w_gate": (w_gate, ANY), "w_up": (w_up, ANY), "w_down": (w_down, ANY)}
    weights = {k: (hbm(w), spec) for k, (w, spec) in weights.items()}

    block = jnp.stack([tokens, grad_out])
    if direct:
        blocks = [block] + [trade(block, s) for s in range(1, n_grid)]
    else:
        blocks = [lax.all_gather(block, "grid", axis=1, tiled=True)]

    across_shape = shape(width // BLK, 1, units, kind=F32)
    along_shape = shape(units // BLK, 1, width, kind=F32)
    masks = dict(zip(MASKS, (mask_gate, mask_up, mask_down.T)))
    values = call(
        fetch_kernel,
        "fetch",
        {**weights, **{"hbm_" + k: (hbm(m), ANY) for k, m in masks.items()}},
        {
            **{k: pinned(across_shape) for k in ("mg", "mu", "mdt")},
            **{k: pinned(along_shape) for k in ("mgt", "mut", "md")},
        },
        scratch={
            **{k: pltpu.VMEM(m.shape, m.dtype) for k, m in masks.items()},
            "sems": pltpu.SemaphoreType.DMA((3 * SPLIT + len(masks),)),
        },
        vmem=grant(4),
    )

    values.update(kg=w_gate, ku=w_up, kd=w_down)
    pair = min(DEPTH, width) // BLK
    pair_shape = shape(width // (pair * BLK), pair * rows, pair * BLK)
    values |= call(
        assemble_kernel,
        "assemble",
        {
            "after": (values["mg"], ANY),
            **{f"block{k}": (b, whole(b)) for k, b in reversed(list(enumerate(blocks)))},
        },
        {
            "cot": pinned(shape(rows, width)),
            "tok_d": pinned(pair_shape),
            "cot_d": pinned(pair_shape),
            "tok_t": pinned(shape(pair_shape.shape[0], pair * BLK, pair * rows)),
        },
        vmem=grant(4),
    )

    def held(*names):
        return {k: pinned(values[k]) for k in names}

    def partials(which, p, after=None, received=None):
        trio = (3, rows, split[p])
        ins = held("tok_d", "cot_d", "mg", "mu", "mdt", *KEPT)
        outs = {"send": pinned(shape(*trio, kind=F32))}
        if after is not None:
            ins["after"] = (after, ANY)
        if received is not None:
            ins["received"] = pinned(received)
            outs = {"own": pinned(shape(*trio, kind=F32)), "send": pinned(shape(*trio))}
        kernel = functools.partial(partial_kernel, which, starts[p], half, tile)
        return call(kernel, "partials", ins, outs, vmem=grant(2))

    def activate(own, others, after):
        ins = {"own": pinned(own), "after": (after, ANY)}
        ins.update({f"other{k}": pinned(a) for k, a in enumerate(others)})
        outs = {"act": pinned(shape(*own.shape))}
        return call(act_kernel, "activate", ins, outs, vmem=grant(2))["act"]

    def back(pieces, do_rows, do_grads, state, last=False):
        items = [(f"act{k}", which, starts[p]) for k, (which, p, _) in enumerate(pieces)]
        ins = {f"act{k}": pinned(act) for k, (_, _, act) in enumerate(pieces)}
        ins.update(held("md"))
        outs, aliases = {}, {}
        spots, size = tile // BLK, split[pieces[0][1]]
        scratch = {"act_d": pltpu.VMEM((size // tile, 3, spots * rows, tile), BF16)}
        if do_rows:
            ins.update(held("mgt", "mut", *KEPT))
            scratch["acc"] = pltpu.VMEM((2, rows, width), F32)
            if "sums" in state:
                ins["sums"] = pinned(state["sums"])
            if last:
                n_out = n_grid if direct else 1
                out = shape(2, rows // n_out, width, kind=BF16 if direct else F32)
                outs.update({f"rows{k}": pinned(out) for k in range(n_out)})
            else:
                outs["new_sums"] = pinned(shape(2, rows, width, kind=F32))
        if do_grads:
            ins.update(held("tok_t", "cot", "mg", "mu"))
            outs["gg"] = (shape(width, units, kind=F32), ANY)
            outs["gu"] = (shape(width, units, kind=F32), ANY)
            outs["gd"] = (shape(units, width, kind=F32), ANY)
            scratch["masked_act"] = pltpu.VMEM((2, pair * rows, size), BF16)
            scratch["masked_cot"] = pltpu.VMEM((spots * rows, width), BF16)
            by_cols, by_rows = 2 * width // (pair * BLK), size // tile
            scratch["col_slots"] = pltpu.VMEM((by_cols, pair * BLK, size), F32)
            scratch["row_slots"] = pltpu.VMEM((by_rows, tile, width), F32)
            scratch["col_sems"] = pltpu.SemaphoreType.DMA((by_cols,))
            scratch["row_sems"] = pltpu.SemaphoreType.DMA((by_rows,))
            for k in ("gg", "gu", "gd"):
                if k in state:
                    ins["old_" + k] = (state[k], ANY)
                    aliases["old_" + k] = k
            if "rows0" in state:
                ins["after"] = (state["rows0"], ANY)
        got = call(
            functools.partial(back_kernel, items, half, do_rows, do_grads),
            "_".join(["back"] + ["rows"] * do_rows + ["grads"] * do_grads),
            ins,
            outs,
            scratch=scratch,
            aliases=aliases,
            vmem=grant(12 if do_grads else 3),
        )
        return {**state, **{k.replace("new_", ""): v for k, v in got.items()}}

    sent, sums, theirs, after = [], [], [], None
    for p in range(n + 1):
        if p < n:
            after = partials(1, p, after)["send"]
            sent.append(swap(after))
        if p > 0:
            got = partials(0, p - 1, after, sent[p - 1])
            after = got["own"]
            sums.append(after)
            theirs.append(across(got["send"]))

    state = {}
    for p in range(n):
        last = p == n - 1
        act = activate(sums[p], theirs[p], state.get("sums", after))
        act_other = swap(act)
        state = back([(0, p, act)], True, not last, state)
        state = back([(1, p, act_other)], True, not last, state, last)
        if last:
            state = back([(0, p, act), (1, p, act_other)], False, True, state)

    if direct:
        both = state["rows0"].astype(F32)
        for s in range(1, n_grid):
            both += trade(state[f"rows{s}"], s).astype(F32)
    else:
        both = lax.psum_scatter(state["rows0"], "grid", scatter_dimension=1, tiled=True)
    both = both.astype(BF16)
    return (both[0], both[1], state["gg"], state["gu"], state["gd"])


def solution(mesh):
    in_specs = (
        P(("groups", "grid"), "dp"),
        P("dp", "grid"),
        P("dp", "grid"),
        P("grid", "dp"),
        P(("groups", "dp"), "grid"),
        P(("groups", "dp"), "grid"),
        P(("groups", "grid"), "dp"),
        P(("groups", "grid"), "dp"),
    )
    out_specs = (
        P(("groups", "grid"), "dp"),
        P(("groups", "grid"), "dp"),
        P(("groups", "dp"), "grid"),
        P(("groups", "dp"), "grid"),
        P(("groups", "grid"), "dp"),
    )
    sizes = (mesh.shape["grid"], mesh.shape["dp"])
    return jax.shard_map(
        functools.partial(shards, sizes),
        mesh=mesh,
        in_specs=in_specs,
        out_specs=out_specs,
        check_vma=False,
    )
```

```python
import functools
import types

import jax
import jax.numpy as jnp
from jax import lax
from jax.experimental import pallas as pl
from jax.experimental.pallas import tpu as pltpu
from jax.sharding import PartitionSpec as P

BLK = 128
MIB = 1024 * 1024
DEPTH = 256
ANY = pl.BlockSpec(memory_space=pl.ANY)
PIECES = [1, 3, 4]
SPLIT = 4
KEPT = ("kg", "ku", "kd")
MASKS = ("mask_gate", "mask_up", "mask_down_t")
F32 = jnp.float32
BF16 = jnp.bfloat16


def dot(left, right, dims=(1, 0)):
    return lax.dot_general(
        left, right, (((dims[0],), (dims[1],)), ((), ())), preferred_element_type=F32
    )


def pinned(array):
    spec = pl.BlockSpec(memory_space=pltpu.VMEM)
    if isinstance(array, jax.ShapeDtypeStruct):
        return (pltpu.VMEM(array.shape, array.dtype), spec)
    return (pltpu.with_memory_space_constraint(array, pltpu.VMEM), spec)


def call(kernel, name, ins, outs, scratch=None, aliases=None, vmem=2):
    scratch = scratch or {}
    names = [*ins, *outs, *scratch]
    in_names, out_names = list(ins), list(outs)

    def body(*refs):
        kernel(types.SimpleNamespace(**dict(zip(names, refs))))

    results = pl.pallas_call(
        body,
        out_shape=[shape for shape, _ in outs.values()],
        in_specs=[spec for _, spec in ins.values()],
        out_specs=[spec for _, spec in outs.values()],
        scratch_shapes=list(scratch.values()),
        input_output_aliases={
            in_names.index(i): out_names.index(o) for i, o in (aliases or {}).items()
        },
        compiler_params=pltpu.CompilerParams(vmem_limit_bytes=vmem * MIB),
        cost_estimate=pl.CostEstimate(flops=1, bytes_accessed=1, transcendentals=0),
        name=name,
    )(*[array for array, _ in ins.values()])
    return dict(zip(out_names, results))


def hbm(array):
    return pltpu.with_memory_space_constraint(array, pltpu.HBM)


def whole(array):
    return pl.BlockSpec(array.shape, lambda *_: (0,) * len(array.shape))


def spread(r):
    def pattern(blocks):
        at = lax.broadcasted_iota(jnp.int32, (blocks, blocks * BLK), 0) * BLK
        column = lax.broadcasted_iota(jnp.int32, (blocks, blocks * BLK), 1)
        return ((column >= at) & (column < at + BLK)).astype(F32).astype(BF16)

    across, along = r.mask_gate.shape
    units, features = pattern(along), pattern(across)
    for mask, by_units, by_features in (
        (r.mask_gate, r.mg, r.mgt),
        (r.mask_up, r.mu, r.mut),
        (r.mask_down_t, r.mdt, r.md),
    ):
        entries = mask[...].astype(F32).astype(BF16)
        value = dot(entries, units)
        for b in range(across):
            by_units[b] = value[b : b + 1, :]
        value = dot(entries, features, (0, 0))
        for b in range(along):
            by_features[b] = value[b : b + 1, :]


def first_unit(which, half):
    core = lax.rem(lax.axis_index("dp"), 2)
    return (core if which == 0 else 1 - core) * half


def span(start, size):
    return pl.ds(pl.multiple_of(start, BLK), size)


def fetch_kernel(r):
    copies = []
    for k in MASKS:
        copies.append((getattr(r, "hbm_" + k), getattr(r, k)))
    copies = [pltpu.make_async_copy(a, b, r.sems.at[k]) for k, (a, b) in enumerate(copies)]
    for copy in copies[-len(MASKS) :] + copies[: -len(MASKS)]:
        copy.start()
    for copy in copies[-len(MASKS) :]:
        copy.wait()
    spread(r)
    for copy in copies[: -len(MASKS)]:
        copy.wait()


def diagonal(out, value):
    rows, size = value.shape
    for b in range(size // BLK):
        band = slice(b * BLK, (b + 1) * BLK)
        out[b * rows : (b + 1) * rows, band] = value[:, band]


def assemble_kernel(r):
    blocks = [ref for name, ref in sorted(vars(r).items()) if name.startswith("block")]
    tok = jnp.concatenate([block[0] for block in blocks], axis=0)
    cot = jnp.concatenate([block[1] for block in blocks], axis=0)
    r.cot[...] = cot
    size = r.tok_d.shape[2]
    r.tok_d[...] = jnp.zeros_like(r.tok_d)
    r.cot_d[...] = jnp.zeros_like(r.cot_d)
    for p in range(r.tok_d.shape[0]):
        part = slice(p * size, (p + 1) * size)
        diagonal(r.tok_d.at[p], tok[:, part])
        diagonal(r.cot_d.at[p], cot[:, part])
    for p in range(r.tok_d.shape[0]):
        r.tok_t[p] = r.tok_d[p].T


def masked_sum(left, right, masks, dims=(1, 0)):
    value = dot(left, right, dims)
    rows = value.shape[0] // len(masks)
    return sum(value[b * rows : (b + 1) * rows, :] * m for b, m in enumerate(masks))


def partial_kernel(which, start, half, tile, r):
    pairs, _, size = r.tok_d.shape
    base = first_unit(which, half) + start
    for first in range(0, r.send.shape[2], tile):
        at = span(base + first, tile)
        local = slice(first, first + tile)
        totals = [0.0, 0.0, 0.0]
        for p in range(pairs):
            part = slice(p * size, (p + 1) * size)
            bands = range(p * size // BLK, (p + 1) * size // BLK)
            for k, (left, right, mask, dims) in enumerate(
                (
                    (r.tok_d[p], r.kg[part, at], r.mg, (1, 0)),
                    (r.tok_d[p], r.ku[part, at], r.mu, (1, 0)),
                    (r.cot_d[p], r.kd[at, part], r.mdt, (1, 1)),
                )
            ):
                totals[k] += masked_sum(left, right, [mask[b, :, at] for b in bands], dims)
        for k, value in enumerate(totals):
            if hasattr(r, "received"):
                value = value + r.received[k, :, local]
                r.own[k, :, local] = value
            r.send[k, :, local] = value.astype(r.send.dtype)


def act_kernel(r):
    others = [ref for name, ref in vars(r).items() if name.startswith("other")]
    gate, up, back = (
        sum((other[k].astype(F32) for other in others), r.own[k]) for k in range(3)
    )
    sigma = 1.0 / (1.0 + jnp.exp(-gate))
    silu = gate * sigma
    slope = sigma * (1.0 + gate * (1.0 - sigma))
    r.act[0] = (silu * up).astype(BF16)
    r.act[1] = (back * up * slope).astype(BF16)
    r.act[2] = (back * silu).astype(BF16)


def add_rows(r, i, block, at):
    width, tile = r.acc.shape[2], r.act_d.shape[3]
    size = min(DEPTH, width)
    for f in range(0, width, size):
        part = slice(f, f + size)

        def masks(mask):
            return [mask[block + b][:, part] for b in range(tile // BLK)]

        r.acc[0, :, part] += masked_sum(r.act_d[i, 0], r.kd[at, part], masks(r.md))
        r.acc[1, :, part] += masked_sum(
            r.act_d[i, 1], r.kg[part, at], masks(r.mgt), (1, 1)
        ) + masked_sum(r.act_d[i, 2], r.ku[part, at], masks(r.mut), (1, 1))


class Outbox:
    def __init__(self, slots, sems):
        self.slots, self.sems = slots, sems
        self.flying, self.count = [None] * slots.shape[0], 0

    def put(self, value, target):
        k = self.count % len(self.flying)
        self.count += 1
        if self.flying[k] is not None:
            self.flying[k].wait()
        self.slots[k] = value
        self.flying[k] = pltpu.make_async_copy(self.slots.at[k], target, self.sems.at[k])
        self.flying[k].start()

    def close(self):
        for copy in self.flying:
            if copy is not None:
                copy.wait()


def back_kernel(items, half, do_rows, do_grads, r):
    tile = r.act_d.shape[3]
    spots = tile // BLK
    r.act_d[...] = jnp.zeros_like(r.act_d)
    if do_rows:
        r.acc[...] = r.sums[...] if hasattr(r, "sums") else jnp.zeros_like(r.acc)
    if do_grads:
        groups, height, _ = r.tok_t.shape
        by_cols, by_rows = Outbox(r.col_slots, r.col_sems), Outbox(r.row_slots, r.row_sems)
    for act, which, start in items:
        act = getattr(r, act)
        _, rows, size = act.shape
        base = first_unit(which, half) + start
        at, block = span(base, size), lax.div(base, BLK)
        tiles = [slice(i * tile, (i + 1) * tile) for i in range(size // tile)]
        for i, local in enumerate(tiles):
            for k in range(3 if do_rows else 1):
                diagonal(r.act_d.at[i, k], act[k, :, local])
        for i in range(max(groups, len(tiles)) if do_grads else 0):
            if i < groups:
                band = slice(i * height, (i + 1) * height)
                for out, k, mask in ((r.gg, 1, r.mg), (r.gu, 2, r.mu)):
                    right = r.masked_act.at[k - 1]
                    for j in range(height // BLK):
                        keep = mask[i * (height // BLK) + j, :, at].astype(BF16)
                        right[j * rows : (j + 1) * rows, :] = act[k] * keep
                    by_cols.put(dot(r.tok_t[i], right[...]), out.at[band, at])
            if i < len(tiles):
                for b in range(spots):
                    keep = r.md[block + i * spots + b].astype(BF16)
                    r.masked_cot[b * rows : (b + 1) * rows, :] = r.cot[...] * keep
                value = dot(r.act_d[i, 0].T, r.masked_cot[...])
                by_rows.put(value, r.gd.at[span(base + i * tile, tile), :])
        for i in range(len(tiles) if do_rows else 0):
            add_rows(r, i, block + i * spots, span(base + i * tile, tile))
    if do_rows:
        if hasattr(r, "new_sums"):
            r.new_sums[...] = r.acc[...]
        else:
            outs = [ref for name, ref in vars(r).items() if name.startswith("rows")]
            count = outs[0].shape[1]
            for k, out in enumerate(outs):
                out[...] = r.acc[:, k * count : (k + 1) * count, :].astype(out.dtype)
    if do_grads:
        by_cols.close()
        by_rows.close()


def shards(sizes, tokens, w_gate, w_up, w_down, mask_gate, mask_up, mask_down, grad_out):
    n_grid, n_dp = sizes
    width, units = w_gate.shape
    rows = n_grid * tokens.shape[0]
    pairs = n_dp // 2
    half = units // 2
    tile = min(DEPTH, half)
    split = PIECES if sum(PIECES) * tile == half else [half // tile]
    split = [tile * count for count in split]
    starts = [sum(split[:p]) for p in range(len(split))]
    n = len(split)
    direct = n_grid == 4
    grant = lambda mib: mib if rows <= 64 else 32

    def trade(array, s):
        return lax.ppermute(array, "grid", [(i, i ^ s) for i in range(n_grid)])

    def swap(array):
        return lax.ppermute(array, "dp", [(i, i ^ 1) for i in range(n_dp)])

    def across(array):
        return [
            lax.ppermute(
                array,
                "dp",
                [(i, ((i // 2 + s) % pairs) * 2 + i % 2) for i in range(n_dp)],
            )
            for s in range(1, pairs)
        ]

    def shape(*dims, kind=BF16):
        return jax.ShapeDtypeStruct(dims, kind)

    weights = {"w_gate": (w_gate, ANY), "w_up": (w_up, ANY), "w_down": (w_down, ANY)}
    weights = {k: (hbm(w), spec) for k, (w, spec) in weights.items()}

    block = jnp.stack([tokens, grad_out])
    if direct:
        blocks = [block, trade(block, 1), trade(block, 2)]
        blocks.append(trade(blocks[2], 1))
    else:
        blocks = [lax.all_gather(block, "grid", axis=1, tiled=True)]

    across_shape = shape(width // BLK, 1, units, kind=F32)
    along_shape = shape(units // BLK, 1, width, kind=F32)
    masks = dict(zip(MASKS, (mask_gate, mask_up, mask_down.T)))
    values = call(
        fetch_kernel,
        "fetch",
        {**weights, **{"hbm_" + k: (hbm(m), ANY) for k, m in masks.items()}},
        {
            **{k: pinned(across_shape) for k in ("mg", "mu", "mdt")},
            **{k: pinned(along_shape) for k in ("mgt", "mut", "md")},
        },
        scratch={
            **{k: pltpu.VMEM(m.shape, m.dtype) for k, m in masks.items()},
            "sems": pltpu.SemaphoreType.DMA((3 * SPLIT + len(masks),)),
        },
        vmem=grant(4),
    )

    values.update(kg=w_gate, ku=w_up, kd=w_down)
    pair = min(DEPTH, width) // BLK
    pair_shape = shape(width // (pair * BLK), pair * rows, pair * BLK)
    values |= call(
        assemble_kernel,
        "assemble",
        {
            "after": (values["mg"], ANY),
            **{f"block{k}": (b, whole(b)) for k, b in reversed(list(enumerate(blocks)))},
        },
        {
            "cot": pinned(shape(rows, width)),
            "tok_d": pinned(pair_shape),
            "cot_d": pinned(pair_shape),
            "tok_t": pinned(shape(pair_shape.shape[0], pair * BLK, pair * rows)),
        },
        vmem=grant(4),
    )

    def held(*names):
        return {k: pinned(values[k]) for k in names}

    def partials(which, p, after=None, received=None):
        trio = (3, rows, split[p])
        ins = held("tok_d", "cot_d", "mg", "mu", "mdt", *KEPT)
        outs = {"send": pinned(shape(*trio, kind=F32))}
        if after is not None:
            ins["after"] = (after, ANY)
        if received is not None:
            ins["received"] = pinned(received)
            outs = {"own": pinned(shape(*trio, kind=F32)), "send": pinned(shape(*trio))}
        kernel = functools.partial(partial_kernel, which, starts[p], half, tile)
        return call(kernel, "partials", ins, outs, vmem=grant(2))

    def activate(own, others, after):
        ins = {"own": pinned(own), "after": (after, ANY)}
        ins.update({f"other{k}": pinned(a) for k, a in enumerate(others)})
        outs = {"act": pinned(shape(*own.shape))}
        return call(act_kernel, "activate", ins, outs, vmem=grant(2))["act"]

    def back(pieces, do_rows, do_grads, state, last=False):
        items = [(f"act{k}", which, starts[p]) for k, (which, p, _) in enumerate(pieces)]
        ins = {f"act{k}": pinned(act) for k, (_, _, act) in enumerate(pieces)}
        ins.update(held("md"))
        outs, aliases = {}, {}
        spots, size = tile // BLK, split[pieces[0][1]]
        scratch = {"act_d": pltpu.VMEM((size // tile, 3, spots * rows, tile), BF16)}
        if do_rows:
            ins.update(held("mgt", "mut", *KEPT))
            scratch["acc"] = pltpu.VMEM((2, rows, width), F32)
            if "sums" in state:
                ins["sums"] = pinned(state["sums"])
            if last:
                n_out = n_grid if direct else 1
                out = shape(2, rows // n_out, width, kind=BF16 if direct else F32)
                outs.update({f"rows{k}": pinned(out) for k in range(n_out)})
            else:
                outs["new_sums"] = pinned(shape(2, rows, width, kind=F32))
        if do_grads:
            ins.update(held("tok_t", "cot", "mg", "mu"))
            outs["gg"] = (shape(width, units, kind=F32), ANY)
            outs["gu"] = (shape(width, units, kind=F32), ANY)
            outs["gd"] = (shape(units, width, kind=F32), ANY)
            scratch["masked_act"] = pltpu.VMEM((2, pair * rows, size), BF16)
            scratch["masked_cot"] = pltpu.VMEM((spots * rows, width), BF16)
            by_cols, by_rows = 2 * width // (pair * BLK), size // tile
            if by_rows > 3:
                by_cols = by_cols * 5 // 8
            scratch["col_slots"] = pltpu.VMEM((by_cols, pair * BLK, size), F32)
            scratch["row_slots"] = pltpu.VMEM((by_rows, tile, width), F32)
            scratch["col_sems"] = pltpu.SemaphoreType.DMA((by_cols,))
            scratch["row_sems"] = pltpu.SemaphoreType.DMA((by_rows,))
            for k in ("gg", "gu", "gd"):
                if k in state:
                    ins["old_" + k] = (state[k], ANY)
                    aliases["old_" + k] = k
            if "rows0" in state:
                ins["after"] = (state["rows0"], ANY)
        got = call(
            functools.partial(back_kernel, items, half, do_rows, do_grads),
            "_".join(["back"] + ["rows"] * do_rows + ["grads"] * do_grads),
            ins,
            outs,
            scratch=scratch,
            aliases=aliases,
            vmem=grant(12 if do_grads else 3),
        )
        return {**state, **{k.replace("new_", ""): v for k, v in got.items()}}

    sent, sums, theirs, after = [], [], [], None
    for p in range(n + 1):
        if p < n:
            after = partials(1, p, after)["send"]
            sent.append(swap(after))
        if p > 0:
            got = partials(0, p - 1, after, sent[p - 1])
            after = got["own"]
            sums.append(after)
            theirs.append(across(got["send"]))

    state = {}
    for p in range(n):
        last = p == n - 1
        act = activate(sums[p], theirs[p], state.get("sums", after))
        act_other = swap(act)
        state = back([(0, p, act)], True, not last, state)
        state = back([(1, p, act_other)], True, not last, state, last)
        if last:
            state = back([(0, p, act), (1, p, act_other)], False, True, state)

    if direct:
        both = state["rows0"].astype(F32)
        for s in range(1, n_grid):
            both += trade(state[f"rows{s}"], s).astype(F32)
    else:
        both = lax.psum_scatter(state["rows0"], "grid", scatter_dimension=1, tiled=True)
    both = both.astype(BF16)
    return (both[0], both[1], state["gg"], state["gu"], state["gd"])


def solution(mesh):
    in_specs = (
        P(("groups", "grid"), "dp"),
        P("dp", "grid"),
        P("dp", "grid"),
        P("grid", "dp"),
        P(("groups", "dp"), "grid"),
        P(("groups", "dp"), "grid"),
        P(("groups", "grid"), "dp"),
        P(("groups", "grid"), "dp"),
    )
    out_specs = (
        P(("groups", "grid"), "dp"),
        P(("groups", "grid"), "dp"),
        P(("groups", "dp"), "grid"),
        P(("groups", "dp"), "grid"),
        P(("groups", "grid"), "dp"),
    )
    sizes = (mesh.shape["grid"], mesh.shape["dp"])
    return jax.shard_map(
        functools.partial(shards, sizes),
        mesh=mesh,
        in_specs=in_specs,
        out_specs=out_specs,
        check_vma=False,
    )
```

```python
import functools
import types

import jax
import jax.numpy as jnp
from jax import lax
from jax.experimental import pallas as pl
from jax.experimental.pallas import tpu as pltpu
from jax.sharding import PartitionSpec as P

BLK = 128
MIB = 1024 * 1024
DEPTH = 256
ANY = pl.BlockSpec(memory_space=pl.ANY)
PIECES = [2,3,3]
SPLIT = 4
KEPT = ("kg", "ku", "kd")
MASKS = ("mask_gate", "mask_up", "mask_down_t")
F32 = jnp.float32
BF16 = jnp.bfloat16


def dot(left, right, dims=(1, 0)):
    return lax.dot_general(
        left, right, (((dims[0],), (dims[1],)), ((), ())), preferred_element_type=F32
    )


def pinned(array):
    spec = pl.BlockSpec(memory_space=pltpu.VMEM)
    if isinstance(array, jax.ShapeDtypeStruct):
        return (pltpu.VMEM(array.shape, array.dtype), spec)
    return (pltpu.with_memory_space_constraint(array, pltpu.VMEM), spec)


def call(kernel, name, ins, outs, scratch=None, aliases=None, vmem=2):
    scratch = scratch or {}
    names = [*ins, *outs, *scratch]
    in_names, out_names = list(ins), list(outs)

    def body(*refs):
        kernel(types.SimpleNamespace(**dict(zip(names, refs))))

    results = pl.pallas_call(
        body,
        out_shape=[shape for shape, _ in outs.values()],
        in_specs=[spec for _, spec in ins.values()],
        out_specs=[spec for _, spec in outs.values()],
        scratch_shapes=list(scratch.values()),
        input_output_aliases={
            in_names.index(i): out_names.index(o) for i, o in (aliases or {}).items()
        },
        compiler_params=pltpu.CompilerParams(vmem_limit_bytes=vmem * MIB),
        cost_estimate=pl.CostEstimate(flops=1, bytes_accessed=1, transcendentals=0),
        name=name,
    )(*[array for array, _ in ins.values()])
    return dict(zip(out_names, results))


def hbm(array):
    return pltpu.with_memory_space_constraint(array, pltpu.HBM)


def whole(array):
    return pl.BlockSpec(array.shape, lambda *_: (0,) * len(array.shape))


def spread(r):
    def pattern(blocks):
        at = lax.broadcasted_iota(jnp.int32, (blocks, blocks * BLK), 0) * BLK
        column = lax.broadcasted_iota(jnp.int32, (blocks, blocks * BLK), 1)
        return ((column >= at) & (column < at + BLK)).astype(F32).astype(BF16)

    across, along = r.mask_gate.shape
    units, features = pattern(along), pattern(across)
    for mask, by_units, by_features in (
        (r.mask_gate, r.mg, r.mgt),
        (r.mask_up, r.mu, r.mut),
        (r.mask_down_t, r.mdt, r.md),
    ):
        entries = mask[...].astype(F32).astype(BF16)
        value = dot(entries, units)
        for b in range(across):
            by_units[b] = value[b : b + 1, :]
        value = dot(entries, features, (0, 0))
        for b in range(along):
            by_features[b] = value[b : b + 1, :]


def first_unit(which, half):
    core = lax.rem(lax.axis_index("dp"), 2)
    return (core if which == 0 else 1 - core) * half


def span(start, size):
    return pl.ds(pl.multiple_of(start, BLK), size)


def fetch_kernel(r):
    copies = []
    for k in MASKS:
        copies.append((getattr(r, "hbm_" + k), getattr(r, k)))
    copies = [pltpu.make_async_copy(a, b, r.sems.at[k]) for k, (a, b) in enumerate(copies)]
    for copy in copies[-len(MASKS) :] + copies[: -len(MASKS)]:
        copy.start()
    for copy in copies[-len(MASKS) :]:
        copy.wait()
    spread(r)
    for copy in copies[: -len(MASKS)]:
        copy.wait()


def diagonal(out, value):
    rows, size = value.shape
    for b in range(size // BLK):
        band = slice(b * BLK, (b + 1) * BLK)
        out[b * rows : (b + 1) * rows, band] = value[:, band]


def assemble_kernel(r):
    blocks = [ref for name, ref in sorted(vars(r).items()) if name.startswith("block")]
    tok = jnp.concatenate([block[0] for block in blocks], axis=0)
    cot = jnp.concatenate([block[1] for block in blocks], axis=0)
    r.cot[...] = cot
    size = r.tok_d.shape[2]
    r.tok_d[...] = jnp.zeros_like(r.tok_d)
    r.cot_d[...] = jnp.zeros_like(r.cot_d)
    for p in range(r.tok_d.shape[0]):
        part = slice(p * size, (p + 1) * size)
        diagonal(r.tok_d.at[p], tok[:, part])
        diagonal(r.cot_d.at[p], cot[:, part])
    for p in range(r.tok_d.shape[0]):
        r.tok_t[p] = r.tok_d[p].T


def masked_sum(left, right, masks, dims=(1, 0)):
    value = dot(left, right, dims)
    rows = value.shape[0] // len(masks)
    return sum(value[b * rows : (b + 1) * rows, :] * m for b, m in enumerate(masks))


def partial_kernel(which, start, half, tile, r):
    pairs, _, size = r.tok_d.shape
    base = first_unit(which, half) + start
    for first in range(0, r.send.shape[2], tile):
        at = span(base + first, tile)
        local = slice(first, first + tile)
        totals = [0.0, 0.0, 0.0]
        for p in range(pairs):
            part = slice(p * size, (p + 1) * size)
            bands = range(p * size // BLK, (p + 1) * size // BLK)
            for k, (left, right, mask, dims) in enumerate(
                (
                    (r.tok_d[p], r.kg[part, at], r.mg, (1, 0)),
                    (r.tok_d[p], r.ku[part, at], r.mu, (1, 0)),
                    (r.cot_d[p], r.kd[at, part], r.mdt, (1, 1)),
                )
            ):
                totals[k] += masked_sum(left, right, [mask[b, :, at] for b in bands], dims)
        for k, value in enumerate(totals):
            if hasattr(r, "received"):
                value = value + r.received[k, :, local]
                r.own[k, :, local] = value
            r.send[k, :, local] = value.astype(r.send.dtype)


def act_kernel(r):
    others = [ref for name, ref in vars(r).items() if name.startswith("other")]
    gate, up, back = (
        sum((other[k].astype(F32) for other in others), r.own[k]) for k in range(3)
    )
    sigma = 1.0 / (1.0 + jnp.exp(-gate))
    silu = gate * sigma
    slope = sigma * (1.0 + gate * (1.0 - sigma))
    r.act[0] = (silu * up).astype(BF16)
    r.act[1] = (back * up * slope).astype(BF16)
    r.act[2] = (back * silu).astype(BF16)


def add_rows(r, i, block, at):
    width, tile = r.acc.shape[2], r.act_d.shape[4]
    size = min(DEPTH, width)
    for f in range(0, width, size):
        part = slice(f, f + size)

        def masks(mask):
            return [mask[block + b][:, part] for b in range(tile // BLK)]

        r.acc[0, :, part] += masked_sum(r.act_d[*i, 0], r.kd[at, part], masks(r.md))
        r.acc[1, :, part] += masked_sum(
            r.act_d[*i, 1], r.kg[part, at], masks(r.mgt), (1, 1)
        ) + masked_sum(r.act_d[*i, 2], r.ku[part, at], masks(r.mut), (1, 1))


class Outbox:
    def __init__(self, slots, sems):
        self.slots, self.sems = slots, sems
        self.flying, self.count = [None] * slots.shape[0], 0

    def put(self, value, target):
        k = self.count % len(self.flying)
        self.count += 1
        if self.flying[k] is not None:
            self.flying[k].wait()
        self.slots[k] = value
        self.flying[k] = pltpu.make_async_copy(self.slots.at[k], target, self.sems.at[k])
        self.flying[k].start()

    def close(self):
        for copy in self.flying:
            if copy is not None:
                copy.wait()


def back_kernel(items, half, do_rows, do_grads, r):
    tile = r.act_d.shape[4]
    spots = tile // BLK
    if do_rows:
        r.acc[...] = r.sums[...] if hasattr(r, "sums") else jnp.zeros_like(r.acc)
    if do_grads:
        groups, height, _ = r.tok_t.shape
        by_cols, by_rows = Outbox(r.col_slots, r.col_sems), Outbox(r.row_slots, r.row_sems)
    waiting = []
    for n, (act, which, start) in enumerate(items):
        act = getattr(r, act)
        _, rows, size = act.shape
        base = first_unit(which, half) + start
        at, block = span(base, size), lax.div(base, BLK)
        tiles = [slice(i * tile, (i + 1) * tile) for i in range(size // tile)]
        for i in range(groups if do_grads else 0):
            band = slice(i * height, (i + 1) * height)
            for out, k, mask in ((r.gg, 1, r.mg), (r.gu, 2, r.mu)):
                right = r.masked_act.at[k - 1]
                for j in range(height // BLK):
                    keep = mask[i * (height // BLK) + j, :, at].astype(BF16)
                    right[j * rows : (j + 1) * rows, :] = act[k] * keep
                by_cols.put(dot(r.tok_t[i], right[...]), out.at[band, at])
        if n == 0:
            r.act_d[...] = jnp.zeros_like(r.act_d)
        for i, local in enumerate(tiles):
            for k in range(3 if do_rows else 1):
                diagonal(r.act_d.at[n, i, k], act[k, :, local])
            if do_grads:
                for b in range(spots):
                    keep = r.md[block + i * spots + b].astype(BF16)
                    r.masked_cot[b * rows : (b + 1) * rows, :] = r.cot[...] * keep
                value = dot(r.act_d[n, i, 0].T, r.masked_cot[...])
                by_rows.put(value, r.gd.at[span(base + i * tile, tile), :])
        if do_rows:
            waiting += [(n, i, block + i * spots, base + i * tile) for i in range(len(tiles))]
    for n, i, block, start in waiting:
        add_rows(r, (n, i), block, span(start, tile))
    if do_rows:
        if hasattr(r, "new_sums"):
            r.new_sums[...] = r.acc[...]
        else:
            outs = [ref for name, ref in vars(r).items() if name.startswith("rows")]
            count = outs[0].shape[1]
            for k, out in enumerate(outs):
                out[...] = r.acc[:, k * count : (k + 1) * count, :].astype(out.dtype)
    if do_grads:
        by_cols.close()
        by_rows.close()


def shards(sizes, tokens, w_gate, w_up, w_down, mask_gate, mask_up, mask_down, grad_out):
    n_grid, n_dp = sizes
    width, units = w_gate.shape
    rows = n_grid * tokens.shape[0]
    pairs = n_dp // 2
    half = units // 2
    tile = min(DEPTH, half)
    split = PIECES if sum(PIECES) * tile == half else [half // tile]
    split = [tile * count for count in split]
    starts = [sum(split[:p]) for p in range(len(split))]
    n = len(split)
    direct = n_grid == 4
    grant = lambda mib: mib if rows <= 64 else 32

    def trade(array, s):
        return lax.ppermute(array, "grid", [(i, i ^ s) for i in range(n_grid)])

    def swap(array):
        return lax.ppermute(array, "dp", [(i, i ^ 1) for i in range(n_dp)])

    def across(array):
        return [
            lax.ppermute(
                array,
                "dp",
                [(i, ((i // 2 + s) % pairs) * 2 + i % 2) for i in range(n_dp)],
            )
            for s in range(1, pairs)
        ]

    def shape(*dims, kind=BF16):
        return jax.ShapeDtypeStruct(dims, kind)

    weights = {"w_gate": (w_gate, ANY), "w_up": (w_up, ANY), "w_down": (w_down, ANY)}
    weights = {k: (hbm(w), spec) for k, (w, spec) in weights.items()}

    block = jnp.stack([tokens, grad_out])
    if direct:
        blocks = [block] + [trade(block, s) for s in range(1, n_grid)]
    else:
        blocks = [lax.all_gather(block, "grid", axis=1, tiled=True)]

    across_shape = shape(width // BLK, 1, units, kind=F32)
    along_shape = shape(units // BLK, 1, width, kind=F32)
    masks = dict(zip(MASKS, (mask_gate, mask_up, mask_down.T)))
    values = call(
        fetch_kernel,
        "fetch",
        {**weights, **{"hbm_" + k: (hbm(m), ANY) for k, m in masks.items()}},
        {
            **{k: pinned(across_shape) for k in ("mg", "mu", "mdt")},
            **{k: pinned(along_shape) for k in ("mgt", "mut", "md")},
        },
        scratch={
            **{k: pltpu.VMEM(m.shape, m.dtype) for k, m in masks.items()},
            "sems": pltpu.SemaphoreType.DMA((3 * SPLIT + len(masks),)),
        },
        vmem=grant(4),
    )

    values.update(kg=w_gate, ku=w_up, kd=w_down)
    pair = min(DEPTH, width) // BLK
    pair_shape = shape(width // (pair * BLK), pair * rows, pair * BLK)
    values |= call(
        assemble_kernel,
        "assemble",
        {
            "after": (values["mg"], ANY),
            **{f"block{k}": (b, whole(b)) for k, b in reversed(list(enumerate(blocks)))},
        },
        {
            "cot": pinned(shape(rows, width)),
            "tok_d": pinned(pair_shape),
            "cot_d": pinned(pair_shape),
            "tok_t": pinned(shape(pair_shape.shape[0], pair * BLK, pair * rows)),
        },
        vmem=grant(4),
    )

    def held(*names):
        return {k: pinned(values[k]) for k in names}

    def partials(which, p, after=None, received=None):
        trio = (3, rows, split[p])
        ins = held("tok_d", "cot_d", "mg", "mu", "mdt", *KEPT)
        outs = {"send": pinned(shape(*trio, kind=F32))}
        if after is not None:
            ins["after"] = (after, ANY)
        if received is not None:
            ins["received"] = pinned(received)
            outs = {"own": pinned(shape(*trio, kind=F32)), "send": pinned(shape(*trio))}
        kernel = functools.partial(partial_kernel, which, starts[p], half, tile)
        return call(kernel, "partials", ins, outs, vmem=grant(2))

    def activate(own, others, after):
        ins = {"own": pinned(own), "after": (after, ANY)}
        ins.update({f"other{k}": pinned(a) for k, a in enumerate(others)})
        outs = {"act": pinned(shape(*own.shape))}
        return call(act_kernel, "activate", ins, outs, vmem=grant(2))["act"]

    def back(pieces, do_rows, do_grads, state, last=False):
        items = [(f"act{k}", which, starts[p]) for k, (which, p, _) in enumerate(pieces)]
        ins = {f"act{k}": pinned(act) for k, (_, _, act) in enumerate(pieces)}
        ins.update(held("md"))
        outs, aliases = {}, {}
        spots, size = tile // BLK, split[pieces[0][1]]
        scratch = {"act_d": pltpu.VMEM((len(pieces), size // tile, 3, spots * rows, tile), BF16)}
        if do_rows:
            ins.update(held("mgt", "mut", *KEPT))
            scratch["acc"] = pltpu.VMEM((2, rows, width), F32)
            if "sums" in state:
                ins["sums"] = pinned(state["sums"])
            if last:
                n_out = n_grid if direct else 1
                out = shape(2, rows // n_out, width, kind=BF16 if direct else F32)
                outs.update({f"rows{k}": pinned(out) for k in range(n_out)})
            else:
                outs["new_sums"] = pinned(shape(2, rows, width, kind=F32))
        if do_grads:
            ins.update(held("tok_t", "cot", "mg", "mu"))
            outs["gg"] = (shape(width, units, kind=F32), ANY)
            outs["gu"] = (shape(width, units, kind=F32), ANY)
            outs["gd"] = (shape(units, width, kind=F32), ANY)
            scratch["masked_act"] = pltpu.VMEM((2, pair * rows, size), BF16)
            scratch["masked_cot"] = pltpu.VMEM((spots * rows, width), BF16)
            by_cols, by_rows = 2 * width // (pair * BLK), size // tile
            scratch["col_slots"] = pltpu.VMEM((by_cols, pair * BLK, size), F32)
            scratch["row_slots"] = pltpu.VMEM((by_rows, tile, width), F32)
            scratch["col_sems"] = pltpu.SemaphoreType.DMA((by_cols,))
            scratch["row_sems"] = pltpu.SemaphoreType.DMA((by_rows,))
            for k in ("gg", "gu", "gd"):
                if k in state:
                    ins["old_" + k] = (state[k], ANY)
                    aliases["old_" + k] = k
            if "rows0" in state:
                ins["after"] = (state["rows0"], ANY)
        got = call(
            functools.partial(back_kernel, items, half, do_rows, do_grads),
            "_".join(["back"] + ["rows"] * do_rows + ["grads"] * do_grads),
            ins,
            outs,
            scratch=scratch,
            aliases=aliases,
            vmem=grant(12 if do_grads else 3),
        )
        return {**state, **{k.replace("new_", ""): v for k, v in got.items()}}

    sent, sums, theirs, after = [], [], [], None
    for p in range(n + 1):
        if p < n:
            after = partials(1, p, after)["send"]
            sent.append(swap(after))
        if p > 0:
            got = partials(0, p - 1, after, sent[p - 1])
            after = got["own"]
            sums.append(after)
            theirs.append(across(got["send"]))

    state = {}
    for p in range(n):
        last = p == n - 1
        act = activate(sums[p], theirs[p], state.get("sums", after))
        act_other = swap(act)
        if 0 < p < n - 1:
            state = back([(0, p, act), (1, p, act_other)], True, True, state)
            continue
        state = back([(0, p, act)], True, not last, state)
        state = back([(1, p, act_other)], True, not last, state, last)
        if last:
            state = back([(0, p, act), (1, p, act_other)], False, True, state)

    if direct:
        both = state["rows0"].astype(F32)
        for s in range(1, n_grid):
            both += trade(state[f"rows{s}"], s).astype(F32)
    else:
        both = lax.psum_scatter(state["rows0"], "grid", scatter_dimension=1, tiled=True)
    both = both.astype(BF16)
    return (both[0], both[1], state["gg"], state["gu"], state["gd"])


def solution(mesh):
    in_specs = (
        P(("groups", "grid"), "dp"),
        P("dp", "grid"),
        P("dp", "grid"),
        P("grid", "dp"),
        P(("groups", "dp"), "grid"),
        P(("groups", "dp"), "grid"),
        P(("groups", "grid"), "dp"),
        P(("groups", "grid"), "dp"),
    )
    out_specs = (
        P(("groups", "grid"), "dp"),
        P(("groups", "grid"), "dp"),
        P(("groups", "dp"), "grid"),
        P(("groups", "dp"), "grid"),
        P(("groups", "grid"), "dp"),
    )
    sizes = (mesh.shape["grid"], mesh.shape["dp"])
    return jax.shard_map(
        functools.partial(shards, sizes),
        mesh=mesh,
        in_specs=in_specs,
        out_specs=out_specs,
        check_vma=False,
    )
```
